128 devices in a mesh: replica: 32 (over x, z_hi, y), shard: 4 (over z_lo, core).
Axes of the slice: x: 4, y: 4, z: 4 (z_hi: 2, z_lo: 2; z = z_hi * 2 + z_lo), core: 2. Of those that a mesh axis runs over, the one named last changes fastest.
Arguments:
- tokens: bfloat16 [32, 1024, 1024], P('replica', 'shard'), may hold values from -6 to 6
- segments: int32 [32, 1024], P('replica'), may hold values from 0 to 3, as said below
- query_weight: bfloat16 [1024, 1024], P(None, 'shard'), may hold values from -0.1875 to 0.1875
- query_bias: bfloat16 [1024], P('shard'), may hold values from -3 to 3
- key_weight: bfloat16 [1024, 1024], P(None, 'shard'), may hold values from -0.1875 to 0.1875
- value_weight: bfloat16 [1024, 1024], P(None, 'shard'), may hold values from -0.1875 to 0.1875
- value_bias: bfloat16 [1024], P('shard'), may hold values from -3 to 3
- output_weight: bfloat16 [1024, 1024], P('shard'), may hold values from -1 to 1
- output_bias: bfloat16 [1024], replicated, may hold values from -2 to 2
- first_gain: bfloat16 [1024], replicated, may hold values from 0.5 to 1.5
- first_shift: bfloat16 [1024], replicated, may hold values from -2 to 2
- inner_weight: bfloat16 [1024, 4096], P(None, 'shard'), may hold values from -0.1875 to 0.1875
- inner_bias: bfloat16 [4096], P('shard'), may hold values from -3 to 3
- outer_weight: bfloat16 [4096, 1024], P('shard'), may hold values from -0.09375 to 0.09375
- outer_bias: bfloat16 [1024], replicated, may hold values from -2 to 2
- second_gain: bfloat16 [1024], replicated, may hold values from 0.5 to 1.5
- second_shift: bfloat16 [1024], replicated, may hold values from -2 to 2
- cotangent: bfloat16 [32, 1024, 1024], P('replica', 'shard'), may hold values from -6 to 6
Outputs:
- layer_out: bfloat16 [32, 1024, 1024], P('replica', 'shard')
- tokens_grad: float32 [32, 1024, 1024], P('replica', 'shard')
- query_weight_grad: float32 [1024, 1024], P('replica', 'shard')
- query_bias_grad: float32 [1024], P('shard')
- key_weight_grad: float32 [1024, 1024], P('replica', 'shard')
- value_weight_grad: float32 [1024, 1024], P('replica', 'shard')
- value_bias_grad: float32 [1024], P('shard')
- output_weight_grad: float32 [1024, 1024], P('shard', 'replica')
- output_bias_grad: float32 [1024], replicated
- first_gain_grad: float32 [1024], replicated
- first_shift_grad: float32 [1024], replicated
- inner_weight_grad: float32 [1024, 4096], P('replica', 'shard')
- inner_bias_grad: float32 [4096], P('shard')
- outer_weight_grad: float32 [4096, 1024], P('shard', 'replica')
- outer_bias_grad: float32 [1024], replicated
- second_gain_grad: float32 [1024], replicated
- second_shift_grad: float32 [1024], replicated
The draws below stay inside these ranges and needn't reach their ends.
Inputs may be any that keep to these rules, and one draw needn't show every extreme that they name: `segments`: every sequence holds exactly four documents, numbered 0 to 3 in order along it. In one sequence of each replica index's 1, drawn from the seed, no document begins between positions 128 and 896.
All inputs are finite; a program needn't handle non-finite values.
Results may differ from the reference program's by a relative error of at most 0.03.
Values may be sent and summed in bfloat16 or wider, within the bound.
No kernel may reach another device: no remote copies, remote signals or barrier semaphores. Data moves between devices by JAX's collectives and lax.ppermute only.
A program may use at most 128 MiB of HBM per device.

```python
import jax
import jax.numpy as jnp
from jax import lax

D = 1024
HEADS = 16
HEAD_DIM = 64
FF = 4096
LEN = 1024
WINDOW = 512
SEQ_GRP = 1
INNER = 1024
SEQS = 32


def draw_segments(key, part):
    key = jax.random.fold_in(key, 11)
    score_key, pick_key = jax.random.split(key)
    position = jnp.arange(LEN, dtype=jnp.int32)
    chosen = jax.random.randint(pick_key, (SEQS // SEQ_GRP,), 0, SEQ_GRP)
    within = jnp.arange(SEQS, dtype=jnp.int32) % SEQ_GRP
    longest = within == jnp.repeat(chosen, SEQ_GRP)
    middle = (position >= LEN // 8) & (position <= 7 * LEN // 8)
    barred = longest[:, None] & middle[None, :] | (position[None, :] == 0)
    raw = jax.random.randint(score_key, (SEQS, LEN), 0, 1048576).astype(jnp.int32)
    scores = raw * LEN + position[None, :]
    scores = jnp.where(barred, -1 - position[None, :], scores).astype(jnp.int32)
    top_values, top_index = lax.top_k(scores, 3)
    starts = jnp.sum((position[None, None, :] == top_index[:, :, None]).astype(jnp.int32), axis=1)
    return jnp.cumsum(starts, axis=1).astype(jnp.int32)


def raised(values, rng, source, target, parts, factor):
    owner, partner = [(jnp.arange(values.shape[dim]) // (values.shape[dim] // parts)).reshape([-1 if axis == dim else 1 for axis in range(values.ndim)]) for dim in (source, target)]
    chosen = jax.random.permutation(rng, parts)[partner]
    strong = (owner == chosen) | (owner == (partner + parts // 2) % parts)
    return jnp.where(strong, factor * values, values)


def levels(key, extent, shards, smallest, largest):
    loudness, own = 1.0, jax.random.fold_in(key, 6)
    for dim, parts in shards:
        steps = jnp.exp(jax.random.uniform(jax.random.fold_in(own, dim), (parts,), jnp.float32, smallest / len(shards), largest / len(shards)))
        loudness = loudness * jnp.repeat(steps, extent[dim] // parts).reshape([-1 if axis == dim else 1 for axis in range(len(extent))])
    return loudness


def scatter_about(stream_key, extent, scale, limit, shards=(), kind=jnp.bfloat16):
    level = levels(stream_key, extent, shards, -0.22, 0.18) if shards else 1.0
    array = jax.random.normal(stream_key, extent, jnp.float32) * scale * level
    return jnp.minimum(jnp.maximum(array, -limit), limit).astype(kind)


def bell_draw_with(own_key, shape, scale, reach, cuts, heavy, held_as=jnp.bfloat16):
    array = scale * jax.random.normal(own_key, shape, jnp.float32)
    if cuts:
        array = array * levels(own_key, shape, cuts, -0.22, 0.18)
    return jnp.clip(raised(array, jax.random.fold_in(own_key, 3), *heavy), -reach, reach).astype(held_as)


def setup_inputs(seed: int = 0) -> dict:
    key_list = jax.random.split(jax.random.key(seed), 19)
    return {
        "tokens": bell_draw_with(key_list[0], (SEQS, LEN, D), 1.0, 6.0, ((0, 32), (1, 4)), (0, 2, 32, 2.75)),
        "segments": draw_segments(jax.random.fold_in(key_list[18], 71), 0),
        "query_weight": scatter_about(key_list[2], (D, INNER), D ** -0.5, 0.1875, ((1, 4),)),
        "query_bias": scatter_about(key_list[3], (INNER,), 0.5, 3.0, ((0, 4),)),
        "key_weight": scatter_about(key_list[4], (D, INNER), D ** -0.5, 0.1875, ((1, 4),)),
        "value_weight": scatter_about(key_list[5], (D, INNER), D ** -0.5, 0.1875, ((1, 4),)),
        "value_bias": scatter_about(key_list[6], (INNER,), 0.5, 3.0, ((0, 4),)),
        "output_weight": scatter_about(key_list[7], (INNER, D), (max(INNER // 32, 1)) ** -0.5, 1.0, ((0, 4),)),
        "output_bias": scatter_about(key_list[8], (D,), 0.3, 2.0),
        "first_gain": jnp.clip(1.0 + 0.1 * jax.random.normal(key_list[9], (D,), jnp.float32), 0.5, 1.5).astype(jnp.bfloat16),
        "first_shift": scatter_about(key_list[10], (D,), 0.3, 2.0),
        "inner_weight": scatter_about(key_list[11], (D, FF), D ** -0.5, 0.1875, ((1, 4),)),
        "inner_bias": scatter_about(key_list[12], (FF,), 0.5, 3.0, ((0, 4),)),
        "outer_weight": scatter_about(key_list[13], (FF, D), FF ** -0.5, 0.09375, ((0, 4),)),
        "outer_bias": scatter_about(key_list[14], (D,), 0.3, 2.0),
        "second_gain": jnp.clip(1.0 + 0.1 * jax.random.normal(key_list[15], (D,), jnp.float32), 0.5, 1.5).astype(jnp.bfloat16),
        "second_shift": scatter_about(key_list[16], (D,), 0.3, 2.0),
        "cotangent": bell_draw_with(key_list[17], (SEQS, LEN, D), 1.0, 6.0, ((0, 32), (1, 4)), (0, 2, 32, 2.75)),
    }


@jax.custom_vjp
def low(v):
    return lax.optimization_barrier(v.astype(jnp.bfloat16)).astype(jnp.float32)

@jax.custom_vjp
def low_back(v):
    return v

def low_keep(v):
    return (low(v), None)

def low_pass(kept, grad):
    return (grad,)

def back_keep(v):
    return (v, None)

def back_low(kept, grad):
    return (low(grad),)
low.defvjp(low_keep, low_pass)
low_back.defvjp(back_keep, back_low)

def matmul(first_op, second_op):
    return jnp.dot(first_op, second_op, precision=lax.Precision.HIGHEST, preferred_element_type=jnp.float32)

def normalize(rows, gain, shift):
    center = lax.optimization_barrier(jnp.mean(rows, axis=-1, keepdims=True))
    centred = rows - center
    spread = lax.optimization_barrier(jnp.mean(centred * centred, axis=-1, keepdims=True))
    return centred * lax.rsqrt(spread + 1e-06) * gain + shift

def gelu_tanh(values):
    return 0.5 * values * (1.0 + jnp.tanh(0.7978845608028654 * (values + 0.044715 * values * values * values)))

def doc_mask(seg_seq):
    position = jnp.arange(LEN, dtype=jnp.int32)
    nearby = jnp.abs(position[:, None] - position[None, :]) <= WINDOW
    return (seg_seq[:, None] == seg_seq[None, :]) & nearby

def sequence(float_params, inputs, seg_seq):
    query_weight, query_bias, key_weight, value_weight, value_bias, output_weight, output_bias, first_gain, first_shift, inner_weight, inner_bias, outer_weight, outer_bias, second_gain, second_shift = float_params
    queries = low(low_back(matmul(inputs, query_weight) + query_bias)).reshape(LEN, HEADS, HEAD_DIM)
    keys_all = low(low_back(matmul(inputs, key_weight))).reshape(LEN, HEADS, HEAD_DIM)
    values_all = low(low_back(matmul(inputs, value_weight) + value_bias)).reshape(LEN, HEADS, HEAD_DIM)
    scores = jnp.einsum('qhe,khe->hqk', queries, keys_all, precision=lax.Precision.HIGHEST) * HEAD_DIM ** (-0.5)
    scores = low_back(scores)
    scores = jnp.where(doc_mask(seg_seq)[None], scores, -1e+30)
    row_max = lax.optimization_barrier(jnp.max(scores, axis=-1, keepdims=True))
    exp_scores = jnp.exp(scores - row_max)
    attn_prob = exp_scores / lax.optimization_barrier(jnp.sum(exp_scores, axis=-1, keepdims=True))
    context = jnp.einsum('hqk,khe->qhe', low(attn_prob), values_all, precision=lax.Precision.HIGHEST)
    context = low(low_back(context.reshape(LEN, HEADS * HEAD_DIM)))
    attended = low_back(matmul(context, output_weight)) + output_bias
    normed = normalize(inputs + attended, first_gain, first_shift)
    hidden = low_back(matmul(low(normed), inner_weight) + inner_bias)
    active = low(gelu_tanh(hidden))
    mixed = low_back(matmul(active, outer_weight)) + outer_bias
    return normalize(normed + mixed, second_gain, second_shift)

def reference(tokens, segments, query_weight, query_bias, key_weight, value_weight, value_bias, output_weight, output_bias, first_gain, first_shift, inner_weight, inner_bias, outer_weight, outer_bias, second_gain, second_shift, cotangent):
    float_params = tuple((weight_arr.astype(jnp.float32) for weight_arr in (query_weight, query_bias, key_weight, value_weight, value_bias, output_weight, output_bias, first_gain, first_shift, inner_weight, inner_bias, outer_weight, outer_bias, second_gain, second_shift)))
    inputs = tokens.astype(jnp.float32)
    checked = jax.checkpoint(sequence)

    def forward(params_in, inputs_in):

        def per_sequence(bundle):
            return checked(params_in, bundle[0], bundle[1])
        return lax.map(per_sequence, (inputs_in, segments))
    result, pullback = jax.vjp(forward, float_params, inputs)
    param_grads, tokens_grad = pullback(cotangent.astype(jnp.float32))
    query_weight_grad, query_bias_grad, key_weight_grad, value_weight_grad, value_bias_grad, output_weight_grad, output_bias_grad, first_gain_grad, first_shift_grad, inner_weight_grad, inner_bias_grad, outer_weight_grad, outer_bias_grad, second_gain_grad, second_shift_grad = param_grads
    return (result.astype(jnp.bfloat16), tokens_grad, query_weight_grad, query_bias_grad, key_weight_grad, value_weight_grad, value_bias_grad, output_weight_grad, output_bias_grad, first_gain_grad, first_shift_grad, inner_weight_grad, inner_bias_grad, outer_weight_grad, outer_bias_grad, second_gain_grad, second_shift_grad)
```

```python
import functools

import jax
import jax.numpy as jnp
from jax import lax
from jax.experimental import pallas as pl
from jax.experimental.pallas import tpu as pltpu
from jax.sharding import Mesh, PartitionSpec as P

HEAD_DIM = 64
WINDOW = 512
TILE = 256
AXES = ("x", "zh", "y", "zl", "c")
REPLICA = ("x", "zh", "y")
F32 = jnp.float32
BF16 = jnp.bfloat16
MIB = 1 << 20


def flat_index(x, zh, y, zl, c):
    return (((x * 2 + zh) * 4 + y) * 2 + zl) * 2 + c


def permutation(move):
    return [
        (flat_index(x, zh, y, zl, c), flat_index(*move(x, zh, y, zl, c)))
        for x in range(4)
        for zh in range(2)
        for y in range(4)
        for zl in range(2)
        for c in range(2)
    ]


LINKS = {
    "xa": permutation(lambda x, zh, y, zl, c: (x ^ 1, zh, y, zl, c)),
    "xb": permutation(lambda x, zh, y, zl, c: (3 - x, zh, y, zl, c)),
    "ya": permutation(lambda x, zh, y, zl, c: (x, zh, y ^ 1, zl, c)),
    "yb": permutation(lambda x, zh, y, zl, c: (x, zh, 3 - y, zl, c)),
    "zl": permutation(lambda x, zh, y, zl, c: (x, zh, y, zl ^ 1, c)),
    "zh": permutation(lambda x, zh, y, zl, c: (x, zh ^ 1, y, zl, c)),
    "c": permutation(lambda x, zh, y, zl, c: (x, zh, y, zl, c ^ 1)),
}
ORDERS = (
    ("xa", "xb", "ya", "yb"),
    ("xb", "ya", "yb", "xa"),
    ("ya", "yb", "xa", "xb"),
    ("yb", "xa", "xb", "ya"),
)


def send(value, link):
    return lax.ppermute(value, AXES, LINKS[link])


def dot_nn(a, b):
    return lax.dot_general(a, b, (((1,), (0,)), ((), ())), preferred_element_type=F32)


def dot_nt(a, b):
    return lax.dot_general(a, b, (((1,), (1,)), ((), ())), preferred_element_type=F32)


def dot_tn(a, b):
    return lax.dot_general(a, b, (((0,), (0,)), ((), ())), preferred_element_type=F32)


def params(limit=48):
    return pltpu.CompilerParams(vmem_limit_bytes=limit * MIB)


def cost(flops, nbytes, trans=0):
    return pl.CostEstimate(flops=int(flops), bytes_accessed=int(nbytes), transcendentals=int(trans))


def whole(shape):
    return pl.BlockSpec(shape, lambda *_: (0,) * len(shape))


def head_lanes(shape, head):
    lane = lax.broadcasted_iota(jnp.int32, shape, len(shape) - 1)
    return (lane >> 6) == head


def attn_fwd_kernel(q_ref, k_ref, v_ref, bias_ref, wo_ref, ctx_ref, lse_ref, term_ref):
    heads = q_ref.shape[1] // HEAD_DIM
    q = q_ref[...] * jnp.asarray(HEAD_DIM ** -0.5, BF16)
    k = k_ref[...]
    v = v_ref[...]
    bias = bias_ref[...].astype(F32)
    ctx = jnp.zeros(q.shape, F32)
    lse_all = jnp.zeros((q.shape[0], 128), F32)
    lane = lax.broadcasted_iota(jnp.int32, lse_all.shape, 1)
    for h in range(heads):
        mine = head_lanes(q.shape, h)
        s = dot_nt(jnp.where(mine, q, jnp.zeros_like(q)), k) + bias
        top = jnp.max(s, axis=-1, keepdims=True)
        p = jnp.exp(s - top)
        total = jnp.sum(p, axis=-1, keepdims=True)
        part = dot_nn(p.astype(BF16), v) * (1.0 / total)
        ctx = jnp.where(mine, part, ctx)
        lse_all = jnp.where(lane == h, top + jnp.log(total), lse_all)
    ctx_low = ctx.astype(BF16)
    ctx_ref[...] = ctx_low
    lse_ref[...] = jnp.transpose(lse_all)[:8]
    term_ref[...] = dot_nn(ctx_low, wo_ref[...]).astype(BF16)


def attn_fwd(q, k, v, bias, wo, first_tile):
    inner = q.shape[1]
    width = wo.shape[1]
    length = k.shape[0]
    tile = lambda i: (i + first_tile, 0)
    return pl.pallas_call(
        attn_fwd_kernel,
        grid=(2,),
        in_specs=[
            pl.BlockSpec((TILE, inner), tile),
            whole(k.shape),
            whole(v.shape),
            pl.BlockSpec((TILE, length), tile),
            whole(wo.shape),
        ],
        out_specs=[
            pl.BlockSpec((TILE, inner), lambda i: (i, 0)),
            pl.BlockSpec((8, TILE), lambda i: (0, i)),
            pl.BlockSpec((TILE, width), lambda i: (i, 0)),
        ],
        out_shape=[
            jax.ShapeDtypeStruct((2 * TILE, inner), BF16),
            jax.ShapeDtypeStruct((8, 2 * TILE), F32),
            jax.ShapeDtypeStruct((2 * TILE, width), BF16),
        ],
        compiler_params=params(),
        cost_estimate=cost(2 * 3 * 2 * TILE * length * inner * 2, 6 * MIB, 2 * TILE * length * 4),
        name="attn_fwd",
    )(q, k, v, bias, wo)


def attn_bwd_kernel(q_ref, k_ref, v_ref, bias_ref, lse_ref, up_ref, wo_ref, dq_ref, dk_ref, dv_ref, dk_acc, dv_acc):
    step = pl.program_id(0)

    @pl.when(step == 0)
    def _():
        dk_acc[...] = jnp.zeros_like(dk_acc)
        dv_acc[...] = jnp.zeros_like(dv_acc)

    heads = q_ref.shape[1] // HEAD_DIM
    q = q_ref[...] * jnp.asarray(HEAD_DIM ** -0.5, BF16)
    k = k_ref[...]
    v = v_ref[...]
    bias = bias_ref[...].astype(F32)
    grad = dot_nt(up_ref[...], wo_ref[...]).astype(BF16)
    dq = jnp.zeros(q.shape, F32)
    for h in range(heads):
        mine = head_lanes(q.shape, h)
        qh = jnp.where(mine, q, jnp.zeros_like(q))
        gh = jnp.where(mine, grad, jnp.zeros_like(grad))
        p = jnp.exp(dot_nt(k, qh) + bias - lse_ref[h : h + 1, :])
        dv_acc[...] += dot_nn(p.astype(BF16), gh)
        dp = dot_nt(v, gh)
        row = jnp.sum(p * dp, axis=0, keepdims=True)
        ds = (p * (dp - row)).astype(BF16)
        dk_acc[...] += dot_nn(ds, qh)
        dq = jnp.where(mine, dot_tn(ds, k), dq)
    dq_ref[...] = (dq * HEAD_DIM ** -0.5).astype(BF16)

    @pl.when(step == pl.num_programs(0) - 1)
    def _():
        dk_ref[...] = dk_acc[...].astype(BF16)
        dv_ref[...] = dv_acc[...].astype(BF16)


def attn_bwd(q, k, v, bias, lse, up, wo):
    length, inner = q.shape
    width = wo.shape[1]
    row = lambda i: (i, 0)
    col = lambda i: (0, i)
    return pl.pallas_call(
        attn_bwd_kernel,
        grid=(length // TILE,),
        in_specs=[
            pl.BlockSpec((TILE, inner), row),
            whole(k.shape),
            whole(v.shape),
            pl.BlockSpec((length, TILE), col),
            pl.BlockSpec((8, TILE), col),
            pl.BlockSpec((TILE, width), row),
            whole(wo.shape),
        ],
        out_specs=[pl.BlockSpec((TILE, inner), row), whole(k.shape), whole(k.shape)],
        out_shape=[jax.ShapeDtypeStruct((length, inner), BF16)] * 3,
        scratch_shapes=[pltpu.VMEM((length, inner), F32), pltpu.VMEM((length, inner), F32)],
        compiler_params=params(),
        cost_estimate=cost(2 * 5 * 4 * length * length * inner, 8 * MIB, length * length * 4),
        name="attn_bwd",
    )(q, k, v, bias, lse, up, wo)


def normal_of(rows):
    center = jnp.mean(rows, axis=-1, keepdims=True)
    centred = rows - center
    scale = lax.rsqrt(jnp.mean(centred * centred, axis=-1, keepdims=True) + 1e-06)
    return centred * scale, scale


def normal_back(up, gain, normal, scale):
    scaled = up * gain
    mean_up = jnp.mean(scaled, axis=-1, keepdims=True)
    mean_un = jnp.mean(scaled * normal, axis=-1, keepdims=True)
    return scale * (scaled - mean_up - normal * mean_un)


def stack_rows(*rows):
    width = rows[0].shape[1]
    return jnp.concatenate([*rows, jnp.zeros((8 - len(rows), width), F32)], axis=0)


def column_sum(rows):
    return jnp.sum(rows, axis=0, keepdims=True)


def norm1_kernel(x_ref, own_ref, near_ref, far_ref, vec_ref, normal_ref, scale_ref, low_ref):
    rows = (
        x_ref[...].astype(F32)
        + own_ref[...].astype(F32)
        + near_ref[...].astype(F32)
        + far_ref[...].astype(F32)
        + vec_ref[0:1]
    )
    normal, scale = normal_of(rows)
    normal_ref[...] = normal
    scale_ref[...] = jnp.broadcast_to(scale, scale_ref.shape)
    low_ref[...] = (normal * vec_ref[1:2] + vec_ref[2:3]).astype(BF16)


def norm2_kernel(normal1_ref, own_ref, near_ref, vec_ref, cot_ref, out_ref, grad_ref, low_ref, sums_ref):
    rows = (
        normal1_ref[...] * vec_ref[1:2]
        + vec_ref[2:3]
        + own_ref[...]
        + near_ref[...].astype(F32)
        + vec_ref[3:4]
    )
    normal, scale = normal_of(rows)
    gain = vec_ref[4:5]
    out_ref[...] = (normal * gain + vec_ref[5:6]).astype(BF16)
    cot = cot_ref[...].astype(F32)
    grad = normal_back(cot, gain, normal, scale)
    grad_ref[...] = grad
    low_ref[...] = grad.astype(BF16)
    sums_ref[...] = stack_rows(column_sum(cot * normal), column_sum(cot), column_sum(grad))


def norm1_back_kernel(up_ref, own_ref, near_ref, normal_ref, scale_ref, vec_ref, grad_ref, low_ref, sums_ref):
    up = up_ref[...] + own_ref[...] + near_ref[...].astype(F32)
    normal = normal_ref[...]
    grad = normal_back(up, vec_ref[1:2], normal, scale_ref[:, 0:1])
    grad_ref[...] = grad
    low_ref[...] = grad.astype(BF16)
    sums_ref[...] = stack_rows(column_sum(up * normal), column_sum(up), column_sum(grad))


def simple(kernel, outs, *operands, name):
    return pl.pallas_call(
        kernel,
        out_shape=[jax.ShapeDtypeStruct(*o) for o in outs],
        compiler_params=params(),
        cost_estimate=cost(20 * TILE * 1024, 5 * MIB),
        name=name,
    )(*operands)


def mlp_fwd_kernel(n_ref, wi0, wi1, bi_ref, wo0, wo1, act0, act1, der0, der1, own_ref, near_ref, acc):
    step = pl.program_id(0)

    @pl.when(step == 0)
    def _():
        acc[...] = jnp.zeros_like(acc)

    n = n_ref[...]
    for b, (wi, wo, act, der) in enumerate(((wi0, wo0, act0, der0), (wi1, wo1, act1, der1))):
        u = dot_nn(n, wi[...]) + bi_ref[b : b + 1, :]
        square = u * u
        th = jnp.tanh(0.7978845608028654 * u * (1.0 + 0.044715 * square))
        half = 0.5 * (1.0 + th)
        low = (u * half).astype(BF16)
        act[...] = low
        slope = 0.7978845608028654 * (1.0 + 3.0 * 0.044715 * square)
        der[...] = (half + 0.5 * u * (1.0 - th * th) * slope).astype(BF16)
        acc[...] += dot_nn(low, wo[...])

    @pl.when(step == pl.num_programs(0) - 1)
    def _():
        own_ref[...] = acc[:TILE]
        near_ref[...] = acc[TILE:].astype(BF16)


def mlp_bwd_kernel(m_ref, wi0, wi1, wo0, wo1, der0, der1, hg0, hg1, own_ref, near_ref, bsum_ref, acc):
    step = pl.program_id(0)

    @pl.when(step == 0)
    def _():
        acc[...] = jnp.zeros_like(acc)

    m = m_ref[...]
    sums = []
    for wi, wo, der, hg in ((wi0, wo0, der0, hg0), (wi1, wo1, der1, hg1)):
        low = (dot_nt(m, wo[...]) * der[...].astype(F32)).astype(BF16)
        hg[...] = low
        sums.append(column_sum(low.astype(F32)))
        acc[...] += dot_nt(low, wi[...])
    bsum_ref[...] = stack_rows(*sums)

    @pl.when(step == pl.num_programs(0) - 1)
    def _():
        own_ref[...] = acc[:TILE]
        near_ref[...] = acc[TILE:].astype(BF16)


CHUNK = 256


def mlp_specs(width, units, tokens):
    wi = pl.BlockSpec((width, CHUNK), lambda i: (0, i))
    wo = pl.BlockSpec((CHUNK, width), lambda i: (i, 0))
    act = pl.BlockSpec((tokens, CHUNK), lambda i: (0, i))
    vec = pl.BlockSpec((8, CHUNK), lambda i: (0, i))
    return wi, wo, act, vec


def mlp_fwd(n, wi, bias, wo):
    tokens, width = n.shape
    units = wi[0].shape[1]
    wi_s, wo_s, act_s, vec_s = mlp_specs(width, units, tokens)
    return pl.pallas_call(
        mlp_fwd_kernel,
        grid=(units // CHUNK,),
        in_specs=[whole(n.shape), wi_s, wi_s, vec_s, wo_s, wo_s],
        out_specs=[act_s] * 4 + [whole((TILE, width))] * 2,
        out_shape=[jax.ShapeDtypeStruct((tokens, units), BF16)] * 4
        + [jax.ShapeDtypeStruct((TILE, width), F32), jax.ShapeDtypeStruct((TILE, width), BF16)],
        scratch_shapes=[pltpu.VMEM((tokens, width), F32)],
        compiler_params=params(),
        cost_estimate=cost(8 * tokens * width * units, 16 * MIB, 2 * tokens * units),
        name="mlp_fwd",
    )(n, wi[0], wi[1], bias, wo[0], wo[1])


def mlp_bwd(m, wi, wo, der):
    tokens, width = m.shape
    units = wi[0].shape[1]
    wi_s, wo_s, act_s, vec_s = mlp_specs(width, units, tokens)
    return pl.pallas_call(
        mlp_bwd_kernel,
        grid=(units // CHUNK,),
        in_specs=[whole(m.shape), wi_s, wi_s, wo_s, wo_s, act_s, act_s],
        out_specs=[act_s] * 2 + [whole((TILE, width))] * 2 + [vec_s],
        out_shape=[jax.ShapeDtypeStruct((tokens, units), BF16)] * 2
        + [
            jax.ShapeDtypeStruct((TILE, width), F32),
            jax.ShapeDtypeStruct((TILE, width), BF16),
            jax.ShapeDtypeStruct((8, units), F32),
        ],
        scratch_shapes=[pltpu.VMEM((tokens, width), F32)],
        compiler_params=params(),
        cost_estimate=cost(8 * tokens * width * units, 14 * MIB),
        name="mlp_bwd",
    )(m, wi[0], wi[1], wo[0], wo[1], der[0], der[1])


def gray(p):
    return p ^ (p >> 1)


def block_index(order, jx, jy):
    bit = {"xa": jx & 1, "xb": jx >> 1, "ya": jy & 1, "yb": jy >> 1}
    index = 0
    for link in order:
        index = index * 2 + bit[link]
    return index


def mlp_grads_kernel(place, n_ref, hg0, hg1, m_ref, act0, act1, *rest):
    outs, scratch = rest[:8], rest[8]
    x_here, zh_here, y_here = place[0], place[1], place[2]
    for mat, (left, rights) in enumerate(((n_ref, (hg0, hg1)), (m_ref, (act0, act1)))):
        for jx in range(4):
            x_there = gray(gray(x_here) ^ jx)
            rows = left[:, pl.ds(pl.multiple_of(x_there * 256, 256), 256)]
            for b in range(2):
                scratch[...] = dot_tn(rows, rights[b][...]).astype(BF16)
                for jy in range(4):
                    y_there = gray(gray(y_here) ^ jy)
                    for a in range(2):
                        off = pl.multiple_of((zh_here ^ a) * 128 + y_there * 32, 32)
                        block = scratch[pl.ds(off, 32), :]
                        for r, order in enumerate(ORDERS):
                            index = block_index(order, jx, jy)
                            out = outs[2 * r + (index >> 3)]
                            out[index & 7, mat, b, a] = block[:, r * 256 : (r + 1) * 256]


def mlp_grads(place, n, hg, m, act):
    tokens, width = n.shape
    units = hg[0].shape[1]
    return pl.pallas_call(
        mlp_grads_kernel,
        grid_spec=pltpu.PrefetchScalarGridSpec(
            num_scalar_prefetch=1,
            grid=(1,),
            in_specs=[whole(v.shape) for v in (n, *hg, m, *act)],
            out_specs=[whole((8, 2, 2, 2, 32, 256))] * 8,
            scratch_shapes=[pltpu.VMEM((256, units), BF16)],
        ),
        out_shape=[jax.ShapeDtypeStruct((8, 2, 2, 2, 32, 256), BF16)] * 8,
        compiler_params=params(60),
        cost_estimate=cost(8 * tokens * width * units, 14 * MIB),
        name="mlp_grads",
    )(place, n, *hg, m, *act)


def add_low(a, b):
    return (a.astype(F32) + b.astype(F32)).astype(BF16)


def reduce_blocks(parts):
    keep, out = list(parts[0::2]), list(parts[1::2])
    for step in range(4):
        for r, order in enumerate(ORDERS):
            came = send(out[r], order[step])
            half = keep[r].shape[0] // 2
            if half:
                out[r] = add_low(keep[r][half:], came[half:])
                keep[r] = add_low(keep[r][:half], came[:half])
            else:
                keep[r] = add_low(keep[r], came)
    rest = jnp.concatenate([v[0] for v in keep], axis=-1).transpose(1, 2, 0, 3, 4)
    rest = add_low(rest[0], send(rest[1], "zl"))
    return rest[0].astype(F32) + send(rest[1], "zh").astype(F32)


def scatter_replicas(grad):
    moved = lax.all_to_all(grad.astype(BF16), REPLICA, split_axis=0, concat_axis=0, tiled=True)
    return jnp.sum(moved.reshape(32, -1, grad.shape[1]).astype(F32), axis=0)


def per_device(
    tokens,
    segments,
    query_weight,
    query_bias,
    key_weight,
    value_weight,
    value_bias,
    output_weight,
    output_bias,
    first_gain,
    first_shift,
    inner_weight,
    inner_bias,
    outer_weight,
    outer_bias,
    second_gain,
    second_shift,
    cotangent,
):
    x_here, zh_here, y_here = lax.axis_index("x"), lax.axis_index("zh"), lax.axis_index("y")
    shard = lax.axis_index("zl") * 2 + lax.axis_index("c")
    width = tokens.shape[2]
    inner = query_weight.shape[1]

    block = (x_here * 4 + y_here) * 64

    def other_half(weight):
        piece = send(lax.dynamic_slice_in_dim(weight, block, 64, 0), "zl")
        return lax.all_gather(piece, ("x", "y"), axis=0, tiled=True)

    own = tokens[0]
    far = send(own, "zl")
    near = send(own, "c")
    wi = (inner_weight, other_half(inner_weight))
    wo = (outer_weight, other_half(outer_weight))
    far_near = send(far, "c")
    flat = jnp.concatenate([own, near, far, far_near], axis=0)

    tiles = shard ^ jnp.arange(4, dtype=jnp.int32)
    seg = jnp.take(segments[0].reshape(4, TILE), tiles, axis=0).reshape(-1)
    pos = (tiles[:, None] * TILE + jnp.arange(TILE, dtype=jnp.int32)[None, :]).reshape(-1)
    allowed = (seg[:, None] == seg[None, :]) & (jnp.abs(pos[:, None] - pos[None, :]) <= WINDOW)
    mask = jnp.where(allowed, 0.0, -1e30).astype(BF16)

    weights = jnp.concatenate([query_weight, key_weight, value_weight], axis=1)
    qkv_bias = jnp.concatenate(
        [query_bias.astype(F32), jnp.zeros((inner,), F32), value_bias.astype(F32)]
    )
    qkv = (jnp.dot(flat, weights, preferred_element_type=F32) + qkv_bias).astype(BF16)
    queries, keys, values = qkv[:, :inner], qkv[:, inner : 2 * inner], qkv[:, 2 * inner :]

    ctx_far, lse_far, term_far = attn_fwd(queries, keys, values, mask, output_weight, 2)
    near_far = send(term_far[TILE:], "c")
    from_far = send(add_low(term_far[:TILE], near_far), "zl")
    ctx_own, lse_own, term_own = attn_fwd(queries, keys, values, mask, output_weight, 0)
    from_near = send(term_own[TILE:], "c")

    vec = jnp.stack(
        [output_bias, first_gain, first_shift, outer_bias, second_gain, second_shift, outer_bias, outer_bias]
    ).astype(F32)
    normal1, scale1, normed_low = simple(
        norm1_kernel,
        [((TILE, width), F32), ((TILE, 128), F32), ((TILE, width), BF16)],
        own, term_own[:TILE], from_near, from_far, vec,
        name="norm1",
    )
    normed_chip = jnp.concatenate([normed_low, send(normed_low, "c")], axis=0)
    bias_rows = jnp.stack([inner_bias, send(inner_bias, "zl")] + [inner_bias] * 6).astype(F32)
    act0, act1, der0, der1, mlp_own, mlp_near = mlp_fwd(normed_chip, wi, bias_rows, wo)
    layer_out, second_grad, mixed_low, sums2 = simple(
        norm2_kernel,
        [((TILE, width), BF16), ((TILE, width), F32), ((TILE, width), BF16), ((8, width), F32)],
        normal1, mlp_own, send(mlp_near, "c"), vec, cotangent[0],
        name="norm2",
    )
    mixed_chip = jnp.concatenate([mixed_low, send(mixed_low, "c")], axis=0)
    hg0, hg1, back_own, back_near, bias_sums = mlp_bwd(mixed_chip, wi, wo, (der0, der1))
    first_grad, attn_low, sums1 = simple(
        norm1_back_kernel,
        [((TILE, width), F32), ((TILE, width), BF16), ((8, width), F32)],
        second_grad, back_own, send(back_near, "c"), normal1, scale1, vec,
        name="norm1_back",
    )
    attn_far = send(attn_low, "zl")
    attn_near = send(attn_low, "c")
    place = jnp.stack([x_here, zh_here, y_here]).astype(jnp.int32)
    parts = mlp_grads(place, normed_chip, (hg0, hg1), mixed_chip, (act0, act1))
    mlp_sums = reduce_blocks(parts)
    attn_all = jnp.concatenate([attn_low, attn_near, attn_far, send(attn_far, "c")], axis=0)

    ctx = jnp.concatenate([ctx_own, ctx_far], axis=0)
    lse = jnp.concatenate([lse_own, lse_far], axis=1)
    output_part = scatter_replicas(dot_tn(attn_all, ctx)).T
    dq, dk, dv = attn_bwd(queries, keys, values, mask, lse, attn_all, output_weight)
    grads = jnp.concatenate([dq, dk, dv], axis=1)
    token_term = dot_nt(grads, weights).astype(BF16).reshape(4, TILE, width)
    near_terms = send(jnp.concatenate([token_term[1], token_term[3]], axis=0), "c")
    far_term = send(add_low(token_term[2], near_terms[TILE:]), "zl")
    tokens_grad = (
        first_grad
        + token_term[0].astype(F32)
        + near_terms[:TILE].astype(F32)
        + far_term.astype(F32)
    )
    qkv_part = scatter_replicas(dot_tn(flat, grads))

    sums = jnp.concatenate([sums2[:3], sums1[:3]], axis=0)
    sums = sums + send(sums, "c")
    sums = sums + send(sums, "zl")
    inner_sum = bias_sums[0] + send(bias_sums[1], "zl")
    vectors = jnp.concatenate(
        [
            sums.reshape(-1),
            inner_sum,
            jnp.sum(dq.astype(F32), axis=0),
            jnp.sum(dv.astype(F32), axis=0),
        ]
    )
    everyone = lax.all_to_all(
        jnp.broadcast_to(vectors, (32, vectors.shape[0])), REPLICA, split_axis=0, concat_axis=0, tiled=True
    )
    vectors = jnp.sum(everyone, axis=0)
    sums = vectors[: 6 * width].reshape(6, width)
    rest = vectors[6 * width :]
    units = inner_bias.shape[0]
    return (
        layer_out[None],
        tokens_grad[None],
        qkv_part[:, :inner],
        rest[units : units + inner],
        qkv_part[:, inner : 2 * inner],
        qkv_part[:, 2 * inner :],
        rest[units + inner :],
        output_part,
        sums[5],
        sums[3],
        sums[4],
        mlp_sums[0],
        rest[:units],
        mlp_sums[1].T,
        sums[2],
        sums[0],
        sums[1],
    )


def solution(mesh):
    fine = Mesh(mesh.devices.reshape(4, 2, 4, 2, 2), AXES)
    shard = ("zl", "c")
    placed = (
        P(REPLICA, shard, None),
        P(REPLICA, None),
        P(None, shard),
        P(shard),
        P(None, shard),
        P(None, shard),
        P(shard),
        P(shard, None),
        P(),
        P(),
        P(),
        P(None, shard),
        P(shard),
        P(shard, None),
        P(),
        P(),
        P(),
        P(REPLICA, shard, None),
    )
    return jax.shard_map(
        per_device,
        mesh=fine,
        in_specs=placed,
        out_specs=(
            P(REPLICA, shard, None),
            P(REPLICA, shard, None),
            P(REPLICA, shard),
            P(shard),
            P(REPLICA, shard),
            P(REPLICA, shard),
            P(shard),
            P(shard, REPLICA),
            P(),
            P(),
            P(),
            P(REPLICA, shard),
            P(shard),
            P(shard, REPLICA),
            P(),
            P(),
            P(),
        ),
        check_vma=False,
    )
```

```python
import functools

import jax
import jax.numpy as jnp
from jax import lax
from jax.experimental import pallas as pl
from jax.experimental.pallas import tpu as pltpu
from jax.sharding import Mesh, PartitionSpec as P

HEAD_DIM = 64
WINDOW = 512
TILE = 256
AXES = ("x", "zh", "y", "zl", "c")
REPLICA = ("x", "zh", "y")
F32 = jnp.float32
BF16 = jnp.bfloat16
MIB = 1 << 20


def flat_index(x, zh, y, zl, c):
    return (((x * 2 + zh) * 4 + y) * 2 + zl) * 2 + c


def permutation(move):
    return [
        (flat_index(x, zh, y, zl, c), flat_index(*move(x, zh, y, zl, c)))
        for x in range(4)
        for zh in range(2)
        for y in range(4)
        for zl in range(2)
        for c in range(2)
    ]


LINKS = {
    "xa": permutation(lambda x, zh, y, zl, c: (x ^ 1, zh, y, zl, c)),
    "xb": permutation(lambda x, zh, y, zl, c: (3 - x, zh, y, zl, c)),
    "ya": permutation(lambda x, zh, y, zl, c: (x, zh, y ^ 1, zl, c)),
    "yb": permutation(lambda x, zh, y, zl, c: (x, zh, 3 - y, zl, c)),
    "zl": permutation(lambda x, zh, y, zl, c: (x, zh, y, zl ^ 1, c)),
    "zz": permutation(lambda x, zh, y, zl, c: (x, zh ^ 1, y, zl ^ 1, c)),
    "zh": permutation(lambda x, zh, y, zl, c: (x, zh ^ 1, y, zl, c)),
    "c": permutation(lambda x, zh, y, zl, c: (x, zh, y, zl, c ^ 1)),
}
ORDERS = (
    ("xa", "xb", "ya", "yb"),
    ("xb", "ya", "yb", "xa"),
    ("ya", "yb", "xa", "xb"),
    ("yb", "xa", "xb", "ya"),
)


def send(value, link):
    return lax.ppermute(value, AXES, LINKS[link])


def dot_nn(a, b):
    return lax.dot_general(a, b, (((1,), (0,)), ((), ())), preferred_element_type=F32)


def dot_nt(a, b):
    return lax.dot_general(a, b, (((1,), (1,)), ((), ())), preferred_element_type=F32)


def dot_tn(a, b):
    return lax.dot_general(a, b, (((0,), (0,)), ((), ())), preferred_element_type=F32)


class Held:
    def __init__(self, source, buffer, sem):
        self.copy = pltpu.make_async_copy(source, buffer, sem)
        self.copy.start()
        self.buffer = buffer
        self.shape = buffer.shape
        self.here = False

    def __getitem__(self, index):
        if not self.here:
            self.copy.wait()
            self.here = True
        return self.buffer[index]


class Gathered:
    def __init__(self, source, buffer, sem, half):
        self.buffer, self.here = buffer, False
        self.copy = pltpu.make_async_copy(source.at[:, pl.ds(64 * half, 64)], buffer, sem)
        self.copy.start()

    def __getitem__(self, index):
        if not self.here:
            self.copy.wait()
            self.here = True
        rows, cols = index
        start, stop = rows.start or 0, rows.stop or 1024
        block = self.buffer[start // 64 : stop // 64, :, cols]
        return block.reshape(stop - start, block.shape[-1])


class Kept:
    def __init__(self, target, buffer, sems):
        self.target, self.buffer, self.sems = target, buffer, sems
        self.shape, self.dtype = buffer.shape, buffer.dtype
        self.copies = []

    def __getitem__(self, index):
        return self.buffer[index]

    def __setitem__(self, index, value):
        self.buffer[index] = value

    def flush(self, index=None):
        source, target = self.buffer, self.target
        if index is not None:
            source, target = source.at[index], target.at[index]
        copy = pltpu.make_async_copy(source, target, self.sems.at[len(self.copies)])
        copy.start()
        self.copies.append(copy)


def flush(ref, index=None):
    if isinstance(ref, Kept):
        ref.flush(index)


def local(kernel, outs, *operands, name, us, scratch=(), limit=16, scalars=0, near_in=(), near_out=(), raw=()):
    small = 1 << 17

    def near(shape, dtype):
        size = jnp.dtype(dtype).itemsize
        for n in shape:
            size *= n
        return size <= small

    ins = [(v.shape, v.dtype) for v in operands]
    in_near = [i in near_in or near(*v) for i, v in enumerate(ins)]
    out_near = [i in near_out or near(*v) for i, v in enumerate(outs)]
    in_bufs = [pltpu.VMEM(*v) for i, v in enumerate(ins) if i >= scalars and not in_near[i] and i not in raw]
    out_bufs = [pltpu.VMEM(*v) for i, v in enumerate(outs) if not out_near[i]]
    user = len(scratch)

    def body(*refs):
        in_refs, refs = refs[: len(ins)], refs[len(ins) :]
        out_refs, refs = refs[: len(outs)], refs[len(outs) :]
        own, refs = refs[:user], list(refs[user:])
        in_sem, out_sem = refs[-2:]
        buffers = iter(refs[:-2])
        wrapped, kept = [], []
        for i, ref in enumerate(in_refs):
            if i < scalars or in_near[i] or i in raw:
                wrapped.append(ref)
            else:
                wrapped.append(Held(ref, next(buffers), in_sem.at[i]))
        for i, ref in enumerate(out_refs):
            if not out_near[i]:
                ref = Kept(ref, next(buffers), out_sem.at[i])
                kept.append(ref)
            wrapped.append(ref)
        kernel(*wrapped, *own)
        for ref in wrapped:
            if isinstance(ref, Held) and not ref.here:
                ref.copy.wait()
        for ref in kept:
            if not ref.copies:
                ref.flush()
        for ref in kept:
            for copy in ref.copies:
                copy.wait()

    vmem = pl.BlockSpec(memory_space=pltpu.VMEM)
    hbm = pl.BlockSpec(memory_space=pltpu.HBM)
    smem = pl.BlockSpec(memory_space=pltpu.SMEM)
    return pl.pallas_call(
        body,
        in_specs=[smem if i < scalars else vmem if in_near[i] else hbm for i in range(len(ins))],
        out_specs=[vmem if v else hbm for v in out_near],
        out_shape=[jax.ShapeDtypeStruct(*o) if v else pltpu.HBM(*o) for o, v in zip(outs, out_near)],
        scratch_shapes=[
            *scratch,
            *in_bufs,
            *out_bufs,
            pltpu.SemaphoreType.DMA((len(ins),)),
            pltpu.SemaphoreType.DMA((len(outs), 2)),
        ],
        compiler_params=pltpu.CompilerParams(vmem_limit_bytes=limit * MIB),
        cost_estimate=pl.CostEstimate(flops=int(us * 1e9), bytes_accessed=MIB, transcendentals=0),
        name=name,
    )(
        *(
            v if i < scalars or in_near[i] else pltpu.with_memory_space_constraint(v, pltpu.HBM)
            for i, v in enumerate(operands)
        )
    )


def after(value, *others):
    return lax.optimization_barrier((value, others))[0]


def head_lanes(shape, head):
    lane = lax.broadcasted_iota(jnp.int32, shape, len(shape) - 1)
    return (lane >> 6) == head


def qkv_kernel(x0, x1, wq, wk, wv, bq, bv, q_ref, k_ref, v_ref):
    for t, x in enumerate((x0, x1)):
        rows = slice(t * TILE, (t + 1) * TILE)
        q_ref[rows, :] = (dot_nn(x[...], wq[...]) + bq[...].astype(F32)).astype(BF16)
        k_ref[rows, :] = dot_nn(x[...], wk[...]).astype(BF16)
        v_ref[rows, :] = (dot_nn(x[...], wv[...]) + bv[...].astype(F32)).astype(BF16)


def attn_fwd_kernel(first, q_ref, k0, k1, v0, v1, mask, wo, ctx_ref, lse_ref, term0, term1):
    rows = q_ref.shape[0]
    half = k0.shape[0]
    q = q_ref[...] * jnp.asarray(HEAD_DIM ** -0.5, BF16)
    mask0 = mask[first : first + rows, :half].astype(F32)
    mask1 = mask[first : first + rows, half:].astype(F32)
    ctx = jnp.zeros(q.shape, F32)
    lse = jnp.zeros((rows, 128), F32)
    lane = lax.broadcasted_iota(jnp.int32, lse.shape, 1)
    for h in range(q.shape[1] // HEAD_DIM):
        mine = head_lanes(q.shape, h)
        qh = jnp.where(mine, q, jnp.zeros_like(q))
        s0 = dot_nt(qh, k0[...]) + mask0
        s1 = dot_nt(qh, k1[...]) + mask1
        top = jnp.max(jnp.maximum(s0, s1), axis=-1, keepdims=True)
        p0 = jnp.exp(s0 - top)
        p1 = jnp.exp(s1 - top)
        total = jnp.sum(p0 + p1, axis=-1, keepdims=True)
        part = (dot_nn(p0.astype(BF16), v0[...]) + dot_nn(p1.astype(BF16), v1[...])) * (1.0 / total)
        ctx = jnp.where(mine, part, ctx)
        lse = jnp.where(lane == h, top + jnp.log(total), lse)
    ctx_ref[...] = ctx.astype(BF16)
    flush(ctx_ref)
    lse_ref[...] = jnp.transpose(lse)[:8]
    term1[...] = dot_nn(ctx_ref[TILE:, :], wo[...]).astype(BF16)
    term0[...] = dot_nn(ctx_ref[:TILE, :], wo[...]).astype(BF16)


def attn_bwd_kernel(up0, up1, wo, q0, k0, k1, v0, v1, mask, lse0, lse1, q1, up2, up3,
                    x0, x1, x2, x3, ctx0, ctx1, note, wq, wk, wv,
                    grads, tok_own, tok_near, tok_far, dq_ref, dk_ref, dv_ref, dk, dv):
    xs = (x0, x1, x2, x3)
    half = k0.shape[0]
    scale = HEAD_DIM ** -0.5
    keys, values = (k0, k1), (v0, v1)
    for t, (q_ref, lse, ups) in enumerate(((q0, lse0, (up0, up1)), (q1, lse1, (up2, up3)))):
        q = q_ref[...] * jnp.asarray(scale, BF16)
        up = jnp.concatenate([ups[0][...], ups[1][...]], axis=0)
        grad = dot_nt(up, wo[...]).astype(BF16)
        dq = jnp.zeros(q.shape, F32)
        for h in range(q.shape[1] // HEAD_DIM):
            mine = head_lanes(q.shape, h)
            qh = jnp.where(mine, q, jnp.zeros_like(q))
            gh = jnp.where(mine, grad, jnp.zeros_like(grad))
            probs, prob_grads, row = [], [], 0.0
            for j in range(2):
                bias = mask[j * half : (j + 1) * half, t * half : (t + 1) * half].astype(F32)
                p = jnp.exp(dot_nt(keys[j][...], qh) + bias - lse[h : h + 1, :])
                dp = dot_nt(values[j][...], gh)
                row = row + jnp.sum(p * dp, axis=0, keepdims=True)
                probs.append(p)
                prob_grads.append(dp)
            part = 0.0
            for j in range(2):
                rows = slice(j * half, (j + 1) * half)
                value_part = dot_nn(probs[j].astype(BF16), gh)
                ds = (probs[j] * (prob_grads[j] - row)).astype(BF16)
                key_part = dot_nn(ds, qh)
                if t == 0 and h == 0:
                    dv[rows, :] = value_part
                    dk[rows, :] = key_part
                else:
                    dv[rows, :] += value_part
                    dk[rows, :] += key_part
                part = part + dot_tn(ds, keys[j][...])
            dq = jnp.where(mine, part, dq)
        dq_ref[t * half : (t + 1) * half, :] = (dq * scale).astype(BF16)
    dk_ref[...] = dk[...].astype(BF16)
    dv_ref[...] = dv[...].astype(BF16)
    inner = dq_ref.shape[1]
    rows = [slice(j * TILE, (j + 1) * TILE) for j in range(4)]
    note_rows = []
    for i, grad in enumerate((dq_ref, dk_ref, dv_ref)):
        total = dot_tn(xs[0][...], grad[rows[0], :])
        for j in range(1, 4):
            total = total + dot_tn(xs[j][...], grad[rows[j], :])
        grads[:, i * inner : (i + 1) * inner] = total.astype(BF16)
        if i != 1:
            note_rows.append(column_sum(grad[...].astype(F32)))
    total = 0.0
    for j, up in enumerate((up0, up1, up2, up3)):
        total = total + dot_tn(up[...], (ctx0, ctx1)[j // 2][rows[j % 2], :])
    grads[:, 3 * inner : 4 * inner] = total.astype(BF16)
    highs = [v.astype(BF16).astype(F32) for v in note_rows]
    lows = [v - high for v, high in zip(note_rows, highs)]
    tile = jnp.concatenate([note[: 32 - 4], *highs, *lows], axis=0).astype(BF16)
    for r in range(32):
        grads[r * 32 : (r + 1) * 32, 4 * inner :] = tile
    flush(grads)
    for j in (3, 1, 2, 0):
        total = dot_nt(dq_ref[rows[j], :], wq[...]) + dot_nt(dk_ref[rows[j], :], wk[...]) + dot_nt(dv_ref[rows[j], :], wv[...])
        if j == 0:
            tok_own[...] = total
        elif j == 2:
            tok_far[...] = total.astype(BF16)
        else:
            tok_near[(j // 2) * TILE : (j // 2 + 1) * TILE, :] = total.astype(BF16)


def normal_of(rows):
    center = jnp.mean(rows, axis=-1, keepdims=True)
    centred = rows - center
    scale = lax.rsqrt(jnp.mean(centred * centred, axis=-1, keepdims=True) + 1e-06)
    return centred * scale, scale


def normal_back(up, gain, normal, scale):
    scaled = up * gain
    mean_up = jnp.mean(scaled, axis=-1, keepdims=True)
    mean_un = jnp.mean(scaled * normal, axis=-1, keepdims=True)
    return scale * (scaled - mean_up - normal * mean_un)


def stack_rows(*rows):
    width = rows[0].shape[1]
    return jnp.concatenate([*rows, jnp.zeros((8 - len(rows), width), F32)], axis=0)


def column_sum(rows):
    return jnp.sum(rows, axis=0, keepdims=True)


def norm1_kernel(x, own, near, far, bias, gain, shift, normal_ref, scale_ref, low_ref):
    rows = x[...].astype(F32) + bias[...].astype(F32)
    rows = rows + own[...].astype(F32) + near[...].astype(F32) + far[...].astype(F32)
    normal, scale = normal_of(rows)
    normal_ref[...] = normal
    flush(normal_ref)
    scale_ref[...] = jnp.broadcast_to(scale, scale_ref.shape)
    low_ref[...] = (normal * gain[...].astype(F32) + shift[...].astype(F32)).astype(BF16)


def norm2_kernel(normal1, own, near, gain1, shift1, bias, gain, shift, cot_ref, out_ref, grad_ref, low_ref, sums_ref):
    rows = normal1[...] * gain1[...].astype(F32) + shift1[...].astype(F32) + bias[...].astype(F32)
    rows = rows + own[...] + near[...].astype(F32)
    normal, scale = normal_of(rows)
    gain_row = gain[...].astype(F32)
    cot = cot_ref[...].astype(F32)
    grad = normal_back(cot, gain_row, normal, scale)
    low_ref[...] = grad.astype(BF16)
    grad_ref[...] = grad
    out_ref[...] = (normal * gain_row + shift[...].astype(F32)).astype(BF16)
    flush(out_ref)
    sums_ref[...] = stack_rows(column_sum(cot * normal), column_sum(cot), column_sum(grad))


def norm1_back_kernel(up_ref, own, near, normal_ref, scale_ref, gain, sums2, hidden_sums, grad_ref, low_ref, sums_ref):
    up = up_ref[...] + own[...] + near[...].astype(F32)
    normal = normal_ref[...]
    grad = normal_back(up, gain[...].astype(F32), normal, scale_ref[:, 0:1])
    low_ref[...] = grad.astype(BF16)
    flush(low_ref)
    grad_ref[...] = grad
    flush(grad_ref)
    sums_ref[...] = jnp.concatenate(
        [sums2[0:3], column_sum(up * normal), column_sum(up), column_sum(grad), hidden_sums[1:2], hidden_sums[0:1]],
        axis=0,
    )


def mlp_fwd_kernel(n0, n1, wi, wo, rest, bias0, bias1, act0, act1, der0, der1, own, near, wi_far, wo_far, sems):
    wi_far = Gathered(rest, wi_far, sems.at[0], 0)
    wo_far = Gathered(rest, wo_far, sems.at[1], 1)
    width = n0.shape[1]
    chunk = 512
    for b, (bias, act, der) in enumerate(((bias0, act0, der0), (bias1, act1, der1))):
        for c in range(0, act.shape[1], chunk):
            cols = slice(c, c + chunk)
            weight = wi[:, cols] if b == 0 else wi_far[0:width, cols]
            for t, n in enumerate((n0, n1)):
                rows = slice(t * TILE, (t + 1) * TILE)
                u = dot_nn(n[...], weight) + bias[:, cols].astype(F32)
                square = u * u
                th = jnp.tanh(0.7978845608028654 * u * (1.0 + 0.044715 * square))
                half = 0.5 * (1.0 + th)
                act[rows, cols] = (u * half).astype(BF16)
                slope = 0.7978845608028654 * (1.0 + 3.0 * 0.044715 * square)
                der[rows, cols] = (half + 0.5 * u * (1.0 - th * th) * slope).astype(BF16)
        flush(act)
    for c in range(0, width, 256):
        cols = slice(c, c + 256)
        other = wo_far[0:1024, cols]
        near[:, cols] = (dot_nn(act0[TILE:], wo[:, cols]) + dot_nn(act1[TILE:], other)).astype(BF16)
        own[:, cols] = dot_nn(act0[:TILE], wo[:, cols]) + dot_nn(act1[:TILE], other)


def mlp_bwd_kernel(m0, m1, wo, wi, rest, der0, der1, hg0, hg1, own, near, sums_ref, wi_far, wo_far, sems):
    wo_far = Gathered(rest, wo_far, sems.at[1], 1)
    wi_far = Gathered(rest, wi_far, sems.at[0], 0)
    units, width = wo.shape
    chunk = 512
    sums_ref[...] = jnp.zeros_like(sums_ref)
    for b, (der, hg) in enumerate(((der0, hg0), (der1, hg1))):
        for c in range(0, units, chunk):
            cols = slice(c, c + chunk)
            weight = wo[cols, :] if b == 0 else wo_far[cols, 0:width]
            total = 0.0
            for t, m in enumerate((m0, m1)):
                rows = slice(t * TILE, (t + 1) * TILE)
                low = (dot_nt(m[...], weight) * der[rows, cols].astype(F32)).astype(BF16)
                hg[rows, cols] = low
                total = total + column_sum(low.astype(F32))
            sums_ref[b : b + 1, cols] = total
        flush(hg)
    for c in range(0, width, 256):
        cols = slice(c, c + 256)
        other = wi_far[cols, 0:1024]
        near[:, cols] = (dot_nt(hg0[TILE:], wi[cols, :]) + dot_nt(hg1[TILE:], other)).astype(BF16)
        own[:, cols] = dot_nt(hg0[:TILE], wi[cols, :]) + dot_nt(hg1[:TILE], other)


def gray(p):
    return p ^ (p >> 1)


def block_index(order, jx, jy):
    bit = {"xa": jx & 1, "xb": jx >> 1, "ya": jy & 1, "yb": jy >> 1}
    index = 0
    for link in order:
        index = index * 2 + bit[link]
    return index


def mlp_grads_kernel(place, n0, n1, hg0, hg1, m0, m1, act0, act1, *rest):
    outs, scratch = rest[:8], rest[8]
    x_here, zh_here, y_here = place[0], place[1], place[2]
    for mat, (lefts, rights) in enumerate((((n0, n1), (hg0, hg1)), ((m0, m1), (act0, act1)))):
        for jx in range(4):
            cols = pl.ds(pl.multiple_of(gray(gray(x_here) ^ jx) * 256, 256), 256)
            for b in range(2):
                slot = b
                scratch[slot] = (
                    dot_tn(lefts[0][:, cols], rights[b][:TILE, :]) + dot_tn(lefts[1][:, cols], rights[b][TILE:, :])
                ).astype(BF16)
                for jy in range(4):
                    y_there = gray(gray(y_here) ^ jy)
                    for a in range(2):
                        off = pl.multiple_of((zh_here ^ a) * 128 + y_there * 32, 32)
                        block = scratch[slot, pl.ds(off, 32), :]
                        for r, order in enumerate(ORDERS):
                            index = block_index(order, jx, jy)
                            out = outs[2 * r + (index >> 3)]
                            out[index & 7, mat, b, a] = block[:, r * 256 : (r + 1) * 256]
        for out in outs:
            flush(out, (slice(None), mat))


def add_step_kernel(*refs):
    count = len(ORDERS)
    keeps, keeps_on, cames, cames_on, stays, goes = (refs[i * count : (i + 1) * count] for i in range(6))
    for keep, came, out in zip((*keeps, *keeps_on), (*cames, *cames_on), (*stays, *goes)):
        out[...] = (keep[...].astype(F32) + came[...].astype(F32)).astype(BF16)


def add_step(keep, came, name):
    half = keep[0].shape[0] // 2
    rest = keep[0].shape[1:]
    stay = pl.BlockSpec((1, *rest), lambda i: (i, 0, 0, 0, 0, 0))
    go = pl.BlockSpec((1, *rest), lambda i: (i + half, 0, 0, 0, 0, 0))
    return pl.pallas_call(
        add_step_kernel,
        grid=(half,),
        in_specs=[stay] * 4 + [go] * 4 + [stay] * 4 + [go] * 4,
        out_specs=[stay] * 8,
        out_shape=[jax.ShapeDtypeStruct((half, *rest), BF16)] * 8,
        compiler_params=pltpu.CompilerParams(vmem_limit_bytes=12 * MIB),
        cost_estimate=pl.CostEstimate(flops=int(half * 1e9), bytes_accessed=MIB, transcendentals=0),
        name=name,
    )(*keep, *keep, *came, *came)


def add_last_kernel(*refs):
    count = len(ORDERS)
    keeps, cames, ways = refs[:count], refs[count : 2 * count], refs[2 * count :]
    for r, (keep, came) in enumerate(zip(keeps, cames)):
        for b in range(2):
            for a in range(2):
                for mat in range(2):
                    total = keep[0, mat, b, a].astype(F32) + came[0, mat, b, a].astype(F32)
                    out = ways[2 * b + a]
                    out[mat, :, r * 256 : (r + 1) * 256] = total.astype(out.dtype)


def finish_kernel(moved, query, key, value, output, query_bias, value_bias, *vectors):
    total = moved[0].astype(F32)
    for i in range(1, moved.shape[0]):
        total = total + moved[i].astype(F32)
    inner = query.shape[1]
    for i, out in enumerate((query, key, value)):
        out[...] = total[:, i * inner : (i + 1) * inner]
    output[...] = jnp.transpose(total[:, 3 * inner : 4 * inner])
    notes = total[:, 4 * inner :]
    query_bias[...] = notes[28:29] + notes[30:31]
    value_bias[...] = notes[29:30] + notes[31:32]
    for i, out in enumerate(vectors):
        for j in range(4):
            out[:, j * inner : (j + 1) * inner] = notes[4 * i + j : 4 * i + j + 1]


def finish_mlp_kernel(here, way1, way2, way3, wi_grad, wo_grad):
    ways = (way1, way2, way3)
    wi_grad[...] = here[0] + sum(w[0].astype(F32) for w in ways)
    wo_grad[...] = jnp.transpose(here[1] + sum(w[1].astype(F32) for w in ways))


def add_low(a, b):
    return (a.astype(F32) + b.astype(F32)).astype(BF16)


def per_device(
    tokens,
    segments,
    query_weight,
    query_bias,
    key_weight,
    value_weight,
    value_bias,
    output_weight,
    output_bias,
    first_gain,
    first_shift,
    inner_weight,
    inner_bias,
    outer_weight,
    outer_bias,
    second_gain,
    second_shift,
    cotangent,
):
    x_here, zh_here, y_here = lax.axis_index("x"), lax.axis_index("zh"), lax.axis_index("y")
    zl_here, c_here = lax.axis_index("zl"), lax.axis_index("c")
    width = tokens.shape[2]
    inner = query_weight.shape[1]
    units = inner_weight.shape[1]
    length = 4 * TILE
    row = lambda v: v.reshape(1, -1)

    x0 = tokens[0]
    x2 = send(x0, "zl")
    x1 = send(x0, "c")
    inner_bias_far = send(row(inner_bias), "zl")

    block = (x_here * 4 + y_here) * 64
    piece = jnp.concatenate(
        [lax.dynamic_slice_in_dim(w, block, 64, 0) for w in (inner_weight, outer_weight)], axis=0
    )
    piece = send(after(piece, x1), "zl")


    gathered = lax.all_gather(piece, ("x", "y"), axis=0)
    place = jnp.stack([x_here, zh_here, y_here]).astype(jnp.int32)

    seg = segments[0].reshape(2, 2, TILE)
    seg = jnp.where(zl_here == 1, seg[::-1], seg)
    seg = jnp.where(c_here == 1, seg[:, ::-1], seg).reshape(-1)
    spot = jnp.arange(length, dtype=jnp.int32)
    pos = ((spot // TILE) ^ (zl_here * 2 + c_here)) * TILE + spot % TILE
    allowed = (seg[:, None] == seg[None, :]) & (jnp.abs(pos[:, None] - pos[None, :]) <= WINDOW)
    mask = jnp.where(allowed, 0.0, -1e30).astype(BF16)

    def project(a, b, near_in):
        return local(
            qkv_kernel, [((2 * TILE, inner), BF16)] * 3,
            a, b, query_weight, key_weight, value_weight, row(query_bias), row(value_bias),
            name="qkv", us=2, near_in=near_in, near_out=(0, 1, 2),
        )

    q0, k0, v0 = project(x0, x1, (1,))
    x2 = after(x2, (inner_bias_far, q0))
    x3 = send(x2, "c")
    q1, k1, v1 = project(x2, x3, (0, 1))

    def attend(q, first):
        return local(
            functools.partial(attn_fwd_kernel, first),
            [((2 * TILE, inner), BF16), ((8, 2 * TILE), F32), ((TILE, width), BF16), ((TILE, width), BF16)],
            q, k0, k1, v0, v1, mask, output_weight,
            name="attn_fwd", us=5, near_in=(0, 1, 2, 3, 4, 5), near_out=(2, 3),
        )

    ctx1, lse1, term2, term3 = attend(q1, 2 * TILE)
    from_far = send(add_low(term2, send(term3, "c")), "zl")
    ctx0, lse0, term0, term1 = attend(after(q0, term2), 0)
    from_near = send(term1, "c")

    normal1, scale1, n0 = local(
        norm1_kernel,
        [((TILE, width), F32), ((TILE, 128), F32), ((TILE, width), BF16)],
        x0, term0, from_near, from_far, row(output_bias), row(first_gain), row(first_shift),
        name="norm1", us=1.5, near_in=(1, 2, 3), near_out=(2,),
    )
    n1 = send(n0, "c")
    far_weights = [pltpu.VMEM((16, 64, units), BF16)] * 2 + [pltpu.SemaphoreType.DMA((2,))]
    act0, act1, der0, der1, mlp_own, mlp_near = local(
        mlp_fwd_kernel,
        [((2 * TILE, units), BF16)] * 4 + [((TILE, width), F32), ((TILE, width), BF16)],
        n0, n1, inner_weight, outer_weight, gathered, row(inner_bias), inner_bias_far,
        name="mlp_fwd", us=8.5, limit=24, near_in=(0, 1), near_out=(2, 3, 4, 5),
        raw=(4,), scratch=far_weights,
    )
    layer_out, second_grad, m0, sums2 = local(
        norm2_kernel,
        [((TILE, width), BF16), ((TILE, width), F32), ((TILE, width), BF16), ((8, width), F32)],
        normal1, mlp_own, send(mlp_near, "c"), row(first_gain), row(first_shift), row(outer_bias),
        row(second_gain), row(second_shift), cotangent[0],
        name="norm2", us=2, near_in=(1, 2), near_out=(1, 2),
    )
    m1 = send(m0, "c")
    hg0, hg1, back_own, back_near, hidden_sums = local(
        mlp_bwd_kernel,
        [((2 * TILE, units), BF16)] * 2 + [((TILE, width), F32), ((TILE, width), BF16), ((8, units), F32)],
        m0, m1, outer_weight, inner_weight, gathered, der0, der1,
        name="mlp_bwd", us=6, limit=24, near_in=(0, 1, 2, 5, 6), near_out=(2, 3),
        raw=(4,), scratch=far_weights,
    )
    first_grad, u0, sums = local(
        norm1_back_kernel,
        [((TILE, width), F32), ((TILE, width), BF16), ((8, width), F32)],
        second_grad, back_own, send(back_near, "c"), normal1, scale1, row(first_gain), sums2, hidden_sums,
        name="norm1_back", us=2, near_in=(0, 1, 2),
    )
    u2 = send(u0, "zl")
    u1 = send(u0, "c")

    parts = local(
        mlp_grads_kernel,
        [((8, 2, 2, 2, 32, 256), BF16)] * 8,
        after(place, u0), n0, n1, hg0, hg1, m0, m1, act0, act1,
        name="mlp_grads", us=8.5, limit=20, scalars=1, scratch=[pltpu.VMEM((2, 256, units), BF16)],
    )
    keep, out = parts[0::2], parts[1::2]
    came = [send(v, order[0]) for v, order in zip(out, ORDERS)]

    total = sums[:6] + send(sums[:6], "c")
    far = send(jnp.concatenate([total, sums[6:7]], axis=0), "zl")
    total = jnp.concatenate([total + far[:6], sums[7:8] + far[6:7]], axis=0)
    note = jnp.pad(total.reshape(7 * width // inner, inner), ((0, 32 - 7 * width // inner), (0, 0)))

    u2 = after(u2, parts[0])
    u3 = send(u2, "c")
    attn_grads, tok_own, tok_near, tok_far = local(
        attn_bwd_kernel,
        [((width, 5 * inner), BF16), ((TILE, width), F32), ((2 * TILE, width), BF16), ((TILE, width), BF16)],
        u0, u1, output_weight, q0, k0, k1, v0, v1, mask, lse0, lse1, q1, u2, u3,
        x0, x1, x2, x3, ctx0, ctx1, note, query_weight, key_weight, value_weight,
        name="attn_bwd", us=23, limit=32, near_in=(0, 1, 12, 13), near_out=(1, 2, 3),
        scratch=[pltpu.VMEM((length, inner), BF16)] * 3 + [pltpu.VMEM((length, inner), F32)] * 2,
    )
    moved = lax.all_to_all(attn_grads, REPLICA, split_axis=0, concat_axis=0, tiled=True)
    tok_near = send(tok_near, "c")
    tok_sum = add_low(tok_far, tok_near[TILE:])
    tok_far = send(tok_sum, "zl")

    came[0] = after(came[0], tok_own)
    for step in range(1, 4):
        if step == 2:
            came[0] = after(came[0], tok_far)
        both = add_step(keep, came, f"add{step}")
        keep, out = both[:4], both[4:]
        came = [send(v, order[step]) for v, order in zip(out, ORDERS)]
    ways = local(
        add_last_kernel,
        [((2, 32, units), F32)] + [((2, 32, units), BF16)] * 3,
        *keep, *came, name="add4", us=1, near_in=range(8), near_out=range(4),
    )
    wi_grad, wo_grad = local(
        finish_mlp_kernel,
        [((32, units), F32), ((units, 32), F32)],
        ways[0], *(send(way, link) for way, link in zip(ways[1:], ("zh", "zl", "zz"))),
        name="finish_mlp", us=1, near_in=range(4), near_out=range(2),
    )
    finished = local(
        finish_kernel,
        [((32, inner), F32)] * 3 + [((inner, 32), F32)] + [((1, inner), F32)] * 2 + [((1, width), F32)] * 7,
        moved.reshape(32, 32, 5 * inner),
        name="finish", us=3, near_out=range(13),
    )
    vectors = [v.reshape(-1) for v in finished[4:]]
    tokens_grad = first_grad + tok_own + tok_near[:TILE].astype(F32) + tok_far.astype(F32)
    return (
        layer_out[None],
        tokens_grad[None],
        finished[0],
        vectors[0],
        finished[1],
        finished[2],
        vectors[1],
        finished[3],
        vectors[7],
        vectors[5],
        vectors[6],
        wi_grad,
        vectors[8],
        wo_grad,
        vectors[4],
        vectors[2],
        vectors[3],
    )


def solution(mesh):
    fine = Mesh(mesh.devices.reshape(4, 2, 4, 2, 2), AXES)
    shard = ("zl", "c")
    placed = (
        P(REPLICA, shard, None),
        P(REPLICA, None),
        P(None, shard),
        P(shard),
        P(None, shard),
        P(None, shard),
        P(shard),
        P(shard, None),
        P(),
        P(),
        P(),
        P(None, shard),
        P(shard),
        P(shard, None),
        P(),
        P(),
        P(),
        P(REPLICA, shard, None),
    )
    return jax.shard_map(
        per_device,
        mesh=fine,
        in_specs=placed,
        out_specs=(
            P(REPLICA, shard, None),
            P(REPLICA, shard, None),
            P(REPLICA, shard),
            P(shard),
            P(REPLICA, shard),
            P(REPLICA, shard),
            P(shard),
            P(shard, REPLICA),
            P(),
            P(),
            P(),
            P(REPLICA, shard),
            P(shard),
            P(shard, REPLICA),
            P(),
            P(),
            P(),
        ),
        check_vma=False,
    )
```

```python
import functools

import jax
import jax.numpy as jnp
from jax import lax
from jax.experimental import pallas as pl
from jax.experimental.pallas import tpu as pltpu
from jax.sharding import Mesh, PartitionSpec as P

HEAD_DIM = 64
WINDOW = 512
TILE = 256
AXES = ("x", "zh", "y", "zl", "c")
REPLICA = ("x", "zh", "y")
F32 = jnp.float32
BF16 = jnp.bfloat16
MIB = 1 << 20


def flat_index(x, zh, y, zl, c):
    return (((x * 2 + zh) * 4 + y) * 2 + zl) * 2 + c


def permutation(move):
    return [
        (flat_index(x, zh, y, zl, c), flat_index(*move(x, zh, y, zl, c)))
        for x in range(4)
        for zh in range(2)
        for y in range(4)
        for zl in range(2)
        for c in range(2)
    ]


LINKS = {
    "xa": permutation(lambda x, zh, y, zl, c: (x ^ 1, zh, y, zl, c)),
    "xb": permutation(lambda x, zh, y, zl, c: (3 - x, zh, y, zl, c)),
    "ya": permutation(lambda x, zh, y, zl, c: (x, zh, y ^ 1, zl, c)),
    "yb": permutation(lambda x, zh, y, zl, c: (x, zh, 3 - y, zl, c)),
    "zl": permutation(lambda x, zh, y, zl, c: (x, zh, y, zl ^ 1, c)),
    "zz": permutation(lambda x, zh, y, zl, c: (x, zh ^ 1, y, zl ^ 1, c)),
    "zh": permutation(lambda x, zh, y, zl, c: (x, zh ^ 1, y, zl, c)),
    "c": permutation(lambda x, zh, y, zl, c: (x, zh, y, zl, c ^ 1)),
}
ORDERS = (
    ("xa", "xb", "ya", "yb"),
    ("xb", "ya", "yb", "xa"),
    ("ya", "yb", "xa", "xb"),
    ("yb", "xa", "xb", "ya"),
)


def send(value, link):
    return lax.ppermute(value, AXES, LINKS[link])


def dot_nn(a, b):
    return lax.dot_general(a, b, (((1,), (0,)), ((), ())), preferred_element_type=F32)


def dot_nt(a, b):
    return lax.dot_general(a, b, (((1,), (1,)), ((), ())), preferred_element_type=F32)


def dot_tn(a, b):
    return lax.dot_general(a, b, (((0,), (0,)), ((), ())), preferred_element_type=F32)


class Held:
    def __init__(self, source, buffer, sem):
        self.copy = pltpu.make_async_copy(source, buffer, sem)
        self.copy.start()
        self.buffer = buffer
        self.shape = buffer.shape
        self.here = False

    def __getitem__(self, index):
        if not self.here:
            self.copy.wait()
            self.here = True
        return self.buffer[index]


class Gathered:
    def __init__(self, source, buffer, sem, half):
        self.buffer, self.here = buffer, False
        self.copy = pltpu.make_async_copy(source.at[:, pl.ds(64 * half, 64)], buffer, sem)
        self.copy.start()

    def __getitem__(self, index):
        if not self.here:
            self.copy.wait()
            self.here = True
        rows, cols = index
        start, stop = rows.start or 0, rows.stop or 1024
        block = self.buffer[start // 64 : stop // 64, :, cols]
        return block.reshape(stop - start, block.shape[-1])


class Kept:
    def __init__(self, target, buffer, sems):
        self.target, self.buffer, self.sems = target, buffer, sems
        self.shape, self.dtype = buffer.shape, buffer.dtype
        self.copies = []

    def __getitem__(self, index):
        return self.buffer[index]

    def __setitem__(self, index, value):
        self.buffer[index] = value

    def flush(self, index=None):
        source, target = self.buffer, self.target
        if index is not None:
            source, target = source.at[index], target.at[index]
        copy = pltpu.make_async_copy(source, target, self.sems.at[len(self.copies)])
        copy.start()
        self.copies.append(copy)


def flush(ref, index=None):
    if isinstance(ref, Kept):
        ref.flush(index)


def local(kernel, outs, *operands, name, us, scratch=(), limit=16, scalars=0, near_in=(), near_out=(), raw=()):
    small = 1 << 17

    def near(shape, dtype):
        size = jnp.dtype(dtype).itemsize
        for n in shape:
            size *= n
        return size <= small

    ins = [(v.shape, v.dtype) for v in operands]
    in_near = [i in near_in or near(*v) for i, v in enumerate(ins)]
    out_near = [i in near_out or near(*v) for i, v in enumerate(outs)]
    in_bufs = [pltpu.VMEM(*v) for i, v in enumerate(ins) if i >= scalars and not in_near[i] and i not in raw]
    out_bufs = [pltpu.VMEM(*v) for i, v in enumerate(outs) if not out_near[i]]
    user = len(scratch)

    def body(*refs):
        in_refs, refs = refs[: len(ins)], refs[len(ins) :]
        out_refs, refs = refs[: len(outs)], refs[len(outs) :]
        own, refs = refs[:user], list(refs[user:])
        in_sem, out_sem = refs[-2:]
        buffers = iter(refs[:-2])
        wrapped, kept = [], []
        for i, ref in enumerate(in_refs):
            if i < scalars or in_near[i] or i in raw:
                wrapped.append(ref)
            else:
                wrapped.append(Held(ref, next(buffers), in_sem.at[i]))
        for i, ref in enumerate(out_refs):
            if not out_near[i]:
                ref = Kept(ref, next(buffers), out_sem.at[i])
                kept.append(ref)
            wrapped.append(ref)
        kernel(*wrapped, *own)
        for ref in wrapped:
            if isinstance(ref, Held) and not ref.here:
                ref.copy.wait()
        for ref in kept:
            if not ref.copies:
                ref.flush()
        for ref in kept:
            for copy in ref.copies:
                copy.wait()

    vmem = pl.BlockSpec(memory_space=pltpu.VMEM)
    hbm = pl.BlockSpec(memory_space=pltpu.HBM)
    smem = pl.BlockSpec(memory_space=pltpu.SMEM)
    return pl.pallas_call(
        body,
        in_specs=[smem if i < scalars else vmem if in_near[i] else hbm for i in range(len(ins))],
        out_specs=[vmem if v else hbm for v in out_near],
        out_shape=[jax.ShapeDtypeStruct(*o) if v else pltpu.HBM(*o) for o, v in zip(outs, out_near)],
        scratch_shapes=[
            *scratch,
            *in_bufs,
            *out_bufs,
            pltpu.SemaphoreType.DMA((len(ins),)),
            pltpu.SemaphoreType.DMA((len(outs), 2)),
        ],
        compiler_params=pltpu.CompilerParams(vmem_limit_bytes=limit * MIB),
        cost_estimate=pl.CostEstimate(flops=int(us * 1e9), bytes_accessed=MIB, transcendentals=0),
        name=name,
    )(
        *(
            v if i < scalars or in_near[i] else pltpu.with_memory_space_constraint(v, pltpu.HBM)
            for i, v in enumerate(operands)
        )
    )


def after(value, *others):
    return lax.optimization_barrier((value, others))[0]


def head_lanes(shape, head):
    lane = lax.broadcasted_iota(jnp.int32, shape, len(shape) - 1)
    return (lane >> 6) == head


def qkv_kernel(x0, x1, wq, wk, wv, bq, bv, q_ref, k_ref, v_ref):
    for t, x in enumerate((x0, x1)):
        rows = slice(t * TILE, (t + 1) * TILE)
        q_ref[rows, :] = (dot_nn(x[...], wq[...]) + bq[...].astype(F32)).astype(BF16)
        k_ref[rows, :] = dot_nn(x[...], wk[...]).astype(BF16)
        v_ref[rows, :] = (dot_nn(x[...], wv[...]) + bv[...].astype(F32)).astype(BF16)


def attn_fwd_kernel(first, q_ref, k0, k1, v0, v1, mask, wo, ctx_ref, lse_ref, term0, term1):
    rows = q_ref.shape[0]
    half = k0.shape[0]
    q = q_ref[...] * jnp.asarray(HEAD_DIM ** -0.5, BF16)
    mask0 = mask[first : first + rows, :half].astype(F32)
    mask1 = mask[first : first + rows, half:].astype(F32)
    ctx = jnp.zeros(q.shape, F32)
    lse = jnp.zeros((rows, 128), F32)
    lane = lax.broadcasted_iota(jnp.int32, lse.shape, 1)
    for h in range(q.shape[1] // HEAD_DIM):
        mine = head_lanes(q.shape, h)
        qh = jnp.where(mine, q, jnp.zeros_like(q))
        s0 = dot_nt(qh, k0[...]) + mask0
        s1 = dot_nt(qh, k1[...]) + mask1
        top = jnp.max(jnp.maximum(s0, s1), axis=-1, keepdims=True)
        p0 = jnp.exp(s0 - top)
        p1 = jnp.exp(s1 - top)
        total = jnp.sum(p0 + p1, axis=-1, keepdims=True)
        part = (dot_nn(p0.astype(BF16), v0[...]) + dot_nn(p1.astype(BF16), v1[...])) * (1.0 / total)
        ctx = jnp.where(mine, part, ctx)
        lse = jnp.where(lane == h, top + jnp.log(total), lse)
    ctx_ref[...] = ctx.astype(BF16)
    flush(ctx_ref)
    lse_ref[...] = jnp.transpose(lse)[:8]
    term1[...] = dot_nn(ctx_ref[TILE:, :], wo[...]).astype(BF16)
    term0[...] = dot_nn(ctx_ref[:TILE, :], wo[...]).astype(BF16)


def attn_bwd_kernel(up0, up1, wo, q0, k0, k1, v0, v1, mask, lse0, lse1, q1, up2, up3,
                    x0, x1, x2, x3, ctx0, ctx1, wq, wk, wv,
                    grads, tok_own, tok_near, tok_far, sums_ref, dq_ref, dk_ref, dv_ref, dk, dv):
    xs = (x0, x1, x2, x3)
    half = k0.shape[0]
    scale = HEAD_DIM ** -0.5
    keys, values = (k0, k1), (v0, v1)
    for t, (q_ref, lse, ups) in enumerate(((q0, lse0, (up0, up1)), (q1, lse1, (up2, up3)))):
        q = q_ref[...] * jnp.asarray(scale, BF16)
        up = jnp.concatenate([ups[0][...], ups[1][...]], axis=0)
        grad = dot_nt(up, wo[...]).astype(BF16)
        dq = jnp.zeros(q.shape, F32)
        for h in range(q.shape[1] // HEAD_DIM):
            mine = head_lanes(q.shape, h)
            qh = jnp.where(mine, q, jnp.zeros_like(q))
            gh = jnp.where(mine, grad, jnp.zeros_like(grad))
            probs, prob_grads, row = [], [], 0.0
            for j in range(2):
                bias = mask[j * half : (j + 1) * half, t * half : (t + 1) * half].astype(F32)
                p = jnp.exp(dot_nt(keys[j][...], qh) + bias - lse[h : h + 1, :])
                dp = dot_nt(values[j][...], gh)
                row = row + jnp.sum(p * dp, axis=0, keepdims=True)
                probs.append(p)
                prob_grads.append(dp)
            part = 0.0
            for j in range(2):
                rows = slice(j * half, (j + 1) * half)
                value_part = dot_nn(probs[j].astype(BF16), gh)
                ds = (probs[j] * (prob_grads[j] - row)).astype(BF16)
                key_part = dot_nn(ds, qh)
                if t == 0 and h == 0:
                    dv[rows, :] = value_part
                    dk[rows, :] = key_part
                else:
                    dv[rows, :] += value_part
                    dk[rows, :] += key_part
                part = part + dot_tn(ds, keys[j][...])
            dq = jnp.where(mine, part, dq)
        dq_ref[t * half : (t + 1) * half, :] = (dq * scale).astype(BF16)
    dk_ref[...] = dk[...].astype(BF16)
    dv_ref[...] = dv[...].astype(BF16)
    inner = dq_ref.shape[1]
    rows = [slice(j * TILE, (j + 1) * TILE) for j in range(4)]
    bias_rows = []

    def place(total, i):
        low = total.astype(BF16)
        for x in range(4):
            for zh in range(2):
                for y in range(4):
                    source, target = (x * 8 + zh * 4 + y) * 32, (y * 8 + x * 2 + zh) * 32
                    grads[target : target + 32, i * inner : (i + 1) * inner] = low[source : source + 32]

    for i, grad in enumerate((dq_ref, dk_ref, dv_ref)):
        total = dot_tn(xs[0][...], grad[rows[0], :])
        for j in range(1, 4):
            total = total + dot_tn(xs[j][...], grad[rows[j], :])
        place(total, i)
        if i != 1:
            bias_rows.append(column_sum(grad[...].astype(F32)))
    total = 0.0
    for j, up in enumerate((up0, up1, up2, up3)):
        total = total + dot_tn(up[...], (ctx0, ctx1)[j // 2][rows[j % 2], :])
    place(total, 3)
    flush(grads)
    sums_ref[...] = stack_rows(*bias_rows)
    for j in (3, 1, 2, 0):
        total = dot_nt(dq_ref[rows[j], :], wq[...]) + dot_nt(dk_ref[rows[j], :], wk[...]) + dot_nt(dv_ref[rows[j], :], wv[...])
        if j == 0:
            tok_own[...] = total
        elif j == 2:
            tok_far[...] = total.astype(BF16)
            flush(tok_far)
        else:
            tok_near[(j // 2) * TILE : (j // 2 + 1) * TILE, :] = total.astype(BF16)
            if j == 1:
                flush(tok_near)


def normal_of(rows):
    center = jnp.mean(rows, axis=-1, keepdims=True)
    centred = rows - center
    scale = lax.rsqrt(jnp.mean(centred * centred, axis=-1, keepdims=True) + 1e-06)
    return centred * scale, scale


def normal_back(up, gain, normal, scale):
    scaled = up * gain
    mean_up = jnp.mean(scaled, axis=-1, keepdims=True)
    mean_un = jnp.mean(scaled * normal, axis=-1, keepdims=True)
    return scale * (scaled - mean_up - normal * mean_un)


def stack_rows(*rows):
    width = rows[0].shape[1]
    return jnp.concatenate([*rows, jnp.zeros((8 - len(rows), width), F32)], axis=0)


def column_sum(rows):
    return jnp.sum(rows, axis=0, keepdims=True)


def norm1_kernel(x, own, near, far, bias, gain, shift, normal_ref, scale_ref, low_ref):
    rows = x[...].astype(F32) + bias[...].astype(F32)
    rows = rows + own[...].astype(F32) + near[...].astype(F32) + far[...].astype(F32)
    normal, scale = normal_of(rows)
    normal_ref[...] = normal
    flush(normal_ref)
    scale_ref[...] = jnp.broadcast_to(scale, scale_ref.shape)
    low_ref[...] = (normal * gain[...].astype(F32) + shift[...].astype(F32)).astype(BF16)


def norm2_kernel(normal1, own, near, gain1, shift1, bias, gain, shift, cot_ref, out_ref, grad_ref, low_ref, sums_ref):
    rows = normal1[...] * gain1[...].astype(F32) + shift1[...].astype(F32) + bias[...].astype(F32)
    rows = rows + own[...] + near[...].astype(F32)
    normal, scale = normal_of(rows)
    gain_row = gain[...].astype(F32)
    cot = cot_ref[...].astype(F32)
    grad = normal_back(cot, gain_row, normal, scale)
    low_ref[...] = grad.astype(BF16)
    grad_ref[...] = grad
    out_ref[...] = (normal * gain_row + shift[...].astype(F32)).astype(BF16)
    flush(out_ref)
    sums_ref[...] = stack_rows(column_sum(cot * normal), column_sum(cot), column_sum(grad))


def norm1_back_kernel(up_ref, own, near, normal_ref, scale_ref, gain, sums2, hidden_sums, grad_ref, low_ref, sums_ref):
    up = up_ref[...] + own[...] + near[...].astype(F32)
    normal = normal_ref[...]
    grad = normal_back(up, gain[...].astype(F32), normal, scale_ref[:, 0:1])
    low_ref[...] = grad.astype(BF16)
    flush(low_ref)
    grad_ref[...] = grad
    flush(grad_ref)
    sums_ref[...] = jnp.concatenate(
        [sums2[0:3], column_sum(up * normal), column_sum(up), column_sum(grad), hidden_sums[1:2], hidden_sums[0:1]],
        axis=0,
    )


def mlp_fwd_kernel(n0, n1, wi, wo, rest, bias0, bias1, act0, act1, der0, der1, own, near, wi_far, wo_far, sems):
    wi_far = Gathered(rest, wi_far, sems.at[0], 0)
    wo_far = Gathered(rest, wo_far, sems.at[1], 1)
    width = n0.shape[1]
    chunk = 512
    for b, (bias, act, der) in enumerate(((bias0, act0, der0), (bias1, act1, der1))):
        for c in range(0, act.shape[1], chunk):
            cols = slice(c, c + chunk)
            weight = wi[:, cols] if b == 0 else wi_far[0:width, cols]
            for t, n in enumerate((n0, n1)):
                rows = slice(t * TILE, (t + 1) * TILE)
                u = dot_nn(n[...], weight) + bias[:, cols].astype(F32)
                square = u * u
                th = jnp.tanh(0.7978845608028654 * u * (1.0 + 0.044715 * square))
                half = 0.5 * (1.0 + th)
                act[rows, cols] = (u * half).astype(BF16)
                slope = 0.7978845608028654 * (1.0 + 3.0 * 0.044715 * square)
                der[rows, cols] = (half + 0.5 * u * (1.0 - th * th) * slope).astype(BF16)
        flush(act)
    for c in range(0, width, 256):
        cols = slice(c, c + 256)
        other = wo_far[0:1024, cols]
        near[:, cols] = (dot_nn(act0[TILE:], wo[:, cols]) + dot_nn(act1[TILE:], other)).astype(BF16)
        own[:, cols] = dot_nn(act0[:TILE], wo[:, cols]) + dot_nn(act1[:TILE], other)


def mlp_bwd_kernel(m0, m1, wo, wi, rest, der0, der1, hg0, hg1, own, near, sums_ref, wi_far, wo_far, sems):
    wo_far = Gathered(rest, wo_far, sems.at[1], 1)
    wi_far = Gathered(rest, wi_far, sems.at[0], 0)
    units, width = wo.shape
    chunk = 512
    sums_ref[...] = jnp.zeros_like(sums_ref)
    for b, (der, hg) in enumerate(((der0, hg0), (der1, hg1))):
        for c in range(0, units, chunk):
            cols = slice(c, c + chunk)
            weight = wo[cols, :] if b == 0 else wo_far[cols, 0:width]
            total = 0.0
            for t, m in enumerate((m0, m1)):
                rows = slice(t * TILE, (t + 1) * TILE)
                low = (dot_nt(m[...], weight) * der[rows, cols].astype(F32)).astype(BF16)
                hg[rows, cols] = low
                total = total + column_sum(low.astype(F32))
            sums_ref[b : b + 1, cols] = total
        flush(hg)
    for c in range(0, width, 256):
        cols = slice(c, c + 256)
        other = wi_far[cols, 0:1024]
        near[:, cols] = (dot_nt(hg0[TILE:], wi[cols, :]) + dot_nt(hg1[TILE:], other)).astype(BF16)
        own[:, cols] = dot_nt(hg0[:TILE], wi[cols, :]) + dot_nt(hg1[:TILE], other)
        if c + 256 in (width // 2, width):
            flush(own, (slice(None), slice(c + 256 - width // 2, c + 256)))


def gray(p):
    return p ^ (p >> 1)


def block_index(order, jx, jy):
    bit = {"xa": jx & 1, "xb": jx >> 1, "ya": jy & 1, "yb": jy >> 1}
    index = 0
    for link in order:
        index = index * 2 + bit[link]
    return index


def mlp_grads_kernel(place, n0, n1, hg0, hg1, m0, m1, act0, act1, *rest):
    outs, scratch = rest[:8], rest[8]
    x_here, zh_here, y_here = place[0], place[1], place[2]
    for mat, (lefts, rights) in enumerate((((n0, n1), (hg0, hg1)), ((m0, m1), (act0, act1)))):
        for jx in range(4):
            cols = pl.ds(pl.multiple_of(gray(gray(x_here) ^ jx) * 256, 256), 256)
            for b in range(2):
                slot = b
                scratch[slot] = (
                    dot_tn(lefts[0][:, cols], rights[b][:TILE, :]) + dot_tn(lefts[1][:, cols], rights[b][TILE:, :])
                ).astype(BF16)
                for jy in range(4):
                    y_there = gray(gray(y_here) ^ jy)
                    for a in range(2):
                        off = pl.multiple_of((zh_here ^ a) * 128 + y_there * 32, 32)
                        block = scratch[slot, pl.ds(off, 32), :]
                        for r, order in enumerate(ORDERS):
                            index = block_index(order, jx, jy)
                            out = outs[2 * r + (index >> 3)]
                            out[index & 7, mat, b, a] = block[:, r * 256 : (r + 1) * 256]
        for out in outs:
            flush(out, (slice(None), mat))


def add_step_kernel(*refs):
    count = len(ORDERS)
    keeps, keeps_on, cames, cames_on, stays, goes = (refs[i * count : (i + 1) * count] for i in range(6))
    for keep, came, out in zip((*keeps, *keeps_on), (*cames, *cames_on), (*stays, *goes)):
        out[...] = (keep[...].astype(F32) + came[...].astype(F32)).astype(BF16)


def add_step(keep, came, name, hbm):
    half = keep[0].shape[0] // 2
    rest = keep[0].shape[1:]
    if hbm:
        keep, came = ([pltpu.with_memory_space_constraint(v, pltpu.HBM) for v in values] for values in (keep, came))
    stay = pl.BlockSpec((1, *rest), lambda i: (i, 0, 0, 0, 0, 0))
    go = pl.BlockSpec((1, *rest), lambda i: (i + half, 0, 0, 0, 0, 0))
    return pl.pallas_call(
        add_step_kernel,
        grid=(half,),
        in_specs=[stay] * 4 + [go] * 4 + [stay] * 4 + [go] * 4,
        out_specs=[stay] * 8,
        out_shape=[pltpu.HBM((half, *rest), BF16) if hbm else jax.ShapeDtypeStruct((half, *rest), BF16)] * 8,
        compiler_params=pltpu.CompilerParams(vmem_limit_bytes=12 * MIB),
        cost_estimate=pl.CostEstimate(flops=int(half * 1e9), bytes_accessed=MIB, transcendentals=0),
        name=name,
    )(*keep, *keep, *came, *came)


def add_last_kernel(*refs):
    count = len(ORDERS)
    keeps, cames, ways = refs[:count], refs[count : 2 * count], refs[2 * count :]
    for r, (keep, came) in enumerate(zip(keeps, cames)):
        for b in range(2):
            for a in range(2):
                for mat in range(2):
                    total = keep[0, mat, b, a].astype(F32) + came[0, mat, b, a].astype(F32)
                    out = ways[2 * b + a]
                    out[mat, :, r * 256 : (r + 1) * 256] = total.astype(out.dtype)


def finish_kernel(here, way_zl, way_zz, way_zh, mine, notes, wi_grad, wo_grad, query, key, value, output,
                  query_bias, value_bias, *vectors):
    sums = [here[m] + way_zl[m].astype(F32) + way_zz[m].astype(F32) + way_zh[m].astype(F32) for m in range(2)]
    wi_grad[...] = sums[0]
    wo_grad[...] = jnp.transpose(sums[1])
    total = mine[...].astype(F32) + way_zh[2].astype(F32)
    inner = query.shape[1]
    for i, out in enumerate((query, key, value)):
        out[...] = total[:, i * inner : (i + 1) * inner]
    output[...] = jnp.transpose(total[:, 3 * inner : 4 * inner])
    query_bias[...] = notes[0:1]
    value_bias[...] = notes[1:2]
    for i, out in enumerate(vectors):
        for j in range(4):
            row = 8 + 4 * i + j
            out[:, j * inner : (j + 1) * inner] = notes[row : row + 1]


def add_low(a, b):
    return (a.astype(F32) + b.astype(F32)).astype(BF16)


def per_device(
    tokens,
    segments,
    query_weight,
    query_bias,
    key_weight,
    value_weight,
    value_bias,
    output_weight,
    output_bias,
    first_gain,
    first_shift,
    inner_weight,
    inner_bias,
    outer_weight,
    outer_bias,
    second_gain,
    second_shift,
    cotangent,
):
    x_here, zh_here, y_here = lax.axis_index("x"), lax.axis_index("zh"), lax.axis_index("y")
    zl_here, c_here = lax.axis_index("zl"), lax.axis_index("c")
    width = tokens.shape[2]
    inner = query_weight.shape[1]
    units = inner_weight.shape[1]
    length = 4 * TILE
    row = lambda v: v.reshape(1, -1)

    x0 = tokens[0]
    x2 = send(x0, "zl")
    x1 = send(x0, "c")
    inner_bias_far = send(row(inner_bias), "zl")

    block = (x_here * 4 + y_here) * 64
    piece = jnp.concatenate(
        [lax.dynamic_slice_in_dim(w, block, 64, 0) for w in (inner_weight, outer_weight)], axis=0
    )
    piece = send(after(piece, x1), "zl")


    gathered = lax.all_gather(piece, ("x", "y"), axis=0)
    place = jnp.stack([x_here, zh_here, y_here]).astype(jnp.int32)

    seg = segments[0].reshape(2, 2, TILE)
    seg = jnp.where(zl_here == 1, seg[::-1], seg)
    seg = jnp.where(c_here == 1, seg[:, ::-1], seg).reshape(-1)
    spot = jnp.arange(length, dtype=jnp.int32)
    pos = ((spot // TILE) ^ (zl_here * 2 + c_here)) * TILE + spot % TILE
    allowed = (seg[:, None] == seg[None, :]) & (jnp.abs(pos[:, None] - pos[None, :]) <= WINDOW)
    mask = jnp.where(allowed, 0.0, -1e30).astype(BF16)

    def project(a, b, near_in):
        return local(
            qkv_kernel, [((2 * TILE, inner), BF16)] * 3,
            a, b, query_weight, key_weight, value_weight, row(query_bias), row(value_bias),
            name="qkv", us=2, near_in=near_in, near_out=(0, 1, 2),
        )

    q0, k0, v0 = project(x0, x1, (1,))
    x2 = after(x2, (inner_bias_far, q0))
    x3 = send(x2, "c")
    q1, k1, v1 = project(x2, x3, (0, 1))

    def attend(q, first):
        return local(
            functools.partial(attn_fwd_kernel, first),
            [((2 * TILE, inner), BF16), ((8, 2 * TILE), F32), ((TILE, width), BF16), ((TILE, width), BF16)],
            q, k0, k1, v0, v1, mask, output_weight,
            name="attn_fwd", us=5, near_in=(0, 1, 2, 3, 4, 5), near_out=(2, 3),
        )

    ctx1, lse1, term2, term3 = attend(q1, 2 * TILE)
    from_far = send(add_low(term2, send(term3, "c")), "zl")
    ctx0, lse0, term0, term1 = attend(after(q0, term2), 0)
    from_near = send(term1, "c")

    normal1, scale1, n0 = local(
        norm1_kernel,
        [((TILE, width), F32), ((TILE, 128), F32), ((TILE, width), BF16)],
        x0, term0, from_near, from_far, row(output_bias), row(first_gain), row(first_shift),
        name="norm1", us=1.5, near_in=(1, 2, 3), near_out=(2,),
    )
    n1 = send(n0, "c")
    far_weights = [pltpu.VMEM((16, 64, units), BF16)] * 2 + [pltpu.SemaphoreType.DMA((2,))]
    act0, act1, der0, der1, mlp_own, mlp_near = local(
        mlp_fwd_kernel,
        [((2 * TILE, units), BF16)] * 4 + [((TILE, width), F32), ((TILE, width), BF16)],
        n0, n1, inner_weight, outer_weight, gathered, row(inner_bias), inner_bias_far,
        name="mlp_fwd", us=8.5, limit=24, near_in=(0, 1), near_out=(2, 3, 4, 5),
        raw=(4,), scratch=far_weights,
    )
    layer_out, second_grad, m0, sums2 = local(
        norm2_kernel,
        [((TILE, width), BF16), ((TILE, width), F32), ((TILE, width), BF16), ((8, width), F32)],
        normal1, mlp_own, send(mlp_near, "c"), row(first_gain), row(first_shift), row(outer_bias),
        row(second_gain), row(second_shift), cotangent[0],
        name="norm2", us=2, near_in=(1, 2), near_out=(1, 2),
    )
    m1 = send(m0, "c")
    hg0, hg1, back_own, back_near, hidden_sums = local(
        mlp_bwd_kernel,
        [((2 * TILE, units), BF16)] * 2 + [((TILE, width), F32), ((TILE, width), BF16), ((8, units), F32)],
        m0, m1, outer_weight, inner_weight, gathered, der0, der1,
        name="mlp_bwd", us=6, limit=24, near_in=(0, 1, 2, 5, 6), near_out=(3,),
        raw=(4,), scratch=far_weights,
    )
    first_grad, u0, sums = local(
        norm1_back_kernel,
        [((TILE, width), F32), ((TILE, width), BF16), ((8, width), F32)],
        second_grad, back_own, send(back_near, "c"), normal1, scale1, row(first_gain), sums2, hidden_sums,
        name="norm1_back", us=2, near_in=(0, 2),
    )
    u2 = send(u0, "zl")
    u1 = send(u0, "c")

    parts = local(
        mlp_grads_kernel,
        [((8, 2, 2, 2, 32, 256), BF16)] * 8,
        after(place, u0), n0, n1, hg0, hg1, m0, m1, act0, act1,
        name="mlp_grads", us=8.5, limit=20, scalars=1, scratch=[pltpu.VMEM((2, 256, units), BF16)],
    )
    keep, out = parts[0::2], parts[1::2]
    came = [send(v, order[0]) for v, order in zip(out, ORDERS)]

    total = sums[:6] + send(sums[:6], "c")
    far = send(jnp.concatenate([total, sums[6:7]], axis=0), "zl")
    total = jnp.concatenate([total + far[:6], sums[7:8] + far[6:7]], axis=0)

    u2 = after(u2, (parts[0], total))
    u3 = send(u2, "c")
    attn_grads, tok_own, tok_near, tok_far, bias_sums = local(
        attn_bwd_kernel,
        [
            ((width, 4 * inner), BF16),
            ((TILE, width), F32),
            ((2 * TILE, width), BF16),
            ((TILE, width), BF16),
            ((8, inner), F32),
        ],
        u0, u1, output_weight, q0, k0, k1, v0, v1, mask, lse0, lse1, q1, u2, u3,
        x0, x1, x2, x3, ctx0, ctx1, query_weight, key_weight, value_weight,
        name="attn_bwd", us=23, limit=32, near_in=(0, 1, 12, 13),
        scratch=[pltpu.VMEM((length, inner), BF16)] * 3 + [pltpu.VMEM((length, inner), F32)] * 2,
    )
    attn_grads = lax.psum_scatter(after(attn_grads, came), "y", scatter_dimension=0, tiled=True)

    came[0] = after(came[0], tok_own)
    for step in range(1, 4):
        if step == 2:
            notes = after(notes, came[0])
            for link in ("xa", "xb"):
                notes = notes + send(notes, link)
            came[0] = after(came[0], (tok_far, notes))
        if step == 3:
            notes = notes + send(notes, "ya")
            came[0] = after(came[0], notes)
        both = add_step(keep, came, f"add{step}", True)
        keep, out = both[:4], both[4:]
        came = [send(v, order[step]) for v, order in zip(out, ORDERS)]
        if step == 1:
            tok_near = send(after(tok_near, keep[0]), "c")
            tok_far = send(add_low(tok_far, tok_near[TILE:]), "zl")
            notes = jnp.concatenate(
                [after(bias_sums, keep[0]), total.reshape(7 * width // inner, inner)], axis=0
            )
        if step == 2:
            attn_grads = lax.psum_scatter(after(attn_grads, keep[0]), "x", scatter_dimension=0, tiled=True)
    notes = notes + send(notes, "yb")
    tokens_grad = first_grad + tok_own + tok_near[:TILE].astype(F32) + tok_far.astype(F32)
    came[0] = after(came[0], (notes, tokens_grad))
    ways = local(
        add_last_kernel,
        [((2, 32, units), F32)] + [((2, 32, units), BF16)] * 3,
        *keep, *came, name="add4", us=1, near_out=range(4),
    )
    mine = lax.dynamic_slice_in_dim(attn_grads, zh_here * 32, 32, 0)
    theirs = lax.dynamic_slice_in_dim(attn_grads, (1 - zh_here) * 32, 32, 0)
    notes = notes + send(after(notes, ways[0]), "zh")
    finished = local(
        finish_kernel,
        [((32, units), F32), ((units, 32), F32)]
        + [((32, inner), F32)] * 3
        + [((inner, 32), F32)]
        + [((1, inner), F32)] * 2
        + [((1, width), F32)] * 7,
        ways[0],
        send(ways[2], "zl"),
        send(ways[3], "zz"),
        send(jnp.concatenate([ways[1], theirs[None]], axis=0), "zh"),
        mine,
        notes,
        name="finish", us=2, near_in=range(6), near_out=range(15),
    )
    wi_grad, wo_grad, *finished = finished
    vectors = [v.reshape(-1) for v in finished[4:]]
    return (
        layer_out[None],
        tokens_grad[None],
        finished[0],
        vectors[0],
        finished[1],
        finished[2],
        vectors[1],
        finished[3],
        vectors[7],
        vectors[5],
        vectors[6],
        wi_grad,
        vectors[8],
        wo_grad,
        vectors[4],
        vectors[2],
        vectors[3],
    )


def solution(mesh):
    fine = Mesh(mesh.devices.reshape(4, 2, 4, 2, 2), AXES)
    shard = ("zl", "c")
    placed = (
        P(REPLICA, shard, None),
        P(REPLICA, None),
        P(None, shard),
        P(shard),
        P(None, shard),
        P(None, shard),
        P(shard),
        P(shard, None),
        P(),
        P(),
        P(),
        P(None, shard),
        P(shard),
        P(shard, None),
        P(),
        P(),
        P(),
        P(REPLICA, shard, None),
    )
    return jax.shard_map(
        per_device,
        mesh=fine,
        in_specs=placed,
        out_specs=(
            P(REPLICA, shard, None),
            P(REPLICA, shard, None),
            P(REPLICA, shard),
            P(shard),
            P(REPLICA, shard),
            P(REPLICA, shard),
            P(shard),
            P(shard, REPLICA),
            P(),
            P(),
            P(),
            P(REPLICA, shard),
            P(shard),
            P(shard, REPLICA),
            P(),
            P(),
            P(),
        ),
        check_vma=False,
    )
```

```python
import functools

import jax
import jax.numpy as jnp
from jax import lax
from jax.experimental import pallas as pl
from jax.experimental.pallas import tpu as pltpu
from jax.sharding import Mesh, PartitionSpec as P

HEAD_DIM = 64
WINDOW = 512
TILE = 256
AXES = ("x", "zh", "y", "zl", "c")
REPLICA = ("x", "zh", "y")
F32 = jnp.float32
BF16 = jnp.bfloat16
MIB = 1 << 20


def flat_index(x, zh, y, zl, c):
    return (((x * 2 + zh) * 4 + y) * 2 + zl) * 2 + c


def permutation(move):
    return [
        (flat_index(x, zh, y, zl, c), flat_index(*move(x, zh, y, zl, c)))
        for x in range(4)
        for zh in range(2)
        for y in range(4)
        for zl in range(2)
        for c in range(2)
    ]


LINKS = {
    "xa": permutation(lambda x, zh, y, zl, c: (x ^ 1, zh, y, zl, c)),
    "xb": permutation(lambda x, zh, y, zl, c: (3 - x, zh, y, zl, c)),
    "ya": permutation(lambda x, zh, y, zl, c: (x, zh, y ^ 1, zl, c)),
    "yb": permutation(lambda x, zh, y, zl, c: (x, zh, 3 - y, zl, c)),
    "zl": permutation(lambda x, zh, y, zl, c: (x, zh, y, zl ^ 1, c)),
    "zz": permutation(lambda x, zh, y, zl, c: (x, zh ^ 1, y, zl ^ 1, c)),
    "zh": permutation(lambda x, zh, y, zl, c: (x, zh ^ 1, y, zl, c)),
    "c": permutation(lambda x, zh, y, zl, c: (x, zh, y, zl, c ^ 1)),
}
ORDERS = (
    ("xa", "xb", "ya", "yb"),
    ("xb", "ya", "yb", "xa"),
    ("ya", "yb", "xa", "xb"),
    ("yb", "xa", "xb", "ya"),
)


def send(value, link):
    return lax.ppermute(value, AXES, LINKS[link])


def dot_nn(a, b):
    return lax.dot_general(a, b, (((1,), (0,)), ((), ())), preferred_element_type=F32)


def dot_nt(a, b):
    return lax.dot_general(a, b, (((1,), (1,)), ((), ())), preferred_element_type=F32)


def dot_tn(a, b):
    return lax.dot_general(a, b, (((0,), (0,)), ((), ())), preferred_element_type=F32)


class Held:
    def __init__(self, source, buffer, sem):
        self.copy = pltpu.make_async_copy(source, buffer, sem)
        self.copy.start()
        self.buffer = buffer
        self.shape = buffer.shape
        self.here = False

    def __getitem__(self, index):
        if not self.here:
            self.copy.wait()
            self.here = True
        return self.buffer[index]


class Gathered:
    def __init__(self, source, buffer, sem, half):
        self.buffer, self.here = buffer, False
        self.copy = pltpu.make_async_copy(source.at[:, pl.ds(64 * half, 64)], buffer, sem)
        self.copy.start()

    def __getitem__(self, index):
        if not self.here:
            self.copy.wait()
            self.here = True
        rows, cols = index
        start, stop = rows.start or 0, rows.stop or 1024
        block = self.buffer[start // 64 : stop // 64, :, cols]
        return block.reshape(stop - start, block.shape[-1])


class Kept:
    def __init__(self, target, buffer, sems):
        self.target, self.buffer, self.sems = target, buffer, sems
        self.shape, self.dtype = buffer.shape, buffer.dtype
        self.copies = []

    def __getitem__(self, index):
        return self.buffer[index]

    def __setitem__(self, index, value):
        self.buffer[index] = value

    def flush(self, index=None):
        source, target = self.buffer, self.target
        if index is not None:
            source, target = source.at[index], target.at[index]
        copy = pltpu.make_async_copy(source, target, self.sems.at[len(self.copies)])
        copy.start()
        self.copies.append(copy)


def flush(ref, index=None):
    if isinstance(ref, Kept):
        ref.flush(index)


def local(kernel, outs, *operands, name, us, scratch=(), limit=16, scalars=0, near_in=(), near_out=(), raw=()):
    small = 1 << 17

    def near(shape, dtype):
        size = jnp.dtype(dtype).itemsize
        for n in shape:
            size *= n
        return size <= small

    ins = [(v.shape, v.dtype) for v in operands]
    in_near = [i in near_in or near(*v) for i, v in enumerate(ins)]
    out_near = [i in near_out or near(*v) for i, v in enumerate(outs)]
    in_bufs = [pltpu.VMEM(*v) for i, v in enumerate(ins) if i >= scalars and not in_near[i] and i not in raw]
    out_bufs = [pltpu.VMEM(*v) for i, v in enumerate(outs) if not out_near[i]]
    user = len(scratch)

    def body(*refs):
        in_refs, refs = refs[: len(ins)], refs[len(ins) :]
        out_refs, refs = refs[: len(outs)], refs[len(outs) :]
        own, refs = refs[:user], list(refs[user:])
        in_sem, out_sem = refs[-2:]
        buffers = iter(refs[:-2])
        wrapped, kept = [], []
        for i, ref in enumerate(in_refs):
            if i < scalars or in_near[i] or i in raw:
                wrapped.append(ref)
            else:
                wrapped.append(Held(ref, next(buffers), in_sem.at[i]))
        for i, ref in enumerate(out_refs):
            if not out_near[i]:
                ref = Kept(ref, next(buffers), out_sem.at[i])
                kept.append(ref)
            wrapped.append(ref)
        kernel(*wrapped, *own)
        for ref in wrapped:
            if isinstance(ref, Held) and not ref.here:
                ref.copy.wait()
        for ref in kept:
            if not ref.copies:
                ref.flush()
        for ref in kept:
            for copy in ref.copies:
                copy.wait()

    vmem = pl.BlockSpec(memory_space=pltpu.VMEM)
    hbm = pl.BlockSpec(memory_space=pltpu.HBM)
    smem = pl.BlockSpec(memory_space=pltpu.SMEM)
    return pl.pallas_call(
        body,
        in_specs=[smem if i < scalars else vmem if in_near[i] else hbm for i in range(len(ins))],
        out_specs=[vmem if v else hbm for v in out_near],
        out_shape=[jax.ShapeDtypeStruct(*o) if v else pltpu.HBM(*o) for o, v in zip(outs, out_near)],
        scratch_shapes=[
            *scratch,
            *in_bufs,
            *out_bufs,
            pltpu.SemaphoreType.DMA((len(ins),)),
            pltpu.SemaphoreType.DMA((len(outs), 2)),
        ],
        compiler_params=pltpu.CompilerParams(vmem_limit_bytes=limit * MIB),
        cost_estimate=pl.CostEstimate(flops=int(us * 1e9), bytes_accessed=MIB, transcendentals=0),
        name=name,
    )(
        *(
            v if i < scalars or in_near[i] else pltpu.with_memory_space_constraint(v, pltpu.HBM)
            for i, v in enumerate(operands)
        )
    )


def after(value, *others):
    return lax.optimization_barrier((value, others))[0]


def head_lanes(shape, head):
    lane = lax.broadcasted_iota(jnp.int32, shape, len(shape) - 1)
    return (lane >> 6) == head


def qkv_kernel(x0, x1, wq, wk, wv, bq, bv, q_ref, k_ref, v_ref):
    for t, x in enumerate((x0, x1)):
        rows = slice(t * TILE, (t + 1) * TILE)
        q_ref[rows, :] = (dot_nn(x[...], wq[...]) + bq[...].astype(F32)).astype(BF16)
        k_ref[rows, :] = dot_nn(x[...], wk[...]).astype(BF16)
        v_ref[rows, :] = (dot_nn(x[...], wv[...]) + bv[...].astype(F32)).astype(BF16)


def attn_fwd_kernel(first, q_ref, k0, k1, v0, v1, mask, wo, ctx_ref, lse_ref, term0, term1):
    rows = q_ref.shape[0]
    half = k0.shape[0]
    q = q_ref[...] * jnp.asarray(HEAD_DIM ** -0.5, BF16)
    mask0 = mask[first : first + rows, :half].astype(F32)
    mask1 = mask[first : first + rows, half:].astype(F32)
    ctx = jnp.zeros(q.shape, F32)
    lse = jnp.zeros((rows, 128), F32)
    lane = lax.broadcasted_iota(jnp.int32, lse.shape, 1)
    for h in range(q.shape[1] // HEAD_DIM):
        mine = head_lanes(q.shape, h)
        qh = jnp.where(mine, q, jnp.zeros_like(q))
        s0 = dot_nt(qh, k0[...]) + mask0
        s1 = dot_nt(qh, k1[...]) + mask1
        top = jnp.max(jnp.maximum(s0, s1), axis=-1, keepdims=True)
        p0 = jnp.exp(s0 - top)
        p1 = jnp.exp(s1 - top)
        total = jnp.sum(p0 + p1, axis=-1, keepdims=True)
        part = (dot_nn(p0.astype(BF16), v0[...]) + dot_nn(p1.astype(BF16), v1[...])) * (1.0 / total)
        ctx = jnp.where(mine, part, ctx)
        lse = jnp.where(lane == h, top + jnp.log(total), lse)
    ctx_ref[...] = ctx.astype(BF16)
    flush(ctx_ref)
    lse_ref[...] = jnp.transpose(lse)[:8]
    term1[...] = dot_nn(ctx_ref[TILE:, :], wo[...]).astype(BF16)
    term0[...] = dot_nn(ctx_ref[:TILE, :], wo[...]).astype(BF16)


def attn_bwd_kernel(up0, up1, wo, q0, k0, k1, v0, v1, mask, lse0, lse1, q1, up2, up3,
                    x0, x1, x2, x3, ctx0, ctx1, wq, wk, wv,
                    grads, tok_own, tok_near, tok_far, sums_ref, dq_ref, dk_ref, dv_ref, dk, dv):
    xs = (x0, x1, x2, x3)
    half = k0.shape[0]
    scale = HEAD_DIM ** -0.5
    keys, values = (k0, k1), (v0, v1)
    for t, (q_ref, lse, ups) in enumerate(((q0, lse0, (up0, up1)), (q1, lse1, (up2, up3)))):
        q = q_ref[...] * jnp.asarray(scale, BF16)
        up = jnp.concatenate([ups[0][...], ups[1][...]], axis=0)
        grad = dot_nt(up, wo[...]).astype(BF16)
        dq = jnp.zeros(q.shape, F32)
        for h in range(q.shape[1] // HEAD_DIM):
            mine = head_lanes(q.shape, h)
            qh = jnp.where(mine, q, jnp.zeros_like(q))
            gh = jnp.where(mine, grad, jnp.zeros_like(grad))
            probs, prob_grads, row = [], [], 0.0
            for j in range(2):
                bias = mask[j * half : (j + 1) * half, t * half : (t + 1) * half].astype(F32)
                p = jnp.exp(dot_nt(keys[j][...], qh) + bias - lse[h : h + 1, :])
                dp = dot_nt(values[j][...], gh)
                row = row + jnp.sum(p * dp, axis=0, keepdims=True)
                probs.append(p)
                prob_grads.append(dp)
            part = 0.0
            for j in range(2):
                rows = slice(j * half, (j + 1) * half)
                value_part = dot_nn(probs[j].astype(BF16), gh)
                ds = (probs[j] * (prob_grads[j] - row)).astype(BF16)
                key_part = dot_nn(ds, qh)
                if t == 0 and h == 0:
                    dv[rows, :] = value_part
                    dk[rows, :] = key_part
                else:
                    dv[rows, :] += value_part
                    dk[rows, :] += key_part
                part = part + dot_tn(ds, keys[j][...])
            dq = jnp.where(mine, part, dq)
        dq_ref[t * half : (t + 1) * half, :] = (dq * scale).astype(BF16)
    dk_ref[...] = dk[...].astype(BF16)
    dv_ref[...] = dv[...].astype(BF16)
    inner = dq_ref.shape[1]
    rows = [slice(j * TILE, (j + 1) * TILE) for j in range(4)]
    bias_rows = []

    def place(total, i):
        low = total.astype(BF16)
        for x in range(4):
            for zh in range(2):
                for y in range(4):
                    source, target = (x * 8 + zh * 4 + y) * 32, (y * 8 + x * 2 + zh) * 32
                    grads[target : target + 32, i * inner : (i + 1) * inner] = low[source : source + 32]

    for i, grad in enumerate((dq_ref, dk_ref, dv_ref)):
        total = dot_tn(xs[0][...], grad[rows[0], :])
        for j in range(1, 4):
            total = total + dot_tn(xs[j][...], grad[rows[j], :])
        place(total, i)
        if i != 1:
            bias_rows.append(column_sum(grad[...].astype(F32)))
    total = 0.0
    for j, up in enumerate((up0, up1, up2, up3)):
        total = total + dot_tn(up[...], (ctx0, ctx1)[j // 2][rows[j % 2], :])
    place(total, 3)
    flush(grads)
    sums_ref[...] = stack_rows(*bias_rows)
    for j in (3, 1, 2, 0):
        total = dot_nt(dq_ref[rows[j], :], wq[...]) + dot_nt(dk_ref[rows[j], :], wk[...]) + dot_nt(dv_ref[rows[j], :], wv[...])
        if j == 0:
            tok_own[...] = total
        elif j == 2:
            tok_far[...] = total.astype(BF16)
            flush(tok_far)
        else:
            tok_near[(j // 2) * TILE : (j // 2 + 1) * TILE, :] = total.astype(BF16)
            if j == 1:
                flush(tok_near)


def normal_of(rows):
    center = jnp.mean(rows, axis=-1, keepdims=True)
    centred = rows - center
    scale = lax.rsqrt(jnp.mean(centred * centred, axis=-1, keepdims=True) + 1e-06)
    return centred * scale, scale


def normal_back(up, gain, normal, scale):
    scaled = up * gain
    mean_up = jnp.mean(scaled, axis=-1, keepdims=True)
    mean_un = jnp.mean(scaled * normal, axis=-1, keepdims=True)
    return scale * (scaled - mean_up - normal * mean_un)


def stack_rows(*rows):
    width = rows[0].shape[1]
    return jnp.concatenate([*rows, jnp.zeros((8 - len(rows), width), F32)], axis=0)


def column_sum(rows):
    return jnp.sum(rows, axis=0, keepdims=True)


def norm1_kernel(x, own, near, far, bias, gain, shift, normal_ref, scale_ref, low_ref):
    rows = x[...].astype(F32) + bias[...].astype(F32)
    rows = rows + own[...].astype(F32) + near[...].astype(F32) + far[...].astype(F32)
    normal, scale = normal_of(rows)
    normal_ref[...] = normal
    flush(normal_ref)
    scale_ref[...] = jnp.broadcast_to(scale, scale_ref.shape)
    low_ref[...] = (normal * gain[...].astype(F32) + shift[...].astype(F32)).astype(BF16)


def norm2_kernel(normal1, own, near, gain1, shift1, bias, gain, shift, cot_ref, out_ref, grad_ref, low_ref, sums_ref):
    rows = normal1[...] * gain1[...].astype(F32) + shift1[...].astype(F32) + bias[...].astype(F32)
    rows = rows + own[...] + near[...].astype(F32)
    normal, scale = normal_of(rows)
    gain_row = gain[...].astype(F32)
    cot = cot_ref[...].astype(F32)
    grad = normal_back(cot, gain_row, normal, scale)
    low_ref[...] = grad.astype(BF16)
    grad_ref[...] = grad
    out_ref[...] = (normal * gain_row + shift[...].astype(F32)).astype(BF16)
    flush(out_ref)
    sums_ref[...] = stack_rows(column_sum(cot * normal), column_sum(cot), column_sum(grad))


def norm1_back_kernel(up_ref, own, near, normal_ref, scale_ref, gain, sums2, hidden_sums, grad_ref, low_ref, sums_ref):
    up = up_ref[...] + own[...] + near[...].astype(F32)
    normal = normal_ref[...]
    grad = normal_back(up, gain[...].astype(F32), normal, scale_ref[:, 0:1])
    low_ref[...] = grad.astype(BF16)
    flush(low_ref)
    grad_ref[...] = grad
    flush(grad_ref)
    sums_ref[...] = jnp.concatenate(
        [sums2[0:3], column_sum(up * normal), column_sum(up), column_sum(grad), hidden_sums[1:2], hidden_sums[0:1]],
        axis=0,
    )


def mlp_fwd_kernel(n0, n1, wi, wo, rest, bias0, bias1, act0, act1, der0, der1, own, near, wi_far, wo_far, sems):
    wi_far = Gathered(rest, wi_far, sems.at[0], 0)
    wo_far = Gathered(rest, wo_far, sems.at[1], 1)
    width = n0.shape[1]
    chunk = 512
    for b, (bias, act, der) in enumerate(((bias0, act0, der0), (bias1, act1, der1))):
        for c in range(0, act.shape[1], chunk):
            cols = slice(c, c + chunk)
            weight = wi[:, cols] if b == 0 else wi_far[0:width, cols]
            for t, n in enumerate((n0, n1)):
                rows = slice(t * TILE, (t + 1) * TILE)
                u = dot_nn(n[...], weight) + bias[:, cols].astype(F32)
                square = u * u
                th = jnp.tanh(0.7978845608028654 * u * (1.0 + 0.044715 * square))
                half = 0.5 * (1.0 + th)
                act[rows, cols] = (u * half).astype(BF16)
                slope = 0.7978845608028654 * (1.0 + 3.0 * 0.044715 * square)
                der[rows, cols] = (half + 0.5 * u * (1.0 - th * th) * slope).astype(BF16)
        flush(act)
    for c in range(0, width, 256):
        cols = slice(c, c + 256)
        other = wo_far[0:1024, cols]
        near[:, cols] = (dot_nn(act0[TILE:], wo[:, cols]) + dot_nn(act1[TILE:], other)).astype(BF16)
        own[:, cols] = dot_nn(act0[:TILE], wo[:, cols]) + dot_nn(act1[:TILE], other)


def mlp_bwd_kernel(m0, m1, wo, wi, rest, der0, der1, hg0, hg1, own, near, sums_ref, wi_far, wo_far, sems):
    wo_far = Gathered(rest, wo_far, sems.at[1], 1)
    wi_far = Gathered(rest, wi_far, sems.at[0], 0)
    units, width = wo.shape
    chunk = 512
    sums_ref[...] = jnp.zeros_like(sums_ref)
    for b, (der, hg) in enumerate(((der0, hg0), (der1, hg1))):
        for c in range(0, units, chunk):
            cols = slice(c, c + chunk)
            weight = wo[cols, :] if b == 0 else wo_far[cols, 0:width]
            total = 0.0
            for t, m in enumerate((m0, m1)):
                rows = slice(t * TILE, (t + 1) * TILE)
                low = (dot_nt(m[...], weight) * der[rows, cols].astype(F32)).astype(BF16)
                hg[rows, cols] = low
                total = total + column_sum(low.astype(F32))
            sums_ref[b : b + 1, cols] = total
        flush(hg)
    for c in range(0, width, 256):
        cols = slice(c, c + 256)
        other = wi_far[cols, 0:1024]
        near[:, cols] = (dot_nt(hg0[TILE:], wi[cols, :]) + dot_nt(hg1[TILE:], other)).astype(BF16)
        own[:, cols] = dot_nt(hg0[:TILE], wi[cols, :]) + dot_nt(hg1[:TILE], other)
        if c + 256 in (width // 2, width):
            flush(own, (slice(None), slice(c + 256 - width // 2, c + 256)))


def gray(p):
    return p ^ (p >> 1)


def block_index(order, jx, jy):
    bit = {"xa": jx & 1, "xb": jx >> 1, "ya": jy & 1, "yb": jy >> 1}
    index = 0
    for link in order:
        index = index * 2 + bit[link]
    return index


def mlp_grads_kernel(place, n0, n1, hg0, hg1, m0, m1, act0, act1, *rest):
    outs, scratch = rest[:8], rest[8]
    x_here, zh_here, y_here = place[0], place[1], place[2]
    for mat, (lefts, rights) in enumerate((((n0, n1), (hg0, hg1)), ((m0, m1), (act0, act1)))):
        for jx in range(4):
            cols = pl.ds(pl.multiple_of(gray(gray(x_here) ^ jx) * 256, 256), 256)
            for b in range(2):
                slot = b
                scratch[slot] = (
                    dot_tn(lefts[0][:, cols], rights[b][:TILE, :]) + dot_tn(lefts[1][:, cols], rights[b][TILE:, :])
                ).astype(BF16)
                for jy in range(4):
                    y_there = gray(gray(y_here) ^ jy)
                    for a in range(2):
                        off = pl.multiple_of((zh_here ^ a) * 128 + y_there * 32, 32)
                        block = scratch[slot, pl.ds(off, 32), :]
                        for r, order in enumerate(ORDERS):
                            index = block_index(order, jx, jy)
                            out = outs[2 * r + (index >> 3)]
                            out[index & 7, mat, b, a] = block[:, r * 256 : (r + 1) * 256]
        for out in outs:
            flush(out, (slice(None), mat))


def add_step_kernel(*refs):
    count = len(ORDERS)
    for r in range(count):
        keep, came = refs[2 * r : 2 * r + 2]
        stay, go = refs[2 * count + r], refs[3 * count + r]
        half = stay.shape[0]
        for out, first in ((go, half), (stay, 0)):
            for i in range(half):
                for a in range(2):
                    out[i, a] = (keep[first + i, a].astype(F32) + came[first + i, a].astype(F32)).astype(BF16)
            flush(out)


def add_step(keep, came, name):
    half = (keep[0].shape[0] // 2, *keep[0].shape[1:])
    pairs = [v for pair in zip(keep, came) for v in pair]
    return local(add_step_kernel, [(half, BF16)] * 8, *pairs, name=name, us=half[0], limit=24)


def add_last_kernel(*refs):
    count = len(ORDERS)
    keeps, cames, ways = refs[:count], refs[count : 2 * count], refs[2 * count :]
    for r, (keep, came) in enumerate(zip(keeps, cames)):
        for b in range(2):
            for a in range(2):
                for mat in range(2):
                    total = keep[0, mat, b, a].astype(F32) + came[0, mat, b, a].astype(F32)
                    out = ways[2 * b + a]
                    out[mat, :, r * 256 : (r + 1) * 256] = total.astype(out.dtype)


def finish_kernel(here, way_zl, way_zz, way_zh, mine, notes, wi_grad, wo_grad, query, key, value, output,
                  query_bias, value_bias, *vectors):
    sums = [here[m] + way_zl[m].astype(F32) + way_zz[m].astype(F32) + way_zh[m].astype(F32) for m in range(2)]
    wi_grad[...] = sums[0]
    wo_grad[...] = sums[1]
    total = mine[...].astype(F32) + way_zh[2].astype(F32)
    inner = query.shape[1]
    for i, out in enumerate((query, key, value)):
        out[...] = total[:, i * inner : (i + 1) * inner]
    output[...] = total[:, 3 * inner : 4 * inner]
    query_bias[...] = notes[0:1]
    value_bias[...] = notes[1:2]
    for i, out in enumerate(vectors):
        for j in range(4):
            row = 8 + 4 * i + j
            out[:, j * inner : (j + 1) * inner] = notes[row : row + 1]


def add_low(a, b):
    return (a.astype(F32) + b.astype(F32)).astype(BF16)


def per_device(
    tokens,
    segments,
    query_weight,
    query_bias,
    key_weight,
    value_weight,
    value_bias,
    output_weight,
    output_bias,
    first_gain,
    first_shift,
    inner_weight,
    inner_bias,
    outer_weight,
    outer_bias,
    second_gain,
    second_shift,
    cotangent,
):
    x_here, zh_here, y_here = lax.axis_index("x"), lax.axis_index("zh"), lax.axis_index("y")
    zl_here, c_here = lax.axis_index("zl"), lax.axis_index("c")
    width = tokens.shape[2]
    inner = query_weight.shape[1]
    units = inner_weight.shape[1]
    length = 4 * TILE
    row = lambda v: v.reshape(1, -1)

    x0 = tokens[0]
    x2 = send(x0, "zl")
    x1 = send(x0, "c")
    inner_bias_far = send(row(inner_bias), "zl")

    block = (x_here * 4 + y_here) * 64
    piece = jnp.concatenate(
        [lax.dynamic_slice_in_dim(w, block, 64, 0) for w in (inner_weight, outer_weight)], axis=0
    )
    piece = send(piece, "zl")


    gathered = lax.all_gather(piece, ("x", "y"), axis=0)
    place = jnp.stack([x_here, zh_here, y_here]).astype(jnp.int32)

    seg = segments[0].reshape(2, 2, TILE)
    seg = jnp.where(zl_here == 1, seg[::-1], seg)
    seg = jnp.where(c_here == 1, seg[:, ::-1], seg).reshape(-1)
    spot = jnp.arange(length, dtype=jnp.int32)
    pos = ((spot // TILE) ^ (zl_here * 2 + c_here)) * TILE + spot % TILE
    allowed = (seg[:, None] == seg[None, :]) & (jnp.abs(pos[:, None] - pos[None, :]) <= WINDOW)
    mask = jnp.where(allowed, 0.0, -1e30).astype(BF16)

    def project(a, b, near_in):
        return local(
            qkv_kernel, [((2 * TILE, inner), BF16)] * 3,
            a, b, query_weight, key_weight, value_weight, row(query_bias), row(value_bias),
            name="qkv", us=2, near_in=near_in, near_out=(0, 1, 2),
        )

    q0, k0, v0 = project(x0, x1, (1,))
    x2 = after(x2, (inner_bias_far, q0))
    x3 = send(x2, "c")
    q1, k1, v1 = project(x2, x3, (0, 1))

    def attend(q, first):
        return local(
            functools.partial(attn_fwd_kernel, first),
            [((2 * TILE, inner), BF16), ((8, 2 * TILE), F32), ((TILE, width), BF16), ((TILE, width), BF16)],
            q, k0, k1, v0, v1, mask, output_weight,
            name="attn_fwd", us=5, near_in=(0, 1, 2, 3, 4, 5), near_out=(2, 3),
        )

    ctx1, lse1, term2, term3 = attend(q1, 2 * TILE)
    from_far = send(add_low(term2, send(term3, "c")), "zl")
    ctx0, lse0, term0, term1 = attend(after(q0, term2), 0)
    from_near = send(term1, "c")

    normal1, scale1, n0 = local(
        norm1_kernel,
        [((TILE, width), F32), ((TILE, 128), F32), ((TILE, width), BF16)],
        x0, term0, from_near, from_far, row(output_bias), row(first_gain), row(first_shift),
        name="norm1", us=1.5, near_in=(1, 2, 3), near_out=(2,),
    )
    n1 = send(n0, "c")
    far_weights = [pltpu.VMEM((16, 64, units), BF16)] * 2 + [pltpu.SemaphoreType.DMA((2,))]
    act0, act1, der0, der1, mlp_own, mlp_near = local(
        mlp_fwd_kernel,
        [((2 * TILE, units), BF16)] * 4 + [((TILE, width), F32), ((TILE, width), BF16)],
        n0, n1, inner_weight, outer_weight, gathered, row(inner_bias), inner_bias_far,
        name="mlp_fwd", us=8.5, limit=24, near_in=(0, 1), near_out=(2, 3, 4, 5),
        raw=(4,), scratch=far_weights,
    )
    layer_out, second_grad, m0, sums2 = local(
        norm2_kernel,
        [((TILE, width), BF16), ((TILE, width), F32), ((TILE, width), BF16), ((8, width), F32)],
        normal1, mlp_own, send(mlp_near, "c"), row(first_gain), row(first_shift), row(outer_bias),
        row(second_gain), row(second_shift), cotangent[0],
        name="norm2", us=2, near_in=(0, 1, 2, 8), near_out=(1, 2),
    )
    m1 = send(m0, "c")
    hg0, hg1, back_own, back_near, hidden_sums = local(
        mlp_bwd_kernel,
        [((2 * TILE, units), BF16)] * 2 + [((TILE, width), F32), ((TILE, width), BF16), ((8, units), F32)],
        m0, m1, outer_weight, inner_weight, gathered, der0, der1,
        name="mlp_bwd", us=6, limit=24, near_in=(0, 1, 2, 5, 6), near_out=(3,),
        raw=(4,), scratch=far_weights,
    )
    first_grad, u0, sums = local(
        norm1_back_kernel,
        [((TILE, width), F32), ((TILE, width), BF16), ((8, width), F32)],
        second_grad, back_own, send(back_near, "c"), normal1, scale1, row(first_gain), sums2, hidden_sums,
        name="norm1_back", us=2, near_in=(0, 2, 3),
    )
    u2 = send(u0, "zl")
    u1 = send(u0, "c")

    parts = local(
        mlp_grads_kernel,
        [((8, 2, 2, 2, 32, 256), BF16)] * 8,
        after(place, u0), n0, n1, hg0, hg1, m0, m1, act0, act1,
        name="mlp_grads", us=8.5, limit=20, scalars=1, scratch=[pltpu.VMEM((2, 256, units), BF16)],
    )
    keep, out = parts[0::2], parts[1::2]
    came = [send(v, order[0]) for v, order in zip(out, ORDERS)]

    total = sums[:6] + send(sums[:6], "c")
    chip_total = jnp.concatenate([total, sums[6:7]], axis=0)
    far = send(chip_total, "zl")
    total = jnp.concatenate([total + far[:6], sums[7:8] + far[6:7]], axis=0)

    u2 = after(u2, (parts[0], chip_total))
    u3 = send(u2, "c")
    attn_grads, tok_own, tok_near, tok_far, bias_sums = local(
        attn_bwd_kernel,
        [
            ((width, 4 * inner), BF16),
            ((TILE, width), F32),
            ((2 * TILE, width), BF16),
            ((TILE, width), BF16),
            ((8, inner), F32),
        ],
        u0, u1, output_weight, q0, k0, k1, v0, v1, mask, lse0, lse1, q1, u2, u3,
        x0, x1, x2, x3, ctx0, ctx1, query_weight, key_weight, value_weight,
        name="attn_bwd", us=23, limit=32, near_in=(0, 1, 12, 13),
        scratch=[pltpu.VMEM((length, inner), BF16)] * 3 + [pltpu.VMEM((length, inner), F32)] * 2,
    )
    attn_grads = lax.psum_scatter(after(attn_grads, came), "y", scatter_dimension=0, tiled=True)

    came[0] = after(came[0], tok_own)
    for step in range(1, 4):
        if step == 2:
            notes = after(notes, came[0])
            for link in ("xa", "xb"):
                notes = notes + send(notes, link)
            came[0] = after(came[0], (tok_far, notes))
        if step == 3:
            notes = notes + send(notes, "ya")
            came[0] = after(came[0], notes)
        both = add_step(keep, came, f"add{step}")
        keep, out = both[:4], both[4:]
        came = [send(v, order[step]) for v, order in zip(out, ORDERS)]
        if step == 1:
            tok_near = send(after(tok_near, keep[0]), "c")
            tok_far = send(add_low(tok_far, tok_near[TILE:]), "zl")
            notes = jnp.concatenate(
                [after(bias_sums, keep[0]), total.reshape(7 * width // inner, inner)], axis=0
            )
        if step == 2:
            attn_grads = lax.psum_scatter(after(attn_grads, keep[0]), "x", scatter_dimension=0, tiled=True)
    notes = after(notes, keep[0])
    notes = notes + send(notes, "yb")
    notes = notes + send(notes, "zh")
    tokens_grad = first_grad + tok_own + tok_near[:TILE].astype(F32) + tok_far.astype(F32)
    came[0] = after(came[0], (notes, tokens_grad))
    ways = local(
        add_last_kernel,
        [((2, 32, units), F32)] + [((2, 32, units), BF16)] * 3,
        *keep, *came, name="add4", us=1, near_out=range(4),
    )
    mine = lax.dynamic_slice_in_dim(attn_grads, zh_here * 32, 32, 0)
    theirs = lax.dynamic_slice_in_dim(attn_grads, (1 - zh_here) * 32, 32, 0)
    finished = local(
        finish_kernel,
        [((32, units), F32)] * 2
        + [((32, inner), F32)] * 4
        + [((1, inner), F32)] * 2
        + [((1, width), F32)] * 7,
        ways[0],
        send(ways[2], "zl"),
        send(ways[3], "zz"),
        send(jnp.concatenate([ways[1], theirs[None]], axis=0), "zh"),
        mine,
        notes,
        name="finish", us=2, near_in=range(6), near_out=range(15),
    )
    wi_grad, wo_grad, *finished = finished
    vectors = [v.reshape(-1) for v in finished[4:]]
    return (
        layer_out[None],
        tokens_grad[None],
        finished[0],
        vectors[0],
        finished[1],
        finished[2],
        vectors[1],
        finished[3].T,
        vectors[7],
        vectors[5],
        vectors[6],
        wi_grad,
        vectors[8],
        wo_grad.T,
        vectors[4],
        vectors[2],
        vectors[3],
    )


def solution(mesh):
    fine = Mesh(mesh.devices.reshape(4, 2, 4, 2, 2), AXES)
    shard = ("zl", "c")
    placed = (
        P(REPLICA, shard, None),
        P(REPLICA, None),
        P(None, shard),
        P(shard),
        P(None, shard),
        P(None, shard),
        P(shard),
        P(shard, None),
        P(),
        P(),
        P(),
        P(None, shard),
        P(shard),
        P(shard, None),
        P(),
        P(),
        P(),
        P(REPLICA, shard, None),
    )
    return jax.shard_map(
        per_device,
        mesh=fine,
        in_specs=placed,
        out_specs=(
            P(REPLICA, shard, None),
            P(REPLICA, shard, None),
            P(REPLICA, shard),
            P(shard),
            P(REPLICA, shard),
            P(REPLICA, shard),
            P(shard),
            P(shard, REPLICA),
            P(),
            P(),
            P(),
            P(REPLICA, shard),
            P(shard),
            P(shard, REPLICA),
            P(),
            P(),
            P(),
        ),
        check_vma=False,
    )
```

```python
import functools

import jax
import jax.numpy as jnp
from jax import lax
from jax.experimental import pallas as pl
from jax.experimental.pallas import tpu as pltpu
from jax.sharding import Mesh, PartitionSpec as P

HEAD_DIM = 64
WINDOW = 512
TILE = 256
AXES = ("x", "zh", "y", "zl", "c")
REPLICA = ("x", "zh", "y")
F32 = jnp.float32
BF16 = jnp.bfloat16
MIB = 1 << 20


def flat_index(x, zh, y, zl, c):
    return (((x * 2 + zh) * 4 + y) * 2 + zl) * 2 + c


def permutation(move):
    return [
        (flat_index(x, zh, y, zl, c), flat_index(*move(x, zh, y, zl, c)))
        for x in range(4)
        for zh in range(2)
        for y in range(4)
        for zl in range(2)
        for c in range(2)
    ]


LINKS = {
    "xa": permutation(lambda x, zh, y, zl, c: (x ^ 1, zh, y, zl, c)),
    "xb": permutation(lambda x, zh, y, zl, c: (3 - x, zh, y, zl, c)),
    "ya": permutation(lambda x, zh, y, zl, c: (x, zh, y ^ 1, zl, c)),
    "yb": permutation(lambda x, zh, y, zl, c: (x, zh, 3 - y, zl, c)),
    "zl": permutation(lambda x, zh, y, zl, c: (x, zh, y, zl ^ 1, c)),
    "zz": permutation(lambda x, zh, y, zl, c: (x, zh ^ 1, y, zl ^ 1, c)),
    "zh": permutation(lambda x, zh, y, zl, c: (x, zh ^ 1, y, zl, c)),
    "c": permutation(lambda x, zh, y, zl, c: (x, zh, y, zl, c ^ 1)),
}
ORDERS = (
    ("xa", "xb", "ya", "yb"),
    ("xb", "ya", "yb", "xa"),
    ("ya", "yb", "xa", "xb"),
    ("yb", "xa", "xb", "ya"),
)


def send(value, link):
    return lax.ppermute(value, AXES, LINKS[link])


def dot_nn(a, b):
    return lax.dot_general(a, b, (((1,), (0,)), ((), ())), preferred_element_type=F32)


def dot_nt(a, b):
    return lax.dot_general(a, b, (((1,), (1,)), ((), ())), preferred_element_type=F32)


def dot_tn(a, b):
    return lax.dot_general(a, b, (((0,), (0,)), ((), ())), preferred_element_type=F32)


class Held:
    def __init__(self, source, buffer, sem):
        self.copy = pltpu.make_async_copy(source, buffer, sem)
        self.copy.start()
        self.buffer = buffer
        self.shape = buffer.shape
        self.here = False

    def __getitem__(self, index):
        if not self.here:
            self.copy.wait()
            self.here = True
        return self.buffer[index]


class Gathered:
    def __init__(self, source, buffer, sem, half):
        self.buffer, self.here = buffer, False
        self.copy = pltpu.make_async_copy(source.at[:, pl.ds(64 * half, 64)], buffer, sem)
        self.copy.start()

    def __getitem__(self, index):
        if not self.here:
            self.copy.wait()
            self.here = True
        rows, cols = index
        start, stop = rows.start or 0, rows.stop or 1024
        block = self.buffer[start // 64 : stop // 64, :, cols]
        return block.reshape(stop - start, block.shape[-1])


class Kept:
    def __init__(self, target, buffer, sems):
        self.target, self.buffer, self.sems = target, buffer, sems
        self.shape, self.dtype = buffer.shape, buffer.dtype
        self.copies = []

    def __getitem__(self, index):
        return self.buffer[index]

    def __setitem__(self, index, value):
        self.buffer[index] = value

    def flush(self, index=None):
        source, target = self.buffer, self.target
        if index is not None:
            source, target = source.at[index], target.at[index]
        copy = pltpu.make_async_copy(source, target, self.sems.at[len(self.copies)])
        copy.start()
        self.copies.append(copy)


def flush(ref, index=None):
    if isinstance(ref, Kept):
        ref.flush(index)


def local(kernel, outs, *operands, name, us, scratch=(), limit=16, scalars=0, near_in=(), near_out=(), raw=(), free=()):
    small = 1 << 17

    def near(shape, dtype):
        size = jnp.dtype(dtype).itemsize
        for n in shape:
            size *= n
        return size <= small

    ins = [(v.shape, v.dtype) for v in operands]
    in_near = [i in near_in or near(*v) for i, v in enumerate(ins)]
    out_near = [i in near_out or near(*v) for i, v in enumerate(outs)]
    in_bufs = [pltpu.VMEM(*v) for i, v in enumerate(ins) if i >= scalars and not in_near[i] and i not in raw]
    out_bufs = [pltpu.VMEM(*v) for i, v in enumerate(outs) if not out_near[i]]
    user = len(scratch)

    def body(*refs):
        in_refs, refs = refs[: len(ins)], refs[len(ins) :]
        out_refs, refs = refs[: len(outs)], refs[len(outs) :]
        own, refs = refs[:user], list(refs[user:])
        in_sem, out_sem = refs[-2:]
        buffers = iter(refs[:-2])
        wrapped, kept = [], []
        for i, ref in enumerate(in_refs):
            if i < scalars or in_near[i] or i in raw:
                wrapped.append(ref)
            else:
                wrapped.append(Held(ref, next(buffers), in_sem.at[i]))
        for i, ref in enumerate(out_refs):
            if not out_near[i]:
                ref = Kept(ref, next(buffers), out_sem.at[i])
                kept.append(ref)
            wrapped.append(ref)
        kernel(*wrapped, *own)
        for ref in wrapped:
            if isinstance(ref, Held) and not ref.here:
                ref.copy.wait()
        for ref in kept:
            if not ref.copies:
                ref.flush()
        for ref in kept:
            for copy in ref.copies:
                copy.wait()

    vmem = pl.BlockSpec(memory_space=pltpu.VMEM)
    hbm = pl.BlockSpec(memory_space=pltpu.HBM)
    anywhere = pl.BlockSpec(memory_space=pl.ANY)
    smem = pl.BlockSpec(memory_space=pltpu.SMEM)
    return pl.pallas_call(
        body,
        in_specs=[
            smem if i < scalars else vmem if in_near[i] else anywhere if i in free else hbm for i in range(len(ins))
        ],
        out_specs=[vmem if v else hbm for v in out_near],
        out_shape=[jax.ShapeDtypeStruct(*o) if v else pltpu.HBM(*o) for o, v in zip(outs, out_near)],
        scratch_shapes=[
            *scratch,
            *in_bufs,
            *out_bufs,
            pltpu.SemaphoreType.DMA((len(ins),)),
            pltpu.SemaphoreType.DMA((len(outs), 2)),
        ],
        compiler_params=pltpu.CompilerParams(vmem_limit_bytes=limit * MIB),
        cost_estimate=pl.CostEstimate(flops=int(us * 1e9), bytes_accessed=MIB, transcendentals=0),
        name=name,
    )(
        *(
            v if i < scalars or in_near[i] or i in free else pltpu.with_memory_space_constraint(v, pltpu.HBM)
            for i, v in enumerate(operands)
        )
    )


def after(value, *others):
    return lax.optimization_barrier((value, others))[0]


def head_lanes(shape, head):
    lane = lax.broadcasted_iota(jnp.int32, shape, len(shape) - 1)
    return (lane >> 6) == head


def qkv_kernel(x0, x1, wq, wk, wv, bq, bv, q_ref, k_ref, v_ref):
    for t, x in enumerate((x0, x1)):
        rows = slice(t * TILE, (t + 1) * TILE)
        q_ref[rows, :] = (dot_nn(x[...], wq[...]) + bq[...].astype(F32)).astype(BF16)
        k_ref[rows, :] = dot_nn(x[...], wk[...]).astype(BF16)
        v_ref[rows, :] = (dot_nn(x[...], wv[...]) + bv[...].astype(F32)).astype(BF16)


def attn_fwd_kernel(first, q_ref, k0, k1, v0, v1, mask, wo, ctx_ref, lse_ref, term0, term1):
    rows = q_ref.shape[0]
    half = k0.shape[0]
    q = q_ref[...] * jnp.asarray(HEAD_DIM ** -0.5, BF16)
    mask0 = mask[first : first + rows, :half].astype(F32)
    mask1 = mask[first : first + rows, half:].astype(F32)
    ctx = jnp.zeros(q.shape, F32)
    lse = jnp.zeros((rows, 128), F32)
    lane = lax.broadcasted_iota(jnp.int32, lse.shape, 1)
    for h in range(q.shape[1] // HEAD_DIM):
        mine = head_lanes(q.shape, h)
        qh = jnp.where(mine, q, jnp.zeros_like(q))
        s0 = dot_nt(qh, k0[...]) + mask0
        s1 = dot_nt(qh, k1[...]) + mask1
        top = jnp.max(jnp.maximum(s0, s1), axis=-1, keepdims=True)
        p0 = jnp.exp(s0 - top)
        p1 = jnp.exp(s1 - top)
        total = jnp.sum(p0 + p1, axis=-1, keepdims=True)
        part = (dot_nn(p0.astype(BF16), v0[...]) + dot_nn(p1.astype(BF16), v1[...])) * (1.0 / total)
        ctx = jnp.where(mine, part, ctx)
        lse = jnp.where(lane == h, top + jnp.log(total), lse)
    ctx_ref[...] = ctx.astype(BF16)
    flush(ctx_ref)
    lse_ref[...] = jnp.transpose(lse)[:8]
    term1[...] = dot_nn(ctx_ref[TILE:, :], wo[...]).astype(BF16)
    term0[...] = dot_nn(ctx_ref[:TILE, :], wo[...]).astype(BF16)


def attn_bwd_kernel(up0, up1, wo, q0, k0, k1, v0, v1, mask, lse0, lse1, q1, up2, up3,
                    x0, x1, x2, x3, ctx0, ctx1, wq, wk, wv,
                    grads, tok_own, tok_near, tok_far, sums_ref, dq_ref, dk_ref, dv_ref, dk, dv):
    xs = (x0, x1, x2, x3)
    half = k0.shape[0]
    scale = HEAD_DIM ** -0.5
    keys, values = (k0, k1), (v0, v1)
    for t, (q_ref, lse, ups) in enumerate(((q0, lse0, (up0, up1)), (q1, lse1, (up2, up3)))):
        q = q_ref[...] * jnp.asarray(scale, BF16)
        up = jnp.concatenate([ups[0][...], ups[1][...]], axis=0)
        grad = dot_nt(up, wo[...]).astype(BF16)
        dq = jnp.zeros(q.shape, F32)
        for h in range(q.shape[1] // HEAD_DIM):
            mine = head_lanes(q.shape, h)
            qh = jnp.where(mine, q, jnp.zeros_like(q))
            gh = jnp.where(mine, grad, jnp.zeros_like(grad))
            probs, prob_grads, row = [], [], 0.0
            for j in range(2):
                bias = mask[j * half : (j + 1) * half, t * half : (t + 1) * half].astype(F32)
                p = jnp.exp(dot_nt(keys[j][...], qh) + bias - lse[h : h + 1, :])
                dp = dot_nt(values[j][...], gh)
                row = row + jnp.sum(p * dp, axis=0, keepdims=True)
                probs.append(p)
                prob_grads.append(dp)
            part = 0.0
            for j in range(2):
                rows = slice(j * half, (j + 1) * half)
                value_part = dot_nn(probs[j].astype(BF16), gh)
                ds = (probs[j] * (prob_grads[j] - row)).astype(BF16)
                key_part = dot_nn(ds, qh)
                if t == 0 and h == 0:
                    dv[rows, :] = value_part
                    dk[rows, :] = key_part
                else:
                    dv[rows, :] += value_part
                    dk[rows, :] += key_part
                part = part + dot_tn(ds, keys[j][...])
            dq = jnp.where(mine, part, dq)
        dq_ref[t * half : (t + 1) * half, :] = (dq * scale).astype(BF16)
    dk_ref[...] = dk[...].astype(BF16)
    dv_ref[...] = dv[...].astype(BF16)
    inner = dq_ref.shape[1]
    rows = [slice(j * TILE, (j + 1) * TILE) for j in range(4)]
    bias_rows = []

    def place(total, i):
        low = total.astype(BF16)
        for x in range(4):
            for zh in range(2):
                for y in range(4):
                    source, target = (x * 8 + zh * 4 + y) * 32, (y * 8 + x * 2 + zh) * 32
                    grads[target : target + 32, i * inner : (i + 1) * inner] = low[source : source + 32]

    for i, grad in enumerate((dq_ref, dk_ref, dv_ref)):
        total = dot_tn(xs[0][...], grad[rows[0], :])
        for j in range(1, 4):
            total = total + dot_tn(xs[j][...], grad[rows[j], :])
        place(total, i)
        if i != 1:
            bias_rows.append(column_sum(grad[...].astype(F32)))
    total = 0.0
    for j, up in enumerate((up0, up1, up2, up3)):
        total = total + dot_tn(up[...], (ctx0, ctx1)[j // 2][rows[j % 2], :])
    place(total, 3)
    flush(grads)
    sums_ref[...] = stack_rows(*bias_rows)
    for j in (3, 1, 2, 0):
        total = dot_nt(dq_ref[rows[j], :], wq[...]) + dot_nt(dk_ref[rows[j], :], wk[...]) + dot_nt(dv_ref[rows[j], :], wv[...])
        if j == 0:
            tok_own[...] = total
        elif j == 2:
            tok_far[...] = total.astype(BF16)
            flush(tok_far)
        else:
            tok_near[(j // 2) * TILE : (j // 2 + 1) * TILE, :] = total.astype(BF16)
            if j == 1:
                flush(tok_near)


def normal_of(rows):
    center = jnp.mean(rows, axis=-1, keepdims=True)
    centred = rows - center
    scale = lax.rsqrt(jnp.mean(centred * centred, axis=-1, keepdims=True) + 1e-06)
    return centred * scale, scale


def normal_back(up, gain, normal, scale):
    scaled = up * gain
    mean_up = jnp.mean(scaled, axis=-1, keepdims=True)
    mean_un = jnp.mean(scaled * normal, axis=-1, keepdims=True)
    return scale * (scaled - mean_up - normal * mean_un)


def stack_rows(*rows):
    width = rows[0].shape[1]
    return jnp.concatenate([*rows, jnp.zeros((8 - len(rows), width), F32)], axis=0)


def column_sum(rows):
    return jnp.sum(rows, axis=0, keepdims=True)


def norm1_kernel(x, own, near, far, bias, gain, shift, normal_ref, scale_ref, low_ref):
    rows = x[...].astype(F32) + bias[...].astype(F32)
    rows = rows + own[...].astype(F32) + near[...].astype(F32) + far[...].astype(F32)
    normal, scale = normal_of(rows)
    normal_ref[...] = normal
    flush(normal_ref)
    scale_ref[...] = jnp.broadcast_to(scale, scale_ref.shape)
    low_ref[...] = (normal * gain[...].astype(F32) + shift[...].astype(F32)).astype(BF16)


def norm2_kernel(normal1, own, near, gain1, shift1, bias, gain, shift, cot_ref, out_ref, grad_ref, low_ref, sums_ref):
    rows = normal1[...] * gain1[...].astype(F32) + shift1[...].astype(F32) + bias[...].astype(F32)
    rows = rows + own[...] + near[...].astype(F32)
    normal, scale = normal_of(rows)
    gain_row = gain[...].astype(F32)
    cot = cot_ref[...].astype(F32)
    grad = normal_back(cot, gain_row, normal, scale)
    low_ref[...] = grad.astype(BF16)
    grad_ref[...] = grad
    out_ref[...] = (normal * gain_row + shift[...].astype(F32)).astype(BF16)
    flush(out_ref)
    sums_ref[...] = stack_rows(column_sum(cot * normal), column_sum(cot), column_sum(grad))


def norm1_back_kernel(up_ref, own, near, normal_ref, scale_ref, gain, sums2, hidden_sums, grad_ref, low_ref, sums_ref):
    up = up_ref[...] + own[...] + near[...].astype(F32)
    normal = normal_ref[...]
    grad = normal_back(up, gain[...].astype(F32), normal, scale_ref[:, 0:1])
    low_ref[...] = grad.astype(BF16)
    flush(low_ref)
    grad_ref[...] = grad
    flush(grad_ref)
    sums_ref[...] = jnp.concatenate(
        [sums2[0:3], column_sum(up * normal), column_sum(up), column_sum(grad), hidden_sums[1:2], hidden_sums[0:1]],
        axis=0,
    )


def mlp_fwd_kernel(n0, n1, wi, wo, rest, bias0, bias1, act0, act1, der0, der1, own, near, wi_far, wo_far, sems):
    wi_far = Gathered(rest, wi_far, sems.at[0], 0)
    wo_far = Gathered(rest, wo_far, sems.at[1], 1)
    width = n0.shape[1]
    chunk = 512
    for b, (bias, act, der) in enumerate(((bias0, act0, der0), (bias1, act1, der1))):
        for c in range(0, act.shape[1], chunk):
            cols = slice(c, c + chunk)
            weight = wi[:, cols] if b == 0 else wi_far[0:width, cols]
            for t, n in enumerate((n0, n1)):
                rows = slice(t * TILE, (t + 1) * TILE)
                u = dot_nn(n[...], weight) + bias[:, cols].astype(F32)
                square = u * u
                th = jnp.tanh(0.7978845608028654 * u * (1.0 + 0.044715 * square))
                half = 0.5 * (1.0 + th)
                act[rows, cols] = (u * half).astype(BF16)
                slope = 0.7978845608028654 * (1.0 + 3.0 * 0.044715 * square)
                der[rows, cols] = (half + 0.5 * u * (1.0 - th * th) * slope).astype(BF16)
        flush(act)
    for c in range(0, width, 256):
        cols = slice(c, c + 256)
        other = wo_far[0:1024, cols]
        near[:, cols] = (dot_nn(act0[TILE:], wo[:, cols]) + dot_nn(act1[TILE:], other)).astype(BF16)
        own[:, cols] = dot_nn(act0[:TILE], wo[:, cols]) + dot_nn(act1[:TILE], other)


def mlp_bwd_kernel(m0, m1, wo, wi, rest, der0, der1, hg0, hg1, own, near, sums_ref, wi_far, wo_far, sems):
    wo_far = Gathered(rest, wo_far, sems.at[1], 1)
    wi_far = Gathered(rest, wi_far, sems.at[0], 0)
    units, width = wo.shape
    chunk = 512
    sums_ref[...] = jnp.zeros_like(sums_ref)
    for b, (der, hg) in enumerate(((der0, hg0), (der1, hg1))):
        for c in range(0, units, chunk):
            cols = slice(c, c + chunk)
            weight = wo[cols, :] if b == 0 else wo_far[cols, 0:width]
            total = 0.0
            for t, m in enumerate((m0, m1)):
                rows = slice(t * TILE, (t + 1) * TILE)
                low = (dot_nt(m[...], weight) * der[rows, cols].astype(F32)).astype(BF16)
                hg[rows, cols] = low
                total = total + column_sum(low.astype(F32))
            sums_ref[b : b + 1, cols] = total
        flush(hg)
    for c in range(0, width, 256):
        cols = slice(c, c + 256)
        other = wi_far[cols, 0:1024]
        near[:, cols] = (dot_nt(hg0[TILE:], wi[cols, :]) + dot_nt(hg1[TILE:], other)).astype(BF16)
        own[:, cols] = dot_nt(hg0[:TILE], wi[cols, :]) + dot_nt(hg1[:TILE], other)
        if c + 256 in (width // 2, width):
            flush(own, (slice(None), slice(c + 256 - width // 2, c + 256)))


def gray(p):
    return p ^ (p >> 1)


def block_index(order, jx, jy):
    bit = {"xa": jx & 1, "xb": jx >> 1, "ya": jy & 1, "yb": jy >> 1}
    index = 0
    for link in order:
        index = index * 2 + bit[link]
    return index


def mlp_grads_kernel(place, n0, n1, hg0, hg1, m0, m1, act0, act1, *rest):
    outs, scratch = rest[:8], rest[8]
    x_here, zh_here, y_here = place[0], place[1], place[2]
    for mat, (lefts, rights) in enumerate((((n0, n1), (hg0, hg1)), ((m0, m1), (act0, act1)))):
        for jx in range(4):
            cols = pl.ds(pl.multiple_of(gray(gray(x_here) ^ jx) * 256, 256), 256)
            for b in range(2):
                slot = b
                scratch[slot] = (
                    dot_tn(lefts[0][:, cols], rights[b][:TILE, :]) + dot_tn(lefts[1][:, cols], rights[b][TILE:, :])
                ).astype(BF16)
                for jy in range(4):
                    y_there = gray(gray(y_here) ^ jy)
                    for a in range(2):
                        off = pl.multiple_of((zh_here ^ a) * 128 + y_there * 32, 32)
                        block = scratch[slot, pl.ds(off, 32), :]
                        for r, order in enumerate(ORDERS):
                            index = block_index(order, jx, jy)
                            out = outs[2 * r + (index >> 3)]
                            out[index & 7, mat, b, a] = block[:, r * 256 : (r + 1) * 256]
        for out in outs:
            flush(out, (slice(None), mat))


def add_step_kernel(*refs):
    count = len(ORDERS)
    for r in range(count):
        keep, came = refs[2 * r : 2 * r + 2]
        stay, go = refs[2 * count + r], refs[3 * count + r]
        half = stay.shape[0]
        for out, first in ((go, half), (stay, 0)):
            for i in range(half):
                for a in range(2):
                    out[i, a] = (keep[first + i, a].astype(F32) + came[first + i, a].astype(F32)).astype(BF16)
            flush(out)


def add_step(keep, came, name):
    half = (keep[0].shape[0] // 2, *keep[0].shape[1:])
    pairs = [v for pair in zip(keep, came) for v in pair]
    return local(add_step_kernel, [(half, BF16)] * 8, *pairs, name=name, us=half[0], limit=24, free=range(1, 8, 2))


def add_last_kernel(*refs):
    count = len(ORDERS)
    keeps, cames, ways = refs[:count], refs[count : 2 * count], refs[2 * count :]
    for r, (keep, came) in enumerate(zip(keeps, cames)):
        for b in range(2):
            for a in range(2):
                for mat in range(2):
                    total = keep[0, mat, b, a].astype(F32) + came[0, mat, b, a].astype(F32)
                    out = ways[2 * b + a]
                    out[mat, :, r * 256 : (r + 1) * 256] = total.astype(out.dtype)


def finish_kernel(here, way_zl, way_zz, way_zh, mine, theirs, notes, wi_grad, wo_grad, query, key, value, output,
                  query_bias, value_bias, *vectors):
    sums = [here[m] + way_zl[m].astype(F32) + way_zz[m].astype(F32) + way_zh[m].astype(F32) for m in range(2)]
    wi_grad[...] = sums[0]
    wo_grad[...] = sums[1]
    total = mine[...].astype(F32) + theirs[...].astype(F32)
    inner = query.shape[1]
    for i, out in enumerate((query, key, value)):
        out[...] = total[:, i * inner : (i + 1) * inner]
    output[...] = total[:, 3 * inner : 4 * inner]
    query_bias[...] = notes[0:1]
    value_bias[...] = notes[1:2]
    for i, out in enumerate(vectors):
        for j in range(4):
            row = 8 + 4 * i + j
            out[:, j * inner : (j + 1) * inner] = notes[row : row + 1]


def add_low(a, b):
    return (a.astype(F32) + b.astype(F32)).astype(BF16)


def per_device(
    tokens,
    segments,
    query_weight,
    query_bias,
    key_weight,
    value_weight,
    value_bias,
    output_weight,
    output_bias,
    first_gain,
    first_shift,
    inner_weight,
    inner_bias,
    outer_weight,
    outer_bias,
    second_gain,
    second_shift,
    cotangent,
):
    x_here, zh_here, y_here = lax.axis_index("x"), lax.axis_index("zh"), lax.axis_index("y")
    zl_here, c_here = lax.axis_index("zl"), lax.axis_index("c")
    width = tokens.shape[2]
    inner = query_weight.shape[1]
    units = inner_weight.shape[1]
    length = 4 * TILE
    row = lambda v: v.reshape(1, -1)

    x0 = tokens[0]
    x2 = send(x0, "zl")
    x1 = send(x0, "c")
    inner_bias_far = send(row(inner_bias), "zl")

    block = (x_here * 4 + y_here) * 64
    piece = jnp.concatenate(
        [lax.dynamic_slice_in_dim(w, block, 64, 0) for w in (inner_weight, outer_weight)], axis=0
    )
    piece = send(piece, "zl")


    gathered = lax.all_gather(piece, ("x", "y"), axis=0)
    place = jnp.stack([x_here, zh_here, y_here]).astype(jnp.int32)

    seg = segments[0].reshape(2, 2, TILE)
    seg = jnp.where(zl_here == 1, seg[::-1], seg)
    seg = jnp.where(c_here == 1, seg[:, ::-1], seg).reshape(-1)
    spot = jnp.arange(length, dtype=jnp.int32)
    pos = ((spot // TILE) ^ (zl_here * 2 + c_here)) * TILE + spot % TILE
    allowed = (seg[:, None] == seg[None, :]) & (jnp.abs(pos[:, None] - pos[None, :]) <= WINDOW)
    mask = jnp.where(allowed, 0.0, -1e30).astype(BF16)

    def project(a, b, near_in):
        return local(
            qkv_kernel, [((2 * TILE, inner), BF16)] * 3,
            a, b, query_weight, key_weight, value_weight, row(query_bias), row(value_bias),
            name="qkv", us=2, near_in=near_in, near_out=(0, 1, 2),
        )

    q0, k0, v0 = project(x0, x1, (1,))
    x2 = after(x2, (inner_bias_far, q0))
    x3 = send(x2, "c")
    q1, k1, v1 = project(x2, x3, (0, 1))

    def attend(q, first):
        return local(
            functools.partial(attn_fwd_kernel, first),
            [((2 * TILE, inner), BF16), ((8, 2 * TILE), F32), ((TILE, width), BF16), ((TILE, width), BF16)],
            q, k0, k1, v0, v1, mask, output_weight,
            name="attn_fwd", us=5, near_in=(0, 1, 2, 3, 4, 5), near_out=(2, 3),
        )

    ctx1, lse1, term2, term3 = attend(q1, 2 * TILE)
    from_far = send(add_low(term2, send(term3, "c")), "zl")
    ctx0, lse0, term0, term1 = attend(after(q0, term2), 0)
    from_near = send(term1, "c")

    normal1, scale1, n0 = local(
        norm1_kernel,
        [((TILE, width), F32), ((TILE, 128), F32), ((TILE, width), BF16)],
        x0, term0, from_near, from_far, row(output_bias), row(first_gain), row(first_shift),
        name="norm1", us=1.5, near_in=(1, 2, 3), near_out=(2,),
    )
    n1 = send(n0, "c")
    far_weights = [pltpu.VMEM((16, 64, units), BF16)] * 2 + [pltpu.SemaphoreType.DMA((2,))]
    act0, act1, der0, der1, mlp_own, mlp_near = local(
        mlp_fwd_kernel,
        [((2 * TILE, units), BF16)] * 4 + [((TILE, width), F32), ((TILE, width), BF16)],
        n0, n1, inner_weight, outer_weight, gathered, row(inner_bias), inner_bias_far,
        name="mlp_fwd", us=8.5, limit=24, near_in=(0, 1), near_out=(2, 3, 4, 5),
        raw=(4,), scratch=far_weights,
    )
    layer_out, second_grad, m0, sums2 = local(
        norm2_kernel,
        [((TILE, width), BF16), ((TILE, width), F32), ((TILE, width), BF16), ((8, width), F32)],
        normal1, mlp_own, send(mlp_near, "c"), row(first_gain), row(first_shift), row(outer_bias),
        row(second_gain), row(second_shift), cotangent[0],
        name="norm2", us=2, near_in=(0, 1, 2, 8), near_out=(1, 2),
    )
    m1 = send(m0, "c")
    hg0, hg1, back_own, back_near, hidden_sums = local(
        mlp_bwd_kernel,
        [((2 * TILE, units), BF16)] * 2 + [((TILE, width), F32), ((TILE, width), BF16), ((8, units), F32)],
        m0, m1, outer_weight, inner_weight, gathered, der0, der1,
        name="mlp_bwd", us=6, limit=24, near_in=(0, 1, 2, 5, 6), near_out=(3,),
        raw=(4,), scratch=far_weights,
    )
    first_grad, u0, sums = local(
        norm1_back_kernel,
        [((TILE, width), F32), ((TILE, width), BF16), ((8, width), F32)],
        second_grad, back_own, send(back_near, "c"), normal1, scale1, row(first_gain), sums2, hidden_sums,
        name="norm1_back", us=2, near_in=(0, 2),
    )
    u2 = send(u0, "zl")
    u1 = send(u0, "c")

    parts = local(
        mlp_grads_kernel,
        [((8, 2, 2, 2, 32, 256), BF16)] * 8,
        after(place, u0), n0, n1, hg0, hg1, m0, m1, act0, act1,
        name="mlp_grads", us=8.5, limit=20, scalars=1, scratch=[pltpu.VMEM((2, 256, units), BF16)],
    )
    keep, out = parts[0::2], parts[1::2]
    came = [send(v, order[0]) for v, order in zip(out, ORDERS)]

    total = sums[:6] + send(sums[:6], "c")
    chip_total = jnp.concatenate([total, sums[6:7]], axis=0)
    far = send(chip_total, "zl")
    total = jnp.concatenate([total + far[:6], sums[7:8] + far[6:7]], axis=0)

    u2 = after(u2, (parts[0], chip_total))
    u3 = send(u2, "c")
    attn_grads, tok_own, tok_near, tok_far, bias_sums = local(
        attn_bwd_kernel,
        [
            ((width, 4 * inner), BF16),
            ((TILE, width), F32),
            ((2 * TILE, width), BF16),
            ((TILE, width), BF16),
            ((8, inner), F32),
        ],
        u0, u1, output_weight, q0, k0, k1, v0, v1, mask, lse0, lse1, q1, u2, u3,
        x0, x1, x2, x3, ctx0, ctx1, query_weight, key_weight, value_weight,
        name="attn_bwd", us=23, limit=32, near_in=(0, 1, 12, 13),
        scratch=[pltpu.VMEM((length, inner), BF16)] * 3 + [pltpu.VMEM((length, inner), F32)] * 2,
    )
    attn_grads = lax.psum_scatter(after(attn_grads, came), "y", scatter_dimension=0, tiled=True)

    came[0] = after(came[0], tok_own)
    for step in range(1, 4):
        if step == 2:
            notes = after(notes, came[0])
            for link in ("xa", "xb"):
                notes = notes + send(notes, link)
            came[0] = after(came[0], (tok_far, notes))
        if step == 3:
            notes = notes + send(notes, "ya")
            came[0] = after(came[0], notes)
        both = add_step(keep, came, f"add{step}")
        keep, out = both[:4], both[4:]
        came = [send(v, order[step]) for v, order in zip(out, ORDERS)]
        if step == 1:
            tok_near = send(after(tok_near, keep[0]), "c")
            tok_far = send(add_low(tok_far, tok_near[TILE:]), "zl")
            notes = jnp.concatenate(
                [after(bias_sums, keep[0]), total.reshape(7 * width // inner, inner)], axis=0
            )
        if step == 2:
            attn_grads = lax.psum_scatter(after(attn_grads, keep[0]), "x", scatter_dimension=0, tiled=True)
    notes = after(notes, keep[0])
    notes = notes + send(notes, "yb")
    notes = notes + send(notes, "zh")
    tokens_grad = first_grad + tok_own + tok_near[:TILE].astype(F32) + tok_far.astype(F32)
    theirs = lax.dynamic_slice_in_dim(attn_grads, (1 - zh_here) * 32, 32, 0)
    came[0] = after(came[0], (notes, tokens_grad, theirs))
    ways = local(
        add_last_kernel,
        [((2, 32, units), F32)] + [((2, 32, units), BF16)] * 3,
        *keep, *came, name="add4", us=1, near_out=range(4),
    )
    mine = lax.dynamic_slice_in_dim(attn_grads, zh_here * 32, 32, 0)
    finished = local(
        finish_kernel,
        [((32, units), F32)] * 2
        + [((32, inner), F32)] * 4
        + [((1, inner), F32)] * 2
        + [((1, width), F32)] * 7,
        ways[0],
        send(ways[2], "zl"),
        send(ways[3], "zz"),
        send(ways[1], "zh"),
        mine,
        send(theirs, "zh"),
        notes,
        name="finish", us=2, near_in=range(7), near_out=range(15),
    )
    wi_grad, wo_grad, *finished = finished
    vectors = [v.reshape(-1) for v in finished[4:]]
    return (
        layer_out[None],
        tokens_grad[None],
        finished[0],
        vectors[0],
        finished[1],
        finished[2],
        vectors[1],
        finished[3].T,
        vectors[7],
        vectors[5],
        vectors[6],
        wi_grad,
        vectors[8],
        wo_grad.T,
        vectors[4],
        vectors[2],
        vectors[3],
    )


def solution(mesh):
    fine = Mesh(mesh.devices.reshape(4, 2, 4, 2, 2), AXES)
    shard = ("zl", "c")
    placed = (
        P(REPLICA, shard, None),
        P(REPLICA, None),
        P(None, shard),
        P(shard),
        P(None, shard),
        P(None, shard),
        P(shard),
        P(shard, None),
        P(),
        P(),
        P(),
        P(None, shard),
        P(shard),
        P(shard, None),
        P(),
        P(),
        P(),
        P(REPLICA, shard, None),
    )
    return jax.shard_map(
        per_device,
        mesh=fine,
        in_specs=placed,
        out_specs=(
            P(REPLICA, shard, None),
            P(REPLICA, shard, None),
            P(REPLICA, shard),
            P(shard),
            P(REPLICA, shard),
            P(REPLICA, shard),
            P(shard),
            P(shard, REPLICA),
            P(),
            P(),
            P(),
            P(REPLICA, shard),
            P(shard),
            P(shard, REPLICA),
            P(),
            P(),
            P(),
        ),
        check_vma=False,
    )
```

```python
import functools

import jax
import jax.numpy as jnp
from jax import lax
from jax.experimental import pallas as pl
from jax.experimental.pallas import tpu as pltpu
from jax.sharding import Mesh, PartitionSpec as P

HEAD_DIM = 64
WINDOW = 512
TILE = 256
AXES = ("x", "zh", "y", "zl", "c")
REPLICA = ("x", "zh", "y")
F32 = jnp.float32
BF16 = jnp.bfloat16
MIB = 1 << 20


def flat_index(x, zh, y, zl, c):
    return (((x * 2 + zh) * 4 + y) * 2 + zl) * 2 + c


def permutation(move):
    return [
        (flat_index(x, zh, y, zl, c), flat_index(*move(x, zh, y, zl, c)))
        for x in range(4)
        for zh in range(2)
        for y in range(4)
        for zl in range(2)
        for c in range(2)
    ]


LINKS = {
    "xa": permutation(lambda x, zh, y, zl, c: (x ^ 1, zh, y, zl, c)),
    "xb": permutation(lambda x, zh, y, zl, c: (3 - x, zh, y, zl, c)),
    "ya": permutation(lambda x, zh, y, zl, c: (x, zh, y ^ 1, zl, c)),
    "yb": permutation(lambda x, zh, y, zl, c: (x, zh, 3 - y, zl, c)),
    "zl": permutation(lambda x, zh, y, zl, c: (x, zh, y, zl ^ 1, c)),
    "zz": permutation(lambda x, zh, y, zl, c: (x, zh ^ 1, y, zl ^ 1, c)),
    "zh": permutation(lambda x, zh, y, zl, c: (x, zh ^ 1, y, zl, c)),
    "c": permutation(lambda x, zh, y, zl, c: (x, zh, y, zl, c ^ 1)),
}
ORDERS = (
    ("xa", "xb", "ya", "yb"),
    ("xb", "xa", "yb", "ya"),
    ("ya", "xa", "yb", "xb"),
    ("yb", "xb", "ya", "xa"),
)


def send(value, link):
    return lax.ppermute(value, AXES, LINKS[link])


def dot_nn(a, b):
    return lax.dot_general(a, b, (((1,), (0,)), ((), ())), preferred_element_type=F32)


def dot_nt(a, b):
    return lax.dot_general(a, b, (((1,), (1,)), ((), ())), preferred_element_type=F32)


def dot_tn(a, b):
    return lax.dot_general(a, b, (((0,), (0,)), ((), ())), preferred_element_type=F32)


class Held:
    def __init__(self, source, buffer, sem, late):
        self.copy = pltpu.make_async_copy(source, buffer, sem)
        self.buffer = buffer
        self.shape = buffer.shape
        self.begun = self.here = False
        if not late:
            self.begin()

    def begin(self):
        if not self.begun:
            self.copy.start()
            self.begun = True

    def wait(self):
        self.begin()
        if not self.here:
            self.copy.wait()
            self.here = True

    def __getitem__(self, index):
        self.wait()
        return self.buffer[index]


def begin(*refs):
    for ref in refs:
        if isinstance(ref, Held):
            ref.begin()


class Gathered:
    def __init__(self, source, buffer, sem, half, late=False):
        self.buffer, self.here = buffer, False
        self.copy = pltpu.make_async_copy(source.at[:, pl.ds(64 * half, 64)], buffer, sem)
        if not late:
            self.begin()

    def begin(self):
        self.copy.start()

    def __getitem__(self, index):
        if not self.here:
            self.copy.wait()
            self.here = True
        rows, cols = index
        start, stop = rows.start or 0, rows.stop or 1024
        block = self.buffer[start // 64 : stop // 64, :, cols]
        return block.reshape(stop - start, block.shape[-1])


class Kept:
    def __init__(self, target, buffer, sems):
        self.target, self.buffer, self.sems = target, buffer, sems
        self.shape, self.dtype = buffer.shape, buffer.dtype
        self.copies = []

    def __getitem__(self, index):
        return self.buffer[index]

    def __setitem__(self, index, value):
        self.buffer[index] = value

    def flush(self, index=None):
        source, target = self.buffer, self.target
        if index is not None:
            source, target = source.at[index], target.at[index]
        copy = pltpu.make_async_copy(source, target, self.sems.at[len(self.copies)])
        copy.start()
        self.copies.append(copy)


def flush(ref, index=None):
    if isinstance(ref, Kept):
        ref.flush(index)


def local(kernel, outs, *operands, name, us, scratch=(), limit=16, scalars=0, near_in=(), near_out=(), raw=(), free=(), late=()):
    small = 1 << 17

    def near(shape, dtype):
        size = jnp.dtype(dtype).itemsize
        for n in shape:
            size *= n
        return size <= small

    ins = [(v.shape, v.dtype) for v in operands]
    in_near = [i in near_in or near(*v) for i, v in enumerate(ins)]
    out_near = [i in near_out or near(*v) for i, v in enumerate(outs)]
    in_bufs = [pltpu.VMEM(*v) for i, v in enumerate(ins) if i >= scalars and not in_near[i] and i not in raw]
    out_bufs = [pltpu.VMEM(*v) for i, v in enumerate(outs) if not out_near[i]]
    user = len(scratch)

    def body(*refs):
        in_refs, refs = refs[: len(ins)], refs[len(ins) :]
        out_refs, refs = refs[: len(outs)], refs[len(outs) :]
        own, refs = refs[:user], list(refs[user:])
        in_sem, out_sem = refs[-2:]
        buffers = iter(refs[:-2])
        wrapped, kept = [], []
        for i, ref in enumerate(in_refs):
            if i < scalars or in_near[i] or i in raw:
                wrapped.append(ref)
            else:
                wrapped.append(Held(ref, next(buffers), in_sem.at[i], i in late))
        for i, ref in enumerate(out_refs):
            if not out_near[i]:
                ref = Kept(ref, next(buffers), out_sem.at[i])
                kept.append(ref)
            wrapped.append(ref)
        kernel(*wrapped, *own)
        for ref in wrapped:
            if isinstance(ref, Held):
                ref.wait()
        for ref in kept:
            if not ref.copies:
                ref.flush()
        for ref in kept:
            for copy in ref.copies:
                copy.wait()

    vmem = pl.BlockSpec(memory_space=pltpu.VMEM)
    hbm = pl.BlockSpec(memory_space=pltpu.HBM)
    anywhere = pl.BlockSpec(memory_space=pl.ANY)
    smem = pl.BlockSpec(memory_space=pltpu.SMEM)
    return pl.pallas_call(
        body,
        in_specs=[
            smem if i < scalars else vmem if in_near[i] else anywhere if i in free else hbm for i in range(len(ins))
        ],
        out_specs=[vmem if v else hbm for v in out_near],
        out_shape=[jax.ShapeDtypeStruct(*o) if v else pltpu.HBM(*o) for o, v in zip(outs, out_near)],
        scratch_shapes=[
            *scratch,
            *in_bufs,
            *out_bufs,
            pltpu.SemaphoreType.DMA((len(ins),)),
            pltpu.SemaphoreType.DMA((len(outs), 2)),
        ],
        compiler_params=pltpu.CompilerParams(vmem_limit_bytes=limit * MIB),
        cost_estimate=pl.CostEstimate(flops=int(us * 1e9), bytes_accessed=MIB, transcendentals=0),
        name=name,
    )(
        *(
            v if i < scalars or in_near[i] or i in free else pltpu.with_memory_space_constraint(v, pltpu.HBM)
            for i, v in enumerate(operands)
        )
    )


def after(value, *others):
    return lax.optimization_barrier((value, others))[0]


def head_lanes(shape, head):
    lane = lax.broadcasted_iota(jnp.int32, shape, len(shape) - 1)
    return (lane >> 6) == head


def qkv_kernel(x0, x1, wq, wk, wv, bq, bv, q_ref, k_ref, v_ref):
    for t, x in enumerate((x0, x1)):
        rows = slice(t * TILE, (t + 1) * TILE)
        q_ref[rows, :] = (dot_nn(x[...], wq[...]) + bq[...].astype(F32)).astype(BF16)
        k_ref[rows, :] = dot_nn(x[...], wk[...]).astype(BF16)
        v_ref[rows, :] = (dot_nn(x[...], wv[...]) + bv[...].astype(F32)).astype(BF16)


def attn_fwd_kernel(first, q_ref, k0, k1, v0, v1, mask, wo, ctx_ref, lse_ref, term0, term1):
    rows = q_ref.shape[0]
    half = k0.shape[0]
    q = q_ref[...] * jnp.asarray(HEAD_DIM ** -0.5, BF16)
    mask0 = mask[first : first + rows, :half].astype(F32)
    mask1 = mask[first : first + rows, half:].astype(F32)
    ctx = jnp.zeros(q.shape, F32)
    lse = jnp.zeros((rows, 128), F32)
    lane = lax.broadcasted_iota(jnp.int32, lse.shape, 1)
    for h in range(q.shape[1] // HEAD_DIM):
        mine = head_lanes(q.shape, h)
        qh = jnp.where(mine, q, jnp.zeros_like(q))
        s0 = dot_nt(qh, k0[...]) + mask0
        s1 = dot_nt(qh, k1[...]) + mask1
        top = jnp.max(jnp.maximum(s0, s1), axis=-1, keepdims=True)
        p0 = jnp.exp(s0 - top)
        p1 = jnp.exp(s1 - top)
        total = jnp.sum(p0 + p1, axis=-1, keepdims=True)
        part = (dot_nn(p0.astype(BF16), v0[...]) + dot_nn(p1.astype(BF16), v1[...])) * (1.0 / total)
        ctx = jnp.where(mine, part, ctx)
        lse = jnp.where(lane == h, top + jnp.log(total), lse)
    ctx_ref[...] = ctx.astype(BF16)
    flush(ctx_ref)
    lse_ref[...] = jnp.transpose(lse)[:8]
    term1[...] = dot_nn(ctx_ref[TILE:, :], wo[...]).astype(BF16)
    term0[...] = dot_nn(ctx_ref[:TILE, :], wo[...]).astype(BF16)


def attn_bwd_kernel(up0, up1, wo, q0, k0, k1, v0, v1, mask, lse0, lse1, q1, up2, up3,
                    x0, x1, x2, x3, ctx0, ctx1, wq, wk, wv,
                    grads, tok_own, tok_near, tok_far, sums_ref, dq_ref, dk_ref, dv_ref, dk, dv):
    xs = (x0, x1, x2, x3)
    half = k0.shape[0]
    scale = HEAD_DIM ** -0.5
    keys, values = (k0, k1), (v0, v1)
    for t, (q_ref, lse, ups) in enumerate(((q0, lse0, (up0, up1)), (q1, lse1, (up2, up3)))):
        q = q_ref[...] * jnp.asarray(scale, BF16)
        up = jnp.concatenate([ups[0][...], ups[1][...]], axis=0)
        grad = dot_nt(up, wo[...]).astype(BF16)
        dq = jnp.zeros(q.shape, F32)
        for h in range(q.shape[1] // HEAD_DIM):
            mine = head_lanes(q.shape, h)
            qh = jnp.where(mine, q, jnp.zeros_like(q))
            gh = jnp.where(mine, grad, jnp.zeros_like(grad))
            probs, prob_grads, row = [], [], 0.0
            for j in range(2):
                bias = mask[j * half : (j + 1) * half, t * half : (t + 1) * half].astype(F32)
                p = jnp.exp(dot_nt(keys[j][...], qh) + bias - lse[h : h + 1, :])
                dp = dot_nt(values[j][...], gh)
                row = row + jnp.sum(p * dp, axis=0, keepdims=True)
                probs.append(p)
                prob_grads.append(dp)
            part = 0.0
            for j in range(2):
                rows = slice(j * half, (j + 1) * half)
                value_part = dot_nn(probs[j].astype(BF16), gh)
                ds = (probs[j] * (prob_grads[j] - row)).astype(BF16)
                key_part = dot_nn(ds, qh)
                if t == 0 and h == 0:
                    dv[rows, :] = value_part
                    dk[rows, :] = key_part
                else:
                    dv[rows, :] += value_part
                    dk[rows, :] += key_part
                part = part + dot_tn(ds, keys[j][...])
            dq = jnp.where(mine, part, dq)
            if t == 0 and h == 0:
                begin(q1, *xs, ctx0, ctx1, wq, wk, wv)
        dq_ref[t * half : (t + 1) * half, :] = (dq * scale).astype(BF16)
    dk_ref[...] = dk[...].astype(BF16)
    dv_ref[...] = dv[...].astype(BF16)
    inner = dq_ref.shape[1]
    rows = [slice(j * TILE, (j + 1) * TILE) for j in range(4)]
    bias_rows = []

    def place(total, i):
        low = total.astype(BF16)
        for x in range(4):
            for zh in range(2):
                for y in range(4):
                    source, target = (x * 8 + zh * 4 + y) * 32, (y * 8 + x * 2 + zh) * 32
                    grads[target : target + 32, i * inner : (i + 1) * inner] = low[source : source + 32]

    for i, grad in enumerate((dq_ref, dk_ref, dv_ref)):
        total = dot_tn(xs[0][...], grad[rows[0], :])
        for j in range(1, 4):
            total = total + dot_tn(xs[j][...], grad[rows[j], :])
        place(total, i)
        if i != 1:
            bias_rows.append(column_sum(grad[...].astype(F32)))
    total = 0.0
    for j, up in enumerate((up0, up1, up2, up3)):
        total = total + dot_tn(up[...], (ctx0, ctx1)[j // 2][rows[j % 2], :])
    place(total, 3)
    flush(grads)
    sums_ref[...] = stack_rows(*bias_rows)
    for j in (3, 1, 2, 0):
        total = dot_nt(dq_ref[rows[j], :], wq[...]) + dot_nt(dk_ref[rows[j], :], wk[...]) + dot_nt(dv_ref[rows[j], :], wv[...])
        if j == 0:
            tok_own[...] = total
        elif j == 2:
            tok_far[...] = total.astype(BF16)
            flush(tok_far)
        else:
            tok_near[(j // 2) * TILE : (j // 2 + 1) * TILE, :] = total.astype(BF16)
            if j == 1:
                flush(tok_near)


def normal_of(rows):
    center = jnp.mean(rows, axis=-1, keepdims=True)
    centred = rows - center
    scale = lax.rsqrt(jnp.mean(centred * centred, axis=-1, keepdims=True) + 1e-06)
    return centred * scale, scale


def normal_back(up, gain, normal, scale):
    scaled = up * gain
    mean_up = jnp.mean(scaled, axis=-1, keepdims=True)
    mean_un = jnp.mean(scaled * normal, axis=-1, keepdims=True)
    return scale * (scaled - mean_up - normal * mean_un)


def stack_rows(*rows):
    width = rows[0].shape[1]
    return jnp.concatenate([*rows, jnp.zeros((8 - len(rows), width), F32)], axis=0)


def column_sum(rows):
    return jnp.sum(rows, axis=0, keepdims=True)


def norm1_kernel(x, own, near, far, bias, gain, shift, normal_ref, scale_ref, low_ref):
    rows = x[...].astype(F32) + bias[...].astype(F32)
    rows = rows + own[...].astype(F32) + near[...].astype(F32) + far[...].astype(F32)
    normal, scale = normal_of(rows)
    normal_ref[...] = normal
    flush(normal_ref)
    scale_ref[...] = jnp.broadcast_to(scale, scale_ref.shape)
    low_ref[...] = (normal * gain[...].astype(F32) + shift[...].astype(F32)).astype(BF16)


def norm2_kernel(normal1, own, near, gain1, shift1, bias, gain, shift, cot_ref, out_ref, grad_ref, low_ref, sums_ref):
    rows = normal1[...] * gain1[...].astype(F32) + shift1[...].astype(F32) + bias[...].astype(F32)
    rows = rows + own[...] + near[...].astype(F32)
    normal, scale = normal_of(rows)
    gain_row = gain[...].astype(F32)
    cot = cot_ref[...].astype(F32)
    grad = normal_back(cot, gain_row, normal, scale)
    low_ref[...] = grad.astype(BF16)
    grad_ref[...] = grad
    out_ref[...] = (normal * gain_row + shift[...].astype(F32)).astype(BF16)
    flush(out_ref)
    sums_ref[...] = stack_rows(column_sum(cot * normal), column_sum(cot), column_sum(grad))


def norm1_back_kernel(up_ref, own, near, normal_ref, scale_ref, gain, sums2, hidden_sums, grad_ref, low_ref, sums_ref):
    up = up_ref[...] + own[...] + near[...].astype(F32)
    normal = normal_ref[...]
    grad = normal_back(up, gain[...].astype(F32), normal, scale_ref[:, 0:1])
    low_ref[...] = grad.astype(BF16)
    flush(low_ref)
    grad_ref[...] = grad
    flush(grad_ref)
    sums_ref[...] = jnp.concatenate(
        [sums2[0:3], column_sum(up * normal), column_sum(up), column_sum(grad), hidden_sums[1:2], hidden_sums[0:1]],
        axis=0,
    )


def mlp_fwd_kernel(n0, n1, wi, wo, rest, bias0, bias1, act0, act1, der0, der1, own, near, wi_far, wo_far, sems):
    wi_far = Gathered(rest, wi_far, sems.at[0], 0)
    wo_far = Gathered(rest, wo_far, sems.at[1], 1, late=True)
    width = n0.shape[1]
    chunk = 512
    for b, (bias, act, der) in enumerate(((bias0, act0, der0), (bias1, act1, der1))):
        for c in range(0, act.shape[1], chunk):
            cols = slice(c, c + chunk)
            weight = wi[:, cols] if b == 0 else wi_far[0:width, cols]
            for t, n in enumerate((n0, n1)):
                rows = slice(t * TILE, (t + 1) * TILE)
                u = dot_nn(n[...], weight) + bias[:, cols].astype(F32)
                square = u * u
                th = jnp.tanh(0.7978845608028654 * u * (1.0 + 0.044715 * square))
                half = 0.5 * (1.0 + th)
                act[rows, cols] = (u * half).astype(BF16)
                slope = 0.7978845608028654 * (1.0 + 3.0 * 0.044715 * square)
                der[rows, cols] = (half + 0.5 * u * (1.0 - th * th) * slope).astype(BF16)
        flush(act)
        if b == 0:
            wo_far.begin()
            begin(wo)
    for c in range(0, width, 256):
        cols = slice(c, c + 256)
        other = wo_far[0:1024, cols]
        near[:, cols] = (dot_nn(act0[TILE:], wo[:, cols]) + dot_nn(act1[TILE:], other)).astype(BF16)
        own[:, cols] = dot_nn(act0[:TILE], wo[:, cols]) + dot_nn(act1[:TILE], other)


def mlp_bwd_kernel(m0, m1, wo, wi, rest, der0, der1, hg0, hg1, own, near, sums_ref, wi_far, wo_far, sems):
    wo_far = Gathered(rest, wo_far, sems.at[1], 1)
    wi_far = Gathered(rest, wi_far, sems.at[0], 0, late=True)
    units, width = wo.shape
    chunk = 512
    sums_ref[...] = jnp.zeros_like(sums_ref)
    for b, (der, hg) in enumerate(((der0, hg0), (der1, hg1))):
        for c in range(0, units, chunk):
            cols = slice(c, c + chunk)
            weight = wo[cols, :] if b == 0 else wo_far[cols, 0:width]
            total = 0.0
            for t, m in enumerate((m0, m1)):
                rows = slice(t * TILE, (t + 1) * TILE)
                low = (dot_nt(m[...], weight) * der[rows, cols].astype(F32)).astype(BF16)
                hg[rows, cols] = low
                total = total + column_sum(low.astype(F32))
            sums_ref[b : b + 1, cols] = total
        flush(hg)
        if b == 0:
            wi_far.begin()
            begin(wi)
    for c in range(0, width, 256):
        cols = slice(c, c + 256)
        other = wi_far[cols, 0:1024]
        near[:, cols] = (dot_nt(hg0[TILE:], wi[cols, :]) + dot_nt(hg1[TILE:], other)).astype(BF16)
        own[:, cols] = dot_nt(hg0[:TILE], wi[cols, :]) + dot_nt(hg1[:TILE], other)
        if c + 256 in (width // 2, width):
            flush(own, (slice(None), slice(c + 256 - width // 2, c + 256)))


def gray(p):
    return p ^ (p >> 1)


def block_index(order, jx, jy):
    bit = {"xa": jx & 1, "xb": jx >> 1, "ya": jy & 1, "yb": jy >> 1}
    index = 0
    for link in order:
        index = index * 2 + bit[link]
    return index


def mlp_grads_kernel(place, n0, n1, hg0, hg1, m0, m1, act0, act1, *rest):
    outs, scratch = rest[:8], rest[8]
    x_here, zh_here, y_here = place[0], place[1], place[2]
    for mat, (lefts, rights) in enumerate((((n0, n1), (hg0, hg1)), ((m0, m1), (act0, act1)))):
        for jx in range(4):
            cols = pl.ds(pl.multiple_of(gray(gray(x_here) ^ jx) * 256, 256), 256)
            for b in range(2):
                slot = b
                if mat == 0 and jx == 0 and b == 1:
                    begin(m0, m1, act0, act1)
                scratch[slot] = (
                    dot_tn(lefts[0][:, cols], rights[b][:TILE, :]) + dot_tn(lefts[1][:, cols], rights[b][TILE:, :])
                ).astype(BF16)
                for jy in range(4):
                    y_there = gray(gray(y_here) ^ jy)
                    for a in range(2):
                        off = pl.multiple_of((zh_here ^ a) * 128 + y_there * 32, 32)
                        block = scratch[slot, pl.ds(off, 32), :]
                        for r, order in enumerate(ORDERS):
                            index = block_index(order, jx, jy)
                            out = outs[2 * r + (index >> 3)]
                            out[index & 7, mat, b, a] = block[:, r * 256 : (r + 1) * 256]
        for out in outs:
            flush(out, (slice(None), mat))


def add_step_kernel(*refs):
    count = len(ORDERS)
    for r in range(count):
        keep, came = refs[2 * r : 2 * r + 2]
        stay, go = refs[2 * count + r], refs[3 * count + r]
        half = stay.shape[0]
        for out, first in ((go, half), (stay, 0)):
            for i in range(half):
                for a in range(2):
                    out[i, a] = (keep[first + i, a].astype(F32) + came[first + i, a].astype(F32)).astype(BF16)
            flush(out)


def add_step(keep, came, name):
    half = (keep[0].shape[0] // 2, *keep[0].shape[1:])
    pairs = [v for pair in zip(keep, came) for v in pair]
    return local(add_step_kernel, [(half, BF16)] * 8, *pairs, name=name, us=half[0], limit=24, free=range(1, 8, 2))


def add_last_kernel(*refs):
    count = len(ORDERS)
    keeps, cames, ways = refs[:count], refs[count : 2 * count], refs[2 * count :]
    for r, (keep, came) in enumerate(zip(keeps, cames)):
        for b in range(2):
            for a in range(2):
                for mat in range(2):
                    total = keep[0, mat, b, a].astype(F32) + came[0, mat, b, a].astype(F32)
                    out = ways[2 * b + a]
                    out[mat, :, r * 256 : (r + 1) * 256] = total.astype(out.dtype)


def finish_kernel(here, way_zl, way_zz, way_zh, mine, theirs, notes, far_notes, wi_grad, wo_grad, query, key, value, output,
                  query_bias, value_bias, *vectors):
    sums = [here[m] + way_zl[m].astype(F32) + way_zz[m].astype(F32) + way_zh[m].astype(F32) for m in range(2)]
    wi_grad[...] = sums[0]
    wo_grad[...] = sums[1]
    total = mine[...].astype(F32) + theirs[...].astype(F32)
    inner = query.shape[1]
    for i, out in enumerate((query, key, value)):
        out[...] = total[:, i * inner : (i + 1) * inner]
    output[...] = total[:, 3 * inner : 4 * inner]
    query_bias[...] = notes[0:1]
    value_bias[...] = notes[1:2]
    for i, out in enumerate(vectors):
        for j in range(4):
            far = 8 + 4 * i + j
            row = far + 4 if i == 6 else far
            out[:, j * inner : (j + 1) * inner] = notes[row : row + 1] + far_notes[far : far + 1]


def add_low(a, b):
    return (a.astype(F32) + b.astype(F32)).astype(BF16)


def per_device(
    tokens,
    segments,
    query_weight,
    query_bias,
    key_weight,
    value_weight,
    value_bias,
    output_weight,
    output_bias,
    first_gain,
    first_shift,
    inner_weight,
    inner_bias,
    outer_weight,
    outer_bias,
    second_gain,
    second_shift,
    cotangent,
):
    x_here, zh_here, y_here = lax.axis_index("x"), lax.axis_index("zh"), lax.axis_index("y")
    zl_here, c_here = lax.axis_index("zl"), lax.axis_index("c")
    width = tokens.shape[2]
    inner = query_weight.shape[1]
    units = inner_weight.shape[1]
    length = 4 * TILE
    row = lambda v: v.reshape(1, -1)

    x0 = tokens[0]
    x2 = send(x0, "zl")
    x1 = send(x0, "c")
    inner_bias_far = send(row(inner_bias), "zl")

    block = (x_here * 4 + y_here) * 64
    piece = jnp.concatenate(
        [lax.dynamic_slice_in_dim(w, block, 64, 0) for w in (inner_weight, outer_weight)], axis=0
    )
    piece = send(piece, "zl")


    gathered = lax.all_gather(piece, ("x", "y"), axis=0)
    place = jnp.stack([x_here, zh_here, y_here]).astype(jnp.int32)

    seg = segments[0].reshape(2, 2, TILE)
    seg = jnp.where(zl_here == 1, seg[::-1], seg)
    seg = jnp.where(c_here == 1, seg[:, ::-1], seg).reshape(-1)
    spot = jnp.arange(length, dtype=jnp.int32)
    pos = ((spot // TILE) ^ (zl_here * 2 + c_here)) * TILE + spot % TILE
    allowed = (seg[:, None] == seg[None, :]) & (jnp.abs(pos[:, None] - pos[None, :]) <= WINDOW)
    mask = jnp.where(allowed, 0.0, -1e30).astype(BF16)

    def project(a, b, near_in):
        return local(
            qkv_kernel, [((2 * TILE, inner), BF16)] * 3,
            a, b, query_weight, key_weight, value_weight, row(query_bias), row(value_bias),
            name="qkv", us=2, near_in=near_in, near_out=(0, 1, 2),
        )

    q0, k0, v0 = project(x0, x1, (1,))
    x2 = after(x2, (inner_bias_far, q0))
    x3 = send(x2, "c")
    q1, k1, v1 = project(x2, x3, (0, 1))

    def attend(q, first):
        return local(
            functools.partial(attn_fwd_kernel, first),
            [((2 * TILE, inner), BF16), ((8, 2 * TILE), F32), ((TILE, width), BF16), ((TILE, width), BF16)],
            q, k0, k1, v0, v1, mask, output_weight,
            name="attn_fwd", us=5, near_in=(0, 1, 2, 3, 4, 5), near_out=(2, 3),
        )

    ctx1, lse1, term2, term3 = attend(q1, 2 * TILE)
    from_far = send(add_low(term2, send(term3, "c")), "zl")
    ctx0, lse0, term0, term1 = attend(after(q0, term2), 0)
    from_near = send(term1, "c")

    normal1, scale1, n0 = local(
        norm1_kernel,
        [((TILE, width), F32), ((TILE, 128), F32), ((TILE, width), BF16)],
        x0, term0, from_near, from_far, row(output_bias), row(first_gain), row(first_shift),
        name="norm1", us=1.5, near_in=(1, 2, 3), near_out=(2,),
    )
    n1 = send(n0, "c")
    far_weights = [pltpu.VMEM((16, 64, units), BF16)] * 2 + [pltpu.SemaphoreType.DMA((2,))]
    act0, act1, der0, der1, mlp_own, mlp_near = local(
        mlp_fwd_kernel,
        [((2 * TILE, units), BF16)] * 4 + [((TILE, width), F32), ((TILE, width), BF16)],
        n0, n1, inner_weight, outer_weight, gathered, row(inner_bias), inner_bias_far,
        name="mlp_fwd", us=8.5, limit=24, near_in=(0, 1), late=(3,), near_out=(2, 3, 4, 5),
        raw=(4,), scratch=far_weights,
    )
    layer_out, second_grad, m0, sums2 = local(
        norm2_kernel,
        [((TILE, width), BF16), ((TILE, width), F32), ((TILE, width), BF16), ((8, width), F32)],
        normal1, mlp_own, send(mlp_near, "c"), row(first_gain), row(first_shift), row(outer_bias),
        row(second_gain), row(second_shift), cotangent[0],
        name="norm2", us=2, near_in=(0, 1, 2, 8), near_out=(1, 2),
    )
    m1 = send(m0, "c")
    hg0, hg1, back_own, back_near, hidden_sums = local(
        mlp_bwd_kernel,
        [((2 * TILE, units), BF16)] * 2 + [((TILE, width), F32), ((TILE, width), BF16), ((8, units), F32)],
        m0, m1, outer_weight, inner_weight, gathered, der0, der1,
        name="mlp_bwd", us=6, limit=24, near_in=(0, 1, 2, 5, 6), late=(3,), near_out=(3,),
        raw=(4,), scratch=far_weights,
    )
    first_grad, u0, sums = local(
        norm1_back_kernel,
        [((TILE, width), F32), ((TILE, width), BF16), ((8, width), F32)],
        second_grad, back_own, send(back_near, "c"), normal1, scale1, row(first_gain), sums2, hidden_sums,
        name="norm1_back", us=2, near_in=(0, 2),
    )
    u2 = send(u0, "zl")
    u1 = send(u0, "c")

    parts = local(
        mlp_grads_kernel,
        [((8, 2, 2, 2, 32, 256), BF16)] * 8,
        after(place, u0), n0, n1, hg0, hg1, m0, m1, act0, act1,
        name="mlp_grads", us=8.5, limit=20, scalars=1, late=(5, 6, 7, 8), scratch=[pltpu.VMEM((2, 256, units), BF16)],
    )
    keep, out = parts[0::2], parts[1::2]
    came = [send(v, order[0]) for v, order in zip(out, ORDERS)]

    chip_total = jnp.concatenate([sums[:6] + send(sums[:6], "c"), sums[6:]], axis=0)
    u2 = after(u2, (parts[0], chip_total))
    u3 = send(u2, "c")
    attn_grads, tok_own, tok_near, tok_far, bias_sums = local(
        attn_bwd_kernel,
        [
            ((width, 4 * inner), BF16),
            ((TILE, width), F32),
            ((2 * TILE, width), BF16),
            ((TILE, width), BF16),
            ((8, inner), F32),
        ],
        u0, u1, output_weight, q0, k0, k1, v0, v1, mask, lse0, lse1, q1, u2, u3,
        x0, x1, x2, x3, ctx0, ctx1, query_weight, key_weight, value_weight,
        name="attn_bwd", us=23, limit=32, near_in=(0, 1, 12, 13), late=(11, *range(14, 23)),
        scratch=[pltpu.VMEM((length, inner), BF16)] * 3 + [pltpu.VMEM((length, inner), F32)] * 2,
    )
    attn_grads = lax.psum_scatter(after(attn_grads, came), "y", scatter_dimension=0, tiled=True)

    came[0] = after(came[0], tok_own)
    for step in range(1, 4):
        if step == 2:
            notes = after(notes, came[0])
            for link in ("zh",):
                notes = notes + send(notes, link)
            came[0] = after(came[0], (tok_far, notes))
        if step == 3:
            for link in ("xa", "xb"):
                notes = notes + send(notes, link)
            came[0] = after(came[0], notes)
        both = add_step(keep, came, f"add{step}")
        keep, out = both[:4], both[4:]
        came = [send(v, order[step]) for v, order in zip(out, ORDERS)]
        if step == 1:
            tok_near = send(after(tok_near, keep[0]), "c")
            tok_sum = add_low(tok_far, tok_near[TILE:])
            tok_far = send(tok_sum, "zl")
            notes = jnp.concatenate(
                [after(bias_sums, keep[0]), chip_total.reshape(8 * width // inner, inner)], axis=0
            )
        if step == 2:
            attn_grads = lax.psum_scatter(after(attn_grads, keep[0]), "x", scatter_dimension=0, tiled=True)
    notes = after(notes, keep[0])
    for link in ("ya", "yb"):
        notes = notes + send(notes, link)
    theirs = lax.dynamic_slice_in_dim(attn_grads, (1 - zh_here) * 32, 32, 0)
    tokens_grad = first_grad + tok_own + tok_near[:TILE].astype(F32) + tok_far.astype(F32)
    came[0] = after(came[0], (notes, tokens_grad, theirs))
    ways = local(
        add_last_kernel,
        [((2, 32, units), F32)] + [((2, 32, units), BF16)] * 3,
        *keep, *came, name="add4", us=1, near_out=range(4),
    )
    mine = lax.dynamic_slice_in_dim(attn_grads, zh_here * 32, 32, 0)
    finished = local(
        finish_kernel,
        [((32, units), F32)] * 2
        + [((32, inner), F32)] * 4
        + [((1, inner), F32)] * 2
        + [((1, width), F32)] * 7,
        ways[0],
        send(ways[2], "zl"),
        send(ways[3], "zz"),
        send(ways[1], "zh"),
        mine,
        send(theirs, "zh"),
        notes,
        send(notes, "zl"),
        name="finish", us=2, near_in=range(8), near_out=range(15),
    )
    wi_grad, wo_grad, *finished = finished
    vectors = [v.reshape(-1) for v in finished[4:]]
    return (
        layer_out[None],
        tokens_grad[None],
        finished[0],
        vectors[0],
        finished[1],
        finished[2],
        vectors[1],
        finished[3].T,
        vectors[7],
        vectors[5],
        vectors[6],
        wi_grad,
        vectors[8],
        wo_grad.T,
        vectors[4],
        vectors[2],
        vectors[3],
    )


def solution(mesh):
    fine = Mesh(mesh.devices.reshape(4, 2, 4, 2, 2), AXES)
    shard = ("zl", "c")
    placed = (
        P(REPLICA, shard, None),
        P(REPLICA, None),
        P(None, shard),
        P(shard),
        P(None, shard),
        P(None, shard),
        P(shard),
        P(shard, None),
        P(),
        P(),
        P(),
        P(None, shard),
        P(shard),
        P(shard, None),
        P(),
        P(),
        P(),
        P(REPLICA, shard, None),
    )
    return jax.shard_map(
        per_device,
        mesh=fine,
        in_specs=placed,
        out_specs=(
            P(REPLICA, shard, None),
            P(REPLICA, shard, None),
            P(REPLICA, shard),
            P(shard),
            P(REPLICA, shard),
            P(REPLICA, shard),
            P(shard),
            P(shard, REPLICA),
            P(),
            P(),
            P(),
            P(REPLICA, shard),
            P(shard),
            P(shard, REPLICA),
            P(),
            P(),
            P(),
        ),
        check_vma=False,
    )
```

```python
import functools

import jax
import jax.numpy as jnp
from jax import lax
from jax.experimental import pallas as pl
from jax.experimental.pallas import tpu as pltpu
from jax.sharding import Mesh, PartitionSpec as P

HEAD_DIM = 64
WINDOW = 512
TILE = 256
AXES = ("x", "zh", "y", "zl", "c")
REPLICA = ("x", "zh", "y")
F32 = jnp.float32
BF16 = jnp.bfloat16
MIB = 1 << 20


def flat_index(x, zh, y, zl, c):
    return (((x * 2 + zh) * 4 + y) * 2 + zl) * 2 + c


def permutation(move):
    return [
        (flat_index(x, zh, y, zl, c), flat_index(*move(x, zh, y, zl, c)))
        for x in range(4)
        for zh in range(2)
        for y in range(4)
        for zl in range(2)
        for c in range(2)
    ]


LINKS = {
    "xa": permutation(lambda x, zh, y, zl, c: (x ^ 1, zh, y, zl, c)),
    "xb": permutation(lambda x, zh, y, zl, c: (3 - x, zh, y, zl, c)),
    "ya": permutation(lambda x, zh, y, zl, c: (x, zh, y ^ 1, zl, c)),
    "yb": permutation(lambda x, zh, y, zl, c: (x, zh, 3 - y, zl, c)),
    "zl": permutation(lambda x, zh, y, zl, c: (x, zh, y, zl ^ 1, c)),
    "zz": permutation(lambda x, zh, y, zl, c: (x, zh ^ 1, y, zl ^ 1, c)),
    "zh": permutation(lambda x, zh, y, zl, c: (x, zh ^ 1, y, zl, c)),
    "c": permutation(lambda x, zh, y, zl, c: (x, zh, y, zl, c ^ 1)),
}
ORDERS = (
    ("xa", "xb", "ya", "yb"),
    ("xb", "xa", "yb", "ya"),
    ("ya", "xa", "yb", "xb"),
    ("yb", "xb", "ya", "xa"),
)


def send(value, link):
    return lax.ppermute(value, AXES, LINKS[link])


def dot_nn(a, b):
    return lax.dot_general(a, b, (((1,), (0,)), ((), ())), preferred_element_type=F32)


def dot_nt(a, b):
    return lax.dot_general(a, b, (((1,), (1,)), ((), ())), preferred_element_type=F32)


def dot_tn(a, b):
    return lax.dot_general(a, b, (((0,), (0,)), ((), ())), preferred_element_type=F32)


class Held:
    def __init__(self, source, buffer, sem, late):
        self.copy = pltpu.make_async_copy(source, buffer, sem)
        self.buffer = buffer
        self.shape = buffer.shape
        self.begun = self.here = False
        if not late:
            self.begin()

    def begin(self):
        if not self.begun:
            self.copy.start()
            self.begun = True

    def wait(self):
        self.begin()
        if not self.here:
            self.copy.wait()
            self.here = True

    def __getitem__(self, index):
        self.wait()
        return self.buffer[index]


def begin(*refs):
    for ref in refs:
        if isinstance(ref, Held):
            ref.begin()


class Gathered:
    def __init__(self, source, buffer, sem, half, late=False):
        self.buffer, self.here = buffer, False
        self.copy = pltpu.make_async_copy(source.at[:, pl.ds(64 * half, 64)], buffer, sem)
        if not late:
            self.begin()

    def begin(self):
        self.copy.start()

    def __getitem__(self, index):
        if not self.here:
            self.copy.wait()
            self.here = True
        rows, cols = index
        start, stop = rows.start or 0, rows.stop or 1024
        block = self.buffer[start // 64 : stop // 64, :, cols]
        return block.reshape(stop - start, block.shape[-1])


class Kept:
    def __init__(self, target, buffer, sems):
        self.target, self.buffer, self.sems = target, buffer, sems
        self.shape, self.dtype = buffer.shape, buffer.dtype
        self.copies = []

    def __getitem__(self, index):
        return self.buffer[index]

    def __setitem__(self, index, value):
        self.buffer[index] = value

    def flush(self, index=None):
        source, target = self.buffer, self.target
        if index is not None:
            source, target = source.at[index], target.at[index]
        copy = pltpu.make_async_copy(source, target, self.sems.at[len(self.copies)])
        copy.start()
        self.copies.append(copy)


def flush(ref, index=None):
    if isinstance(ref, Kept):
        ref.flush(index)


def local(kernel, outs, *operands, name, us, scratch=(), limit=16, scalars=0, near_in=(), near_out=(), raw=(), free=(), late=()):
    small = 1 << 17

    def near(shape, dtype):
        size = jnp.dtype(dtype).itemsize
        for n in shape:
            size *= n
        return size <= small

    ins = [(v.shape, v.dtype) for v in operands]
    in_near = [i in near_in or near(*v) for i, v in enumerate(ins)]
    out_near = [i in near_out or near(*v) for i, v in enumerate(outs)]
    in_bufs = [pltpu.VMEM(*v) for i, v in enumerate(ins) if i >= scalars and not in_near[i] and i not in raw]
    out_bufs = [pltpu.VMEM(*v) for i, v in enumerate(outs) if not out_near[i]]
    user = len(scratch)

    def body(*refs):
        in_refs, refs = refs[: len(ins)], refs[len(ins) :]
        out_refs, refs = refs[: len(outs)], refs[len(outs) :]
        own, refs = refs[:user], list(refs[user:])
        in_sem, out_sem = refs[-2:]
        buffers = iter(refs[:-2])
        wrapped, kept = [], []
        for i, ref in enumerate(in_refs):
            if i < scalars or in_near[i] or i in raw:
                wrapped.append(ref)
            else:
                wrapped.append(Held(ref, next(buffers), in_sem.at[i], i in late))
        for i, ref in enumerate(out_refs):
            if not out_near[i]:
                ref = Kept(ref, next(buffers), out_sem.at[i])
                kept.append(ref)
            wrapped.append(ref)
        kernel(*wrapped, *own)
        for ref in wrapped:
            if isinstance(ref, Held):
                ref.wait()
        for ref in kept:
            if not ref.copies:
                ref.flush()
        for ref in kept:
            for copy in ref.copies:
                copy.wait()

    vmem = pl.BlockSpec(memory_space=pltpu.VMEM)
    hbm = pl.BlockSpec(memory_space=pltpu.HBM)
    anywhere = pl.BlockSpec(memory_space=pl.ANY)
    smem = pl.BlockSpec(memory_space=pltpu.SMEM)
    return pl.pallas_call(
        body,
        in_specs=[
            smem if i < scalars else vmem if in_near[i] else anywhere if i in free else hbm for i in range(len(ins))
        ],
        out_specs=[vmem if v else hbm for v in out_near],
        out_shape=[jax.ShapeDtypeStruct(*o) if v else pltpu.HBM(*o) for o, v in zip(outs, out_near)],
        scratch_shapes=[
            *scratch,
            *in_bufs,
            *out_bufs,
            pltpu.SemaphoreType.DMA((len(ins),)),
            pltpu.SemaphoreType.DMA((len(outs), 2)),
        ],
        compiler_params=pltpu.CompilerParams(vmem_limit_bytes=limit * MIB),
        cost_estimate=pl.CostEstimate(flops=int(us * 1e9), bytes_accessed=MIB, transcendentals=0),
        name=name,
    )(
        *(
            v if i < scalars or in_near[i] or i in free else pltpu.with_memory_space_constraint(v, pltpu.HBM)
            for i, v in enumerate(operands)
        )
    )


def after(value, *others):
    return lax.optimization_barrier((value, others))[0]


def head_lanes(shape, head):
    lane = lax.broadcasted_iota(jnp.int32, shape, len(shape) - 1)
    return (lane >> 6) == head


def qkv_kernel(x0, x1, wq, wk, wv, bq, bv, q_ref, k_ref, v_ref):
    for t, x in enumerate((x0, x1)):
        rows = slice(t * TILE, (t + 1) * TILE)
        q_ref[rows, :] = (dot_nn(x[...], wq[...]) + bq[...].astype(F32)).astype(BF16)
        k_ref[rows, :] = dot_nn(x[...], wk[...]).astype(BF16)
        v_ref[rows, :] = (dot_nn(x[...], wv[...]) + bv[...].astype(F32)).astype(BF16)


def attn_fwd_kernel(first, q_ref, k0, k1, v0, v1, mask, wo, ctx_ref, lse_ref, term0, term1):
    rows = q_ref.shape[0]
    half = k0.shape[0]
    q = q_ref[...] * jnp.asarray(HEAD_DIM ** -0.5, BF16)
    mask0 = mask[first : first + rows, :half].astype(F32)
    mask1 = mask[first : first + rows, half:].astype(F32)
    ctx = jnp.zeros(q.shape, F32)
    lse = jnp.zeros((rows, 128), F32)
    lane = lax.broadcasted_iota(jnp.int32, lse.shape, 1)
    for h in range(q.shape[1] // HEAD_DIM):
        mine = head_lanes(q.shape, h)
        qh = jnp.where(mine, q, jnp.zeros_like(q))
        s0 = dot_nt(qh, k0[...]) + mask0
        s1 = dot_nt(qh, k1[...]) + mask1
        top = jnp.max(jnp.maximum(s0, s1), axis=-1, keepdims=True)
        p0 = jnp.exp(s0 - top)
        p1 = jnp.exp(s1 - top)
        total = jnp.sum(p0 + p1, axis=-1, keepdims=True)
        part = (dot_nn(p0.astype(BF16), v0[...]) + dot_nn(p1.astype(BF16), v1[...])) * (1.0 / total)
        ctx = jnp.where(mine, part, ctx)
        lse = jnp.where(lane == h, top + jnp.log(total), lse)
    ctx_ref[...] = ctx.astype(BF16)
    flush(ctx_ref)
    lse_ref[...] = jnp.transpose(lse)[:8]
    term1[...] = dot_nn(ctx_ref[TILE:, :], wo[...]).astype(BF16)
    term0[...] = dot_nn(ctx_ref[:TILE, :], wo[...]).astype(BF16)


def attn_bwd_kernel(up0, up1, wo, q0, k0, k1, v0, v1, mask, lse0, lse1, q1, up2, up3,
                    x0, x1, x2, x3, ctx0, ctx1, wq, wk, wv,
                    grads, tok_own, tok_near, tok_far, sums_ref, dq_ref, dk_ref, dv_ref, dk, dv):
    xs = (x0, x1, x2, x3)
    half = k0.shape[0]
    scale = HEAD_DIM ** -0.5
    keys, values = (k0, k1), (v0, v1)
    for t, (q_ref, lse, ups) in enumerate(((q0, lse0, (up0, up1)), (q1, lse1, (up2, up3)))):
        q = q_ref[...] * jnp.asarray(scale, BF16)
        up = jnp.concatenate([ups[0][...], ups[1][...]], axis=0)
        grad = dot_nt(up, wo[...]).astype(BF16)
        dq = jnp.zeros(q.shape, F32)
        for h in range(q.shape[1] // HEAD_DIM):
            mine = head_lanes(q.shape, h)
            qh = jnp.where(mine, q, jnp.zeros_like(q))
            gh = jnp.where(mine, grad, jnp.zeros_like(grad))
            probs, prob_grads, row = [], [], 0.0
            for j in range(2):
                bias = mask[j * half : (j + 1) * half, t * half : (t + 1) * half].astype(F32)
                p = jnp.exp(dot_nt(keys[j][...], qh) + bias - lse[h : h + 1, :])
                dp = dot_nt(values[j][...], gh)
                row = row + jnp.sum(p * dp, axis=0, keepdims=True)
                probs.append(p)
                prob_grads.append(dp)
            part = 0.0
            for j in range(2):
                rows = slice(j * half, (j + 1) * half)
                value_part = dot_nn(probs[j].astype(BF16), gh)
                ds = (probs[j] * (prob_grads[j] - row)).astype(BF16)
                key_part = dot_nn(ds, qh)
                if t == 0 and h == 0:
                    dv[rows, :] = value_part
                    dk[rows, :] = key_part
                else:
                    dv[rows, :] += value_part
                    dk[rows, :] += key_part
                part = part + dot_tn(ds, keys[j][...])
            dq = jnp.where(mine, part, dq)
            if t == 0 and h == 0:
                begin(q1, *xs, ctx0, ctx1, wq, wk, wv)
        dq_ref[t * half : (t + 1) * half, :] = (dq * scale).astype(BF16)
    dk_ref[...] = dk[...].astype(BF16)
    dv_ref[...] = dv[...].astype(BF16)
    inner = dq_ref.shape[1]
    rows = [slice(j * TILE, (j + 1) * TILE) for j in range(4)]
    bias_rows = []

    def place(total, i):
        low = total.astype(BF16)
        for x in range(4):
            for zh in range(2):
                for y in range(4):
                    source, target = (x * 8 + zh * 4 + y) * 32, (y * 8 + x * 2 + zh) * 32
                    grads[target : target + 32, i * inner : (i + 1) * inner] = low[source : source + 32]

    for i, grad in enumerate((dq_ref, dk_ref, dv_ref)):
        total = dot_tn(xs[0][...], grad[rows[0], :])
        for j in range(1, 4):
            total = total + dot_tn(xs[j][...], grad[rows[j], :])
        place(total, i)
        if i != 1:
            bias_rows.append(column_sum(grad[...].astype(F32)))
    total = 0.0
    for j, up in enumerate((up0, up1, up2, up3)):
        total = total + dot_tn(up[...], (ctx0, ctx1)[j // 2][rows[j % 2], :])
    place(total, 3)
    flush(grads)
    sums_ref[...] = stack_rows(*bias_rows)
    for j in (3, 1, 2, 0):
        total = dot_nt(dq_ref[rows[j], :], wq[...]) + dot_nt(dk_ref[rows[j], :], wk[...]) + dot_nt(dv_ref[rows[j], :], wv[...])
        if j == 0:
            tok_own[...] = total
        elif j == 2:
            tok_far[...] = total.astype(BF16)
            flush(tok_far)
        else:
            tok_near[(j // 2) * TILE : (j // 2 + 1) * TILE, :] = total.astype(BF16)
            if j == 1:
                flush(tok_near)


def normal_of(rows):
    center = jnp.mean(rows, axis=-1, keepdims=True)
    centred = rows - center
    scale = lax.rsqrt(jnp.mean(centred * centred, axis=-1, keepdims=True) + 1e-06)
    return centred * scale, scale


def normal_back(up, gain, normal, scale):
    scaled = up * gain
    mean_up = jnp.mean(scaled, axis=-1, keepdims=True)
    mean_un = jnp.mean(scaled * normal, axis=-1, keepdims=True)
    return scale * (scaled - mean_up - normal * mean_un)


def stack_rows(*rows):
    width = rows[0].shape[1]
    return jnp.concatenate([*rows, jnp.zeros((8 - len(rows), width), F32)], axis=0)


def column_sum(rows):
    return jnp.sum(rows, axis=0, keepdims=True)


def norm1_kernel(x, own, near, far, bias, gain, shift, normal_ref, scale_ref, low_ref):
    rows = x[...].astype(F32) + bias[...].astype(F32)
    rows = rows + own[...].astype(F32) + near[...].astype(F32) + far[...].astype(F32)
    normal, scale = normal_of(rows)
    normal_ref[...] = normal
    flush(normal_ref)
    scale_ref[...] = jnp.broadcast_to(scale, scale_ref.shape)
    low_ref[...] = (normal * gain[...].astype(F32) + shift[...].astype(F32)).astype(BF16)


def norm2_kernel(normal1, own, near, gain1, shift1, bias, gain, shift, cot_ref, out_ref, grad_ref, low_ref, sums_ref):
    rows = normal1[...] * gain1[...].astype(F32) + shift1[...].astype(F32) + bias[...].astype(F32)
    rows = rows + own[...] + near[...].astype(F32)
    normal, scale = normal_of(rows)
    gain_row = gain[...].astype(F32)
    cot = cot_ref[...].astype(F32)
    grad = normal_back(cot, gain_row, normal, scale)
    low_ref[...] = grad.astype(BF16)
    grad_ref[...] = grad
    out_ref[...] = (normal * gain_row + shift[...].astype(F32)).astype(BF16)
    flush(out_ref)
    sums_ref[...] = stack_rows(column_sum(cot * normal), column_sum(cot), column_sum(grad))


def norm1_back_kernel(up_ref, own, near, normal_ref, scale_ref, gain, sums2, hidden_sums, grad_ref, low_ref, sums_ref):
    up = up_ref[...] + own[...] + near[...].astype(F32)
    normal = normal_ref[...]
    grad = normal_back(up, gain[...].astype(F32), normal, scale_ref[:, 0:1])
    low_ref[...] = grad.astype(BF16)
    flush(low_ref)
    grad_ref[...] = grad
    flush(grad_ref)
    sums_ref[...] = jnp.concatenate(
        [sums2[0:3], column_sum(up * normal), column_sum(up), column_sum(grad), hidden_sums[1:2], hidden_sums[0:1]],
        axis=0,
    )


def mlp_fwd_kernel(n0, n1, wi, wo, rest, bias0, bias1, act0, act1, der0, der1, own, near, wi_far, wo_far, sems):
    wi_far = Gathered(rest, wi_far, sems.at[0], 0)
    wo_far = Gathered(rest, wo_far, sems.at[1], 1, late=True)
    width = n0.shape[1]
    chunk = 512
    for b, (bias, act, der) in enumerate(((bias0, act0, der0), (bias1, act1, der1))):
        for c in range(0, act.shape[1], chunk):
            cols = slice(c, c + chunk)
            weight = wi[:, cols] if b == 0 else wi_far[0:width, cols]
            for t, n in enumerate((n0, n1)):
                rows = slice(t * TILE, (t + 1) * TILE)
                u = dot_nn(n[...], weight) + bias[:, cols].astype(F32)
                square = u * u
                th = jnp.tanh(0.7978845608028654 * u * (1.0 + 0.044715 * square))
                half = 0.5 * (1.0 + th)
                act[rows, cols] = (u * half).astype(BF16)
                slope = 0.7978845608028654 * (1.0 + 3.0 * 0.044715 * square)
                der[rows, cols] = (half + 0.5 * u * (1.0 - th * th) * slope).astype(BF16)
        flush(act)
        if b == 0:
            wo_far.begin()
            begin(wo)
    for c in range(0, width, 256):
        cols = slice(c, c + 256)
        other = wo_far[0:1024, cols]
        near[:, cols] = (dot_nn(act0[TILE:], wo[:, cols]) + dot_nn(act1[TILE:], other)).astype(BF16)
        own[:, cols] = dot_nn(act0[:TILE], wo[:, cols]) + dot_nn(act1[:TILE], other)


def mlp_bwd_kernel(m0, m1, wo, wi, rest, der0, der1, hg0, hg1, own, near, sums_ref, wi_far, wo_far, sems):
    wo_far = Gathered(rest, wo_far, sems.at[1], 1)
    wi_far = Gathered(rest, wi_far, sems.at[0], 0, late=True)
    units, width = wo.shape
    chunk = 512
    sums_ref[...] = jnp.zeros_like(sums_ref)
    for b, (der, hg) in enumerate(((der0, hg0), (der1, hg1))):
        for c in range(0, units, chunk):
            cols = slice(c, c + chunk)
            weight = wo[cols, :] if b == 0 else wo_far[cols, 0:width]
            total = 0.0
            for t, m in enumerate((m0, m1)):
                rows = slice(t * TILE, (t + 1) * TILE)
                low = (dot_nt(m[...], weight) * der[rows, cols].astype(F32)).astype(BF16)
                hg[rows, cols] = low
                total = total + column_sum(low.astype(F32))
            sums_ref[b : b + 1, cols] = total
        flush(hg)
        if b == 0:
            wi_far.begin()
            begin(wi)
    for c in range(0, width, 256):
        cols = slice(c, c + 256)
        other = wi_far[cols, 0:1024]
        near[:, cols] = (dot_nt(hg0[TILE:], wi[cols, :]) + dot_nt(hg1[TILE:], other)).astype(BF16)
        own[:, cols] = dot_nt(hg0[:TILE], wi[cols, :]) + dot_nt(hg1[:TILE], other)
        if c + 256 in (width // 2, width):
            flush(own, (slice(None), slice(c + 256 - width // 2, c + 256)))


def gray(p):
    return p ^ (p >> 1)


def block_index(order, jx, jy):
    bit = {"xa": jx & 1, "xb": jx >> 1, "ya": jy & 1, "yb": jy >> 1}
    index = 0
    for link in order:
        index = index * 2 + bit[link]
    return index


def mlp_grads_kernel(place, n0, n1, hg0, hg1, m0, m1, act0, act1, *rest):
    outs, scratch = rest[:8], rest[8]
    x_here, zh_here, y_here = place[0], place[1], place[2]
    for mat, (lefts, rights) in enumerate((((n0, n1), (hg0, hg1)), ((m0, m1), (act0, act1)))):
        for jx in range(4):
            cols = pl.ds(pl.multiple_of(gray(gray(x_here) ^ jx) * 256, 256), 256)
            for b in range(2):
                slot = b
                if mat == 0 and jx == 0 and b == 1:
                    begin(m0, m1, act0, act1)
                scratch[slot] = (
                    dot_tn(lefts[0][:, cols], rights[b][:TILE, :]) + dot_tn(lefts[1][:, cols], rights[b][TILE:, :])
                ).astype(BF16)
                for jy in range(4):
                    y_there = gray(gray(y_here) ^ jy)
                    for a in range(2):
                        off = pl.multiple_of((zh_here ^ a) * 128 + y_there * 32, 32)
                        block = scratch[slot, pl.ds(off, 32), :]
                        for r, order in enumerate(ORDERS):
                            index = block_index(order, jx, jy)
                            out = outs[2 * r + (index >> 3)]
                            out[index & 7, mat, b, a] = block[:, r * 256 : (r + 1) * 256]
        for out in outs:
            flush(out, (slice(None), mat))


def add_step_kernel(*refs):
    count = len(ORDERS)
    for r in range(count):
        keep, came = refs[2 * r : 2 * r + 2]
        stay, go = refs[2 * count + r], refs[3 * count + r]
        half = stay.shape[0]
        for out, first in ((go, half), (stay, 0)):
            for i in range(half):
                for a in range(2):
                    out[i, a] = (keep[first + i, a].astype(F32) + came[first + i, a].astype(F32)).astype(BF16)
            flush(out)


def add_step(keep, came, name):
    half = (keep[0].shape[0] // 2, *keep[0].shape[1:])
    pairs = [v for pair in zip(keep, came) for v in pair]
    return local(add_step_kernel, [(half, BF16)] * 8, *pairs, name=name, us=half[0], limit=24, free=range(1, 8, 2))


def add_last_kernel(*refs):
    count = len(ORDERS)
    keeps, cames, ways = refs[:count], refs[count : 2 * count], refs[2 * count :]
    for r, (keep, came) in enumerate(zip(keeps, cames)):
        for b in range(2):
            for a in range(2):
                for mat in range(2):
                    total = keep[0, mat, b, a].astype(F32) + came[0, mat, b, a].astype(F32)
                    out = ways[2 * b + a]
                    out[mat, :, r * 256 : (r + 1) * 256] = total.astype(out.dtype)


def finish_kernel(here, way_zl, way_zz, way_zh, mine, theirs, notes, far_notes, wi_grad, wo_grad, query, key, value, output,
                  query_bias, value_bias, *vectors):
    sums = [here[m] + way_zl[m].astype(F32) + way_zz[m].astype(F32) + way_zh[m].astype(F32) for m in range(2)]
    wi_grad[...] = sums[0]
    wo_grad[...] = sums[1]
    total = mine[...].astype(F32) + theirs[...].astype(F32)
    inner = query.shape[1]
    for i, out in enumerate((query, key, value)):
        out[...] = total[:, i * inner : (i + 1) * inner]
    output[...] = total[:, 3 * inner : 4 * inner]
    query_bias[...] = notes[0:1]
    value_bias[...] = notes[1:2]
    for i, out in enumerate(vectors):
        for j in range(4):
            far = 8 + 4 * i + j
            row = far + 4 if i == 6 else far
            out[:, j * inner : (j + 1) * inner] = notes[row : row + 1] + far_notes[far : far + 1]


def add_low(a, b):
    return (a.astype(F32) + b.astype(F32)).astype(BF16)


def per_device(
    tokens,
    segments,
    query_weight,
    query_bias,
    key_weight,
    value_weight,
    value_bias,
    output_weight,
    output_bias,
    first_gain,
    first_shift,
    inner_weight,
    inner_bias,
    outer_weight,
    outer_bias,
    second_gain,
    second_shift,
    cotangent,
):
    x_here, zh_here, y_here = lax.axis_index("x"), lax.axis_index("zh"), lax.axis_index("y")
    zl_here, c_here = lax.axis_index("zl"), lax.axis_index("c")
    width = tokens.shape[2]
    inner = query_weight.shape[1]
    units = inner_weight.shape[1]
    length = 4 * TILE
    row = lambda v: v.reshape(1, -1)

    x0 = tokens[0]
    x2 = send(x0, "zl")
    x1 = send(x0, "c")
    inner_bias_far = send(row(inner_bias), "zl")

    block = (x_here * 4 + y_here) * 64
    piece = jnp.concatenate(
        [lax.dynamic_slice_in_dim(w, block, 64, 0) for w in (inner_weight, outer_weight)], axis=0
    )
    piece = send(piece, "zl")


    gathered = lax.all_gather(piece, ("x", "y"), axis=0)
    place = jnp.stack([x_here, zh_here, y_here]).astype(jnp.int32)

    seg = segments[0].reshape(2, 2, TILE)
    seg = jnp.where(zl_here == 1, seg[::-1], seg)
    seg = jnp.where(c_here == 1, seg[:, ::-1], seg).reshape(-1)
    spot = jnp.arange(length, dtype=jnp.int32)
    pos = ((spot // TILE) ^ (zl_here * 2 + c_here)) * TILE + spot % TILE
    allowed = (seg[:, None] == seg[None, :]) & (jnp.abs(pos[:, None] - pos[None, :]) <= WINDOW)
    mask = jnp.where(allowed, 0.0, -1e30).astype(BF16)

    def project(a, b, near_in):
        return local(
            qkv_kernel, [((2 * TILE, inner), BF16)] * 3,
            a, b, query_weight, key_weight, value_weight, row(query_bias), row(value_bias),
            name="qkv", us=2, near_in=near_in, near_out=(0, 1, 2),
        )

    q0, k0, v0 = project(x0, x1, (1,))
    x2 = after(x2, (inner_bias_far, q0))
    x3 = send(x2, "c")
    q1, k1, v1 = project(x2, x3, (0, 1))

    def attend(q, first):
        return local(
            functools.partial(attn_fwd_kernel, first),
            [((2 * TILE, inner), BF16), ((8, 2 * TILE), F32), ((TILE, width), BF16), ((TILE, width), BF16)],
            q, k0, k1, v0, v1, mask, output_weight,
            name="attn_fwd", us=5, near_in=(0, 1, 2, 3, 4, 5), near_out=(2, 3),
        )

    ctx1, lse1, term2, term3 = attend(q1, 2 * TILE)
    from_far = send(add_low(term2, send(term3, "c")), "zl")
    ctx0, lse0, term0, term1 = attend(after(q0, term2), 0)
    from_near = send(term1, "c")

    normal1, scale1, n0 = local(
        norm1_kernel,
        [((TILE, width), F32), ((TILE, 128), F32), ((TILE, width), BF16)],
        x0, term0, from_near, from_far, row(output_bias), row(first_gain), row(first_shift),
        name="norm1", us=1.5, near_in=(1, 2, 3), near_out=(2,),
    )
    n1 = send(n0, "c")
    far_weights = [pltpu.VMEM((16, 64, units), BF16)] * 2 + [pltpu.SemaphoreType.DMA((2,))]
    act0, act1, der0, der1, mlp_own, mlp_near = local(
        mlp_fwd_kernel,
        [((2 * TILE, units), BF16)] * 4 + [((TILE, width), F32), ((TILE, width), BF16)],
        n0, n1, inner_weight, outer_weight, gathered, row(inner_bias), inner_bias_far,
        name="mlp_fwd", us=8.5, limit=24, near_in=(0, 1), late=(3,), near_out=(2, 3, 4, 5),
        raw=(4,), scratch=far_weights,
    )
    layer_out, second_grad, m0, sums2 = local(
        norm2_kernel,
        [((TILE, width), BF16), ((TILE, width), F32), ((TILE, width), BF16), ((8, width), F32)],
        normal1, mlp_own, send(mlp_near, "c"), row(first_gain), row(first_shift), row(outer_bias),
        row(second_gain), row(second_shift), cotangent[0],
        name="norm2", us=2, near_in=(0, 1, 2, 8), near_out=(2,),
    )
    m1 = send(m0, "c")
    hg0, hg1, back_own, back_near, hidden_sums = local(
        mlp_bwd_kernel,
        [((2 * TILE, units), BF16)] * 2 + [((TILE, width), F32), ((TILE, width), BF16), ((8, units), F32)],
        m0, m1, outer_weight, inner_weight, gathered, der0, der1,
        name="mlp_bwd", us=6, limit=24, near_in=(0, 1, 2, 5, 6), late=(3,), near_out=(3,),
        raw=(4,), scratch=far_weights,
    )
    first_grad, u0, sums = local(
        norm1_back_kernel,
        [((TILE, width), F32), ((TILE, width), BF16), ((8, width), F32)],
        second_grad, back_own, send(back_near, "c"), normal1, scale1, row(first_gain), sums2, hidden_sums,
        name="norm1_back", us=2, near_in=(2,),
    )
    u2 = send(u0, "zl")
    u1 = send(u0, "c")

    parts = local(
        mlp_grads_kernel,
        [((8, 2, 2, 2, 32, 256), BF16)] * 8,
        after(place, u0), n0, n1, hg0, hg1, m0, m1, act0, act1,
        name="mlp_grads", us=8.5, limit=20, scalars=1, late=(5, 6, 7, 8), scratch=[pltpu.VMEM((2, 256, units), BF16)],
    )
    keep, out = parts[0::2], parts[1::2]
    came = [send(v, order[0]) for v, order in zip(out, ORDERS)]

    chip_total = jnp.concatenate([sums[:6] + send(sums[:6], "c"), sums[6:]], axis=0)
    u2 = after(u2, (parts[0], chip_total))
    u3 = send(u2, "c")
    attn_grads, tok_own, tok_near, tok_far, bias_sums = local(
        attn_bwd_kernel,
        [
            ((width, 4 * inner), BF16),
            ((TILE, width), F32),
            ((2 * TILE, width), BF16),
            ((TILE, width), BF16),
            ((8, inner), F32),
        ],
        u0, u1, output_weight, q0, k0, k1, v0, v1, mask, lse0, lse1, q1, u2, u3,
        x0, x1, x2, x3, ctx0, ctx1, query_weight, key_weight, value_weight,
        name="attn_bwd", us=23, limit=32, near_in=(0, 1, 12, 13), late=(11, *range(14, 23)),
        scratch=[pltpu.VMEM((length, inner), BF16)] * 3 + [pltpu.VMEM((length, inner), F32)] * 2,
    )
    attn_grads = lax.psum_scatter(after(attn_grads, came), "y", scatter_dimension=0, tiled=True)

    came[0] = after(came[0], tok_own)
    for step in range(1, 4):
        if step == 2:
            notes = after(notes, came[0])
            for link in ("zh", "ya"):
                notes = notes + send(notes, link)
            came[0] = after(came[0], (tok_far, notes))
        if step == 3:
            for link in ("xa",):
                notes = notes + send(notes, link)
            came[0] = after(came[0], notes)
        both = add_step(keep, came, f"add{step}")
        keep, out = both[:4], both[4:]
        came = [send(v, order[step]) for v, order in zip(out, ORDERS)]
        if step == 1:
            tok_near = send(after(tok_near, keep[0]), "c")
            tok_sum = add_low(tok_far, tok_near[TILE:])
            tok_far = send(tok_sum, "zl")
            notes = jnp.concatenate(
                [after(bias_sums, keep[0]), chip_total.reshape(8 * width // inner, inner)], axis=0
            )
        if step == 2:
            attn_grads = lax.psum_scatter(after(attn_grads, keep[0]), "x", scatter_dimension=0, tiled=True)
    notes = after(notes, keep[0])
    for link in ("xb", "yb"):
        notes = notes + send(notes, link)
    theirs = lax.dynamic_slice_in_dim(attn_grads, (1 - zh_here) * 32, 32, 0)
    tokens_grad = first_grad + tok_own + tok_near[:TILE].astype(F32) + tok_far.astype(F32)
    came[0] = after(came[0], (notes, tokens_grad, theirs))
    ways = local(
        add_last_kernel,
        [((2, 32, units), F32)] + [((2, 32, units), BF16)] * 3,
        *keep, *came, name="add4", us=1, near_out=range(4),
    )
    mine = lax.dynamic_slice_in_dim(attn_grads, zh_here * 32, 32, 0)
    finished = local(
        finish_kernel,
        [((32, units), F32)] * 2
        + [((32, inner), F32)] * 4
        + [((1, inner), F32)] * 2
        + [((1, width), F32)] * 7,
        ways[0],
        send(ways[2], "zl"),
        send(ways[3], "zz"),
        send(ways[1], "zh"),
        mine,
        send(theirs, "zh"),
        notes,
        send(notes, "zl"),
        name="finish", us=2, near_in=range(8), near_out=range(15),
    )
    wi_grad, wo_grad, *finished = finished
    vectors = [v.reshape(-1) for v in finished[4:]]
    return (
        layer_out[None],
        tokens_grad[None],
        finished[0],
        vectors[0],
        finished[1],
        finished[2],
        vectors[1],
        finished[3].T,
        vectors[7],
        vectors[5],
        vectors[6],
        wi_grad,
        vectors[8],
        wo_grad.T,
        vectors[4],
        vectors[2],
        vectors[3],
    )


def solution(mesh):
    fine = Mesh(mesh.devices.reshape(4, 2, 4, 2, 2), AXES)
    shard = ("zl", "c")
    placed = (
        P(REPLICA, shard, None),
        P(REPLICA, None),
        P(None, shard),
        P(shard),
        P(None, shard),
        P(None, shard),
        P(shard),
        P(shard, None),
        P(),
        P(),
        P(),
        P(None, shard),
        P(shard),
        P(shard, None),
        P(),
        P(),
        P(),
        P(REPLICA, shard, None),
    )
    return jax.shard_map(
        per_device,
        mesh=fine,
        in_specs=placed,
        out_specs=(
            P(REPLICA, shard, None),
            P(REPLICA, shard, None),
            P(REPLICA, shard),
            P(shard),
            P(REPLICA, shard),
            P(REPLICA, shard),
            P(shard),
            P(shard, REPLICA),
            P(),
            P(),
            P(),
            P(REPLICA, shard),
            P(shard),
            P(shard, REPLICA),
            P(),
            P(),
            P(),
        ),
        check_vma=False,
    )
```
